32 devices in a mesh: wide: 8 (over z, y), narrow: 4 (over x, core).
Axes of the slice: x: 2, y: 2, z: 4, core: 2. Of those that a mesh axis runs over, the one named last changes fastest.
Arguments:
- enc_input: bfloat16 [8192, 768], P(('wide', 'narrow')), may hold values from -6 to 6
- dec_input: bfloat16 [4096, 768], P(('wide', 'narrow')), may hold values from -6 to 6
- enc_lengths: int32 [64], P(('wide', 'narrow')), may hold values from 32 to 192, as said below
- dec_lengths: int32 [64], P(('wide', 'narrow')), may hold values from 16 to 96, as said below
- enc_attn_gain: bfloat16 [768], P(('wide', 'narrow')), may hold values from 0.25 to 1.75
- enc_qkv: bfloat16 [768, 2304], P(('wide', 'narrow')), may hold values from -0.21875 to 0.21875
- enc_attn_out: bfloat16 [768, 768], P(('wide', 'narrow')), may hold values from -1.75 to 1.75
- enc_mlp_gain: bfloat16 [768], P(('wide', 'narrow')), may hold values from 0.25 to 1.75
- enc_mlp_in: bfloat16 [768, 4096], P(('wide', 'narrow')), may hold values from -0.21875 to 0.21875
- enc_mlp_out: bfloat16 [2048, 768], P(('wide', 'narrow')), may hold values from -0.125 to 0.125
- dec_self_gain: bfloat16 [768], P(('wide', 'narrow')), may hold values from 0.25 to 1.75
- dec_qkv: bfloat16 [768, 2304], P(('wide', 'narrow')), may hold values from -0.21875 to 0.21875
- dec_self_out: bfloat16 [768, 768], P(('wide', 'narrow')), may hold values from -1.75 to 1.75
- cross_gain: bfloat16 [768], P(('wide', 'narrow')), may hold values from 0.25 to 1.75
- memory_gain: bfloat16 [768], P(('wide', 'narrow')), may hold values from 0.25 to 1.75
- cross_query: bfloat16 [768, 768], P(('wide', 'narrow')), may hold values from -0.21875 to 0.21875
- cross_kv: bfloat16 [768, 1536], P(('wide', 'narrow')), may hold values from -0.21875 to 0.21875
- cross_out: bfloat16 [768, 768], P(('wide', 'narrow')), may hold values from -1.75 to 1.75
- dec_mlp_gain: bfloat16 [768], P(('wide', 'narrow')), may hold values from 0.25 to 1.75
- dec_mlp_in: bfloat16 [768, 4096], P(('wide', 'narrow')), may hold values from -0.21875 to 0.21875
- dec_mlp_out: bfloat16 [2048, 768], P(('wide', 'narrow')), may hold values from -0.125 to 0.125
- enc_cotangent: bfloat16 [8192, 768], P(('wide', 'narrow')), may hold values from -6 to 6
- dec_cotangent: bfloat16 [4096, 768], P(('wide', 'narrow')), may hold values from -6 to 6
Outputs:
- enc_output: bfloat16 [8192, 768], P(('wide', 'narrow'))
- dec_output: bfloat16 [4096, 768], P(('wide', 'narrow'))
- enc_input_grad: float32 [8192, 768], P(('wide', 'narrow'))
- dec_input_grad: float32 [4096, 768], P(('wide', 'narrow'))
- grad_enc_attn_gain: float32 [768], P(('wide', 'narrow'))
- grad_enc_qkv: float32 [768, 2304], P(('wide', 'narrow'))
- grad_enc_attn_out: float32 [768, 768], P(('wide', 'narrow'))
- grad_enc_mlp_gain: float32 [768], P(('wide', 'narrow'))
- grad_enc_mlp_in: float32 [768, 4096], P(('wide', 'narrow'))
- grad_enc_mlp_out: float32 [2048, 768], P(('wide', 'narrow'))
- grad_dec_self_gain: float32 [768], P(('wide', 'narrow'))
- grad_dec_qkv: float32 [768, 2304], P(('wide', 'narrow'))
- grad_dec_self_out: float32 [768, 768], P(('wide', 'narrow'))
- grad_cross_gain: float32 [768], P(('wide', 'narrow'))
- grad_memory_gain: float32 [768], P(('wide', 'narrow'))
- grad_cross_query: float32 [768, 768], P(('wide', 'narrow'))
- grad_cross_kv: float32 [768, 1536], P(('wide', 'narrow'))
- grad_cross_out: float32 [768, 768], P(('wide', 'narrow'))
- grad_dec_mlp_gain: float32 [768], P(('wide', 'narrow'))
- grad_dec_mlp_in: float32 [768, 4096], P(('wide', 'narrow'))
- grad_dec_mlp_out: float32 [2048, 768], P(('wide', 'narrow'))
The draws below stay inside these ranges and needn't reach their ends.
Inputs may be any that keep to these rules, and one draw needn't show every extreme that they name: `enc_lengths`: the 2 patch counts of one device sum to at most 256; some item has exactly 192 patches. `dec_lengths`: the 2 table lengths of one device sum to at most 128; some item has exactly 96 tokens.
All inputs are finite; a program needn't handle non-finite values.
Results may differ from the reference program's by a relative error of at most 0.02.
Values may be sent and summed in bfloat16 or wider, within the bound.
A program may use at most 320 MiB of HBM per device.

```python
import jax
import jax.numpy as jnp
from jax import lax

D = 768
HEADS = 12
HEAD_DIM = 64
FF = 2048
ENC_DEV = 256
ITEMS_DEV = 2
DEC_DEV = 128
ENC_LEAST = 32
ENC_MOST = 192
DEC_LEAST = 16
DEC_MOST = 96
ENC_ROWS = 8192
DEC_ROWS = 4096
ITEMS = 64
N_WIDE = 8
N_NARROW = 4


def lengths_draw(key, capacity, shortest, longest):
    blocks = ITEMS // ITEMS_DEV
    leading_key, trailing_key, chosen_key = jax.random.split(key, 3)
    leading = jax.random.randint(leading_key, (blocks,), shortest, longest + 1)
    chosen = jax.random.randint(chosen_key, (), 0, blocks)
    leading = jnp.where(jnp.arange(blocks) == chosen, longest, leading)
    ceiling = jnp.minimum(longest, capacity - leading) + 1
    trailing = jax.random.randint(trailing_key, (blocks,), shortest, ceiling)
    return jnp.stack([leading, trailing], axis=1).reshape(blocks * 2).astype(jnp.int32)


def draw_enc_lengths(key, part):
    return lengths_draw(jax.random.fold_in(key, 11), ENC_DEV, ENC_LEAST, ENC_MOST)


def draw_dec_lengths(key, part):
    return lengths_draw(jax.random.fold_in(key, 23), DEC_DEV, DEC_LEAST, DEC_MOST)


def block_levels(rng, dims, pieces, smallest, high):
    loudness, own = 1.0, jax.random.fold_in(rng, 6)
    for dim, shards_of in pieces:
        heights = jnp.exp(jax.random.uniform(jax.random.fold_in(own, dim), (shards_of,), jnp.float32, smallest / len(pieces), high / len(pieces)))
        loudness = loudness * jnp.repeat(heights, dims[dim] // shards_of).reshape([-1 if axis == dim else 1 for axis in range(len(dims))])
    return loudness


def centred(rng, dims, width, most, cuts=(), kind=jnp.bfloat16):
    loudness = block_levels(rng, dims, cuts, -0.22, 0.18) if cuts else 1.0
    drawn = jax.random.normal(rng, dims, jnp.float32) * width * loudness
    return jnp.minimum(jnp.maximum(drawn, -most), most).astype(kind)


def setup_inputs(seed: int = 0) -> dict:
    streams_of = jax.random.split(jax.random.key(seed), 24)
    return {
        "enc_input": centred(streams_of[0], (ENC_ROWS, D), 1.0, 6.0, ((0, 32),)),
        "dec_input": centred(streams_of[1], (DEC_ROWS, D), 1.0, 6.0, ((0, 32),)),
        "enc_lengths": draw_enc_lengths(jax.random.fold_in(streams_of[23], 71), 0),
        "dec_lengths": draw_dec_lengths(jax.random.fold_in(streams_of[23], 71), 0),
        "enc_attn_gain": jnp.clip(1.0 + 0.15 * jax.random.normal(streams_of[4], (D,), jnp.float32), 0.25, 1.75).astype(jnp.bfloat16),
        "enc_qkv": centred(streams_of[5], (D, 3 * D), D ** -0.5, 0.21875, ((0, 32),)),
        "enc_attn_out": centred(streams_of[6], (D, D), (D // 64) ** -0.5, 1.75, ((0, 32),)),
        "enc_mlp_gain": jnp.clip(1.0 + 0.15 * jax.random.normal(streams_of[7], (D,), jnp.float32), 0.25, 1.75).astype(jnp.bfloat16),
        "enc_mlp_in": centred(streams_of[8], (D, 2 * FF), D ** -0.5, 0.21875, ((0, 32),)),
        "enc_mlp_out": centred(streams_of[9], (FF, D), FF ** -0.5, 0.125, ((0, 32),)),
        "dec_self_gain": jnp.clip(1.0 + 0.15 * jax.random.normal(streams_of[10], (D,), jnp.float32), 0.25, 1.75).astype(jnp.bfloat16),
        "dec_qkv": centred(streams_of[11], (D, 3 * D), D ** -0.5, 0.21875, ((0, 32),)),
        "dec_self_out": centred(streams_of[12], (D, D), (D // 64) ** -0.5, 1.75, ((0, 32),)),
        "cross_gain": jnp.clip(1.0 + 0.15 * jax.random.normal(streams_of[13], (D,), jnp.float32), 0.25, 1.75).astype(jnp.bfloat16),
        "memory_gain": jnp.clip(1.0 + 0.15 * jax.random.normal(streams_of[14], (D,), jnp.float32), 0.25, 1.75).astype(jnp.bfloat16),
        "cross_query": centred(streams_of[15], (D, D), D ** -0.5, 0.21875, ((0, 32),)),
        "cross_kv": centred(streams_of[16], (D, 2 * D), D ** -0.5, 0.21875, ((0, 32),)),
        "cross_out": centred(streams_of[17], (D, D), (D // 64) ** -0.5, 1.75, ((0, 32),)),
        "dec_mlp_gain": jnp.clip(1.0 + 0.15 * jax.random.normal(streams_of[18], (D,), jnp.float32), 0.25, 1.75).astype(jnp.bfloat16),
        "dec_mlp_in": centred(streams_of[19], (D, 2 * FF), D ** -0.5, 0.21875, ((0, 32),)),
        "dec_mlp_out": centred(streams_of[20], (FF, D), FF ** -0.5, 0.125, ((0, 32),)),
        "enc_cotangent": centred(streams_of[21], (ENC_ROWS, D), 1.0, 6.0, ((0, 32),)),
        "dec_cotangent": centred(streams_of[22], (DEC_ROWS, D), 1.0, 6.0, ((0, 32),)),
    }


epsilon = 1e-06
masked_value = -1000000000.0

@jax.custom_vjp
def low(v):
    return lax.optimization_barrier(v.astype(jnp.bfloat16)).astype(jnp.float32)

@jax.custom_vjp
def low_back(v):
    return v

def low_keep(v):
    return (low(v), None)

def low_pass(kept, grad):
    return (grad,)

def back_keep(v):
    return (v, None)

def back_low(kept, grad):
    return (low(grad),)
low.defvjp(low_keep, low_pass)
low_back.defvjp(back_keep, back_low)

def norm_rows(values, scales):
    return values * lax.rsqrt(lax.optimization_barrier(jnp.mean(values * values, axis=-1, keepdims=True)) + epsilon) * scales

def gated_units(united):
    halfway = united.shape[-1] // 2
    return jax.nn.gelu(united[:, :halfway], approximate=True) * united[:, halfway:]

def row_items(lengths, row_count):
    boundary = jnp.cumsum(lengths)
    places = jnp.arange(row_count, dtype=jnp.int32)
    return lax.optimization_barrier(jnp.sum((places[:, None] >= boundary[None, :]).astype(jnp.int32), axis=1))

def project(left, matrix):
    return jnp.dot(left, matrix, precision=lax.Precision.HIGHEST)

def head_split(matrix):
    return matrix.reshape(matrix.shape[0], HEADS, HEAD_DIM)

def attend(queries, keys_in, values_in, allowed):
    raw_scores = jnp.einsum('qhd,khd->hqk', head_split(queries), head_split(keys_in), precision=lax.Precision.HIGHEST)
    scores = jnp.where(allowed[None], low_back(raw_scores) * HEAD_DIM ** (-0.5), masked_value)
    largest = lax.optimization_barrier(jnp.max(scores, axis=2, keepdims=True))
    expanded = jnp.exp(scores - largest)
    weights = low(expanded / lax.optimization_barrier(jnp.sum(expanded, axis=2, keepdims=True)))
    mixed = jnp.einsum('hqk,khd->qhd', weights, head_split(values_in), precision=lax.Precision.HIGHEST)
    return mixed.reshape(queries.shape[0], D)

def self_layer(inputs, params, allowed, live_rows):
    scales, joined, outward = params
    normed = low(norm_rows(inputs, scales))
    projected = low(low_back(project(normed, joined)))
    mixed = low(low_back(attend(projected[:, :D], projected[:, D:2 * D], projected[:, 2 * D:], allowed)))
    branch = low_back(project(mixed, outward))
    return inputs + live_rows[:, None] * branch

def cross_layer(inputs, memory, params, allowed, live_rows):
    scales, memory_scales, query_map, pair_map, outward = params
    normed = low(norm_rows(inputs, scales))
    memory_normed = low(norm_rows(memory, memory_scales))
    queries = low(low_back(project(normed, query_map)))
    pairs = low(low_back(project(memory_normed, pair_map)))
    mixed = low(low_back(attend(queries, pairs[:, :D], pairs[:, D:], allowed)))
    branch = low_back(project(mixed, outward))
    return inputs + live_rows[:, None] * branch

def mlp_layer(inputs, params, live_rows):
    scales, inward, outward = params
    normed = low(norm_rows(inputs, scales))
    united = low_back(project(normed, inward))
    activated = low(gated_units(united))
    branch = low_back(project(activated, outward))
    return inputs + live_rows[:, None] * branch

def device_layer(piece, weight_set):
    enc_block, dec_block, enc_split, dec_split = piece
    enc_items = row_items(enc_split, ENC_DEV)
    dec_items = row_items(dec_split, DEC_DEV)
    enc_live = (enc_items < ITEMS_DEV).astype(jnp.float32)
    dec_live = (dec_items < ITEMS_DEV).astype(jnp.float32)
    enc_padded = enc_items[:, None] == ITEMS_DEV
    dec_padded = dec_items[:, None] == ITEMS_DEV
    enc_allowed = (enc_items[:, None] == enc_items[None, :]) | enc_padded
    dec_places = jnp.arange(DEC_DEV, dtype=jnp.int32)
    self_allowed = (dec_items[:, None] == dec_items[None, :]) & (dec_places[None, :] <= dec_places[:, None]) | dec_padded
    cross_allowed = (dec_items[:, None] == enc_items[None, :]) | dec_padded
    enc_middle = self_layer(enc_block, weight_set[0:3], enc_allowed, enc_live)
    enc_final = mlp_layer(enc_middle, weight_set[3:6], enc_live)
    dec_middle = self_layer(dec_block, weight_set[6:9], self_allowed, dec_live)
    dec_crossed = cross_layer(dec_middle, enc_final, weight_set[9:14], cross_allowed, dec_live)
    dec_final = mlp_layer(dec_crossed, weight_set[14:17], dec_live)
    return (enc_final, dec_final)

def reference(enc_input, dec_input, enc_lengths, dec_lengths, enc_attn_gain, enc_qkv, enc_attn_out, enc_mlp_gain, enc_mlp_in, enc_mlp_out, dec_self_gain, dec_qkv, dec_self_out, cross_gain, memory_gain, cross_query, cross_kv, cross_out, dec_mlp_gain, dec_mlp_in, dec_mlp_out, enc_cotangent, dec_cotangent):
    device_count = N_WIDE * N_NARROW
    weights = tuple((matrix.astype(jnp.float32) for matrix in (enc_attn_gain, enc_qkv, enc_attn_out, enc_mlp_gain, enc_mlp_in, enc_mlp_out, dec_self_gain, dec_qkv, dec_self_out, cross_gain, memory_gain, cross_query, cross_kv, cross_out, dec_mlp_gain, dec_mlp_in, dec_mlp_out)))
    enc_blocks = enc_input.astype(jnp.float32).reshape(device_count, ENC_DEV, D)
    dec_blocks = dec_input.astype(jnp.float32).reshape(device_count, DEC_DEV, D)
    enc_splits = enc_lengths.reshape(device_count, ITEMS_DEV)
    dec_splits = dec_lengths.reshape(device_count, ITEMS_DEV)

    def whole(enc_all, dec_all, weight_set):

        def per_device(piece):
            return device_layer(piece, weight_set)
        return lax.map(jax.checkpoint(per_device), (enc_all, dec_all, enc_splits, dec_splits))
    outputs, pullback = jax.vjp(whole, enc_blocks, dec_blocks, weights)
    cotangents = (enc_cotangent.astype(jnp.float32).reshape(device_count, ENC_DEV, D), dec_cotangent.astype(jnp.float32).reshape(device_count, DEC_DEV, D))
    grad_enc, grad_dec, grad_weights = pullback(cotangents)
    return (outputs[0].reshape(ENC_ROWS, D).astype(jnp.bfloat16), outputs[1].reshape(DEC_ROWS, D).astype(jnp.bfloat16), grad_enc.reshape(ENC_ROWS, D), grad_dec.reshape(DEC_ROWS, D), grad_weights[0], grad_weights[1], grad_weights[2], grad_weights[3], grad_weights[4], grad_weights[5], grad_weights[6], grad_weights[7], grad_weights[8], grad_weights[9], grad_weights[10], grad_weights[11], grad_weights[12], grad_weights[13], grad_weights[14], grad_weights[15], grad_weights[16])
```

```python
import functools

import jax
import jax.numpy as jnp
from jax import lax
from jax.experimental import pallas as pl
from jax.experimental.pallas import tpu as pltpu
from jax.sharding import PartitionSpec as P

D = 768
HEADS = 12
HEAD_DIM = 64
AXES = ("wide", "narrow")
MESH = pl.DeviceIdType.MESH

Z = 4
PIECES = (
    (11, 0, 768, False),
    (0, 0, 1152, False), (0, 1152, 1152, False), (1, 0, 768, True),
    (2, 0, 2048, False), (2, 2048, 2048, True), (3, 0, 768, False),
    (4, 0, 1152, False), (4, 1152, 1152, True), (5, 0, 768, False), (6, 0, 768, False),
    (7, 0, 1536, True), (8, 0, 768, False),
    (9, 0, 2048, False), (9, 2048, 2048, True), (10, 0, 768, False),
)


class Place:
    def __init__(self):
        self.w, self.n = lax.axis_index("wide"), lax.axis_index("narrow")
        self.z, self.y = self.w // 2, self.w % 2
        self.x, self.c = self.n // 2, self.n % 2
        w, n, y, x, c = self.w, self.n, self.y, self.x, self.c
        self.sibling = (w, n + 1 - 2 * c)
        self.first = (w + (1 - c) * (1 - 2 * y), n + c * (2 - 4 * x))
        self.last = (w + c * (1 - 2 * y), n + (1 - c) * (2 - 4 * x))
        self.above = (w + 2, n)
        self.below = (w - 2, n)

    def barrier(self):
        sem = pltpu.get_barrier_semaphore()
        for device in (self.sibling, self.first, self.last):
            pl.semaphore_signal(sem, inc=1, device_id=device, device_id_type=MESH)

        @pl.when(self.z < Z - 1)
        def _():
            pl.semaphore_signal(sem, inc=1, device_id=self.above, device_id_type=MESH)

        @pl.when(self.z > 0)
        def _():
            pl.semaphore_signal(sem, inc=1, device_id=self.below, device_id_type=MESH)

        inner = jnp.where(self.z * (Z - 1 - self.z) > 0, 1, 0)
        pl.semaphore_wait(sem, 4 + inner)

    def by_core(self, do):
        @pl.when(self.c == 0)
        def _():
            do(0)

        @pl.when(self.c == 1)
        def _():
            do(1)


def remote(src, dst, sems, index, device):
    send, recv = sems
    return pltpu.make_async_remote_copy(
        src_ref=src, dst_ref=dst, send_sem=send.at[index], recv_sem=recv.at[index],
        device_id=device, device_id_type=MESH,
    )


class Gather:
    PHASES = 7
    SEMS = 10

    def __init__(self, place, part, whole, columns, z_first, sems, base, local_sem):
        self.p, self.z_first, self.sems, self.base = place, z_first, sems, base
        self.part = part.at[:, :, columns]
        self.whole = whole.at[:, :, :, :, :, :, columns]
        self.local = pltpu.make_async_copy(self.part, self.own(), local_sem)

    def own(self):
        p = self.p
        return self.whole.at[p.z, p.y, p.x, p.c]

    def copy(self, src, dst, slot, device):
        return remote(src, dst, self.sems, self.base + slot, device)

    def layer(self, zz, core):
        p = self.p
        if self.z_first:
            return self.whole.at[zz, p.y, p.x, core]
        return self.whole.at[zz, :, p.x, 0] if core == 0 else self.whole.at[zz, p.y, :, 1]

    def half(self, core, mine):
        p = self.p
        if core == 0:
            return self.whole.at[:, :, p.x if mine else 1 - p.x, 0]
        return self.whole.at[:, p.y if mine else 1 - p.y, :, 1]

    def along_z(self, step, sending):
        p = self.p

        def go(core):
            for up in (True, False):
                if sending:
                    zz = p.z - step if up else p.z + step
                    there = (p.z < Z - 1) & (zz >= 0) if up else (p.z > 0) & (zz < Z)
                else:
                    zz = p.z - 1 - step if up else p.z + 1 + step
                    there = zz >= 0 if up else zz < Z

                target = (p.above if up else p.below) if sending else p.last

                @pl.when(there)
                def _():
                    block = self.layer(zz, core)
                    copy = self.copy(block, block, 1 + step * 2 + up, target)
                    copy.start() if sending else copy.wait_recv()

        p.by_core(go)

    def along_z_sent(self):
        p = self.p

        def go(core):
            for step in range(3):
                for up in (True, False):
                    zz = p.z - step if up else p.z + step
                    there = (p.z < Z - 1) & (zz >= 0) if up else (p.z > 0) & (zz < Z)

                    @pl.when(there)
                    def _():
                        block = self.layer(zz, core)
                        self.copy(block, block, 1 + step * 2 + up, p.last).wait_send()

        p.by_core(go)

    def first(self, core):
        p = self.p
        if not self.z_first:
            return self.copy(self.part, self.own(), 0, p.first)
        block = self.whole.at[:, p.y, p.x, core]
        return self.copy(block, block, 0, p.first)

    def last(self, core):
        block = self.half(core, True)
        return self.copy(block, block, 7, self.p.last)

    def across(self, core, mine):
        block = self.half(core, mine)
        return self.copy(block, block, 8 if mine else 9, self.p.sibling)

    def each(self, make, *verbs):
        def go(core):
            copy = make(core)
            for verb in verbs:
                getattr(copy, verb)()

        self.p.by_core(go)

    def phase(self, number):
        early = not self.z_first
        if number == 0:
            self.local.start()
            if early:
                self.each(self.first, "start")
            self.local.wait()
            if not early:
                self.along_z(0, True)
        elif number == 1:
            if early:
                self.each(self.first, "wait_recv")
                self.along_z(0, True)
            else:
                self.along_z(0, False)
                self.along_z(1, True)
        elif number == 2:
            self.along_z(0 if early else 1, False)
            self.along_z(1 if early else 2, True)
        elif number == 3:
            self.along_z(1 if early else 2, False)
            if early:
                self.along_z(2, True)
            else:
                self.each(self.first, "start")
        elif number == 4:
            if early:
                self.along_z(2, False)
            else:
                self.each(self.first, "wait_recv")
            self.each(self.last, "start")
            self.each(lambda core: self.across(core, True), "start")
        elif number == 5:
            self.each(self.last, "wait_recv")
            self.each(lambda core: self.across(core, False), "start")
        else:
            for core in (0, 1):
                @pl.when(self.p.c == core)
                def _():
                    for mine in (True, False):
                        self.across(1 - core, mine).wait_recv()
                        self.across(core, mine).wait_send()
                    self.first(core).wait_send()
                    self.last(core).wait_send()
            self.along_z_sent()


class Scatter:
    PHASES = 8
    SEMS = 9

    def __init__(self, place, parts, columns, z_first, out, total, mine, lasts, zs, firsts, sems, base, local_sem):
        self.p, self.z_first, self.sems, self.base = place, z_first, sems, base
        self.parts = parts.at[:, :, :, :, :, :, columns]
        self.out = out.at[:, :, columns]
        self.total, self.mine, self.lasts, self.zs, self.firsts = total, mine, lasts, zs, firsts
        self.local_sem = local_sem

    def copy(self, src, dst, slot, device):
        return remote(src, dst, self.sems, self.base + slot, device)

    def spot(self, core, last, first=None):
        every = slice(None)
        if first is None:
            return (every, last) if core else (every, every, last)
        return (last, first) if core else (first, last)

    def place_of(self, core):
        p = self.p
        return (p.y, p.x) if core else (p.x, p.y)

    def across(self, core):
        return self.copy(self.parts.at[:, :, :, 1 - core], self.total, 0, self.p.sibling)

    def take(self, core):
        return pltpu.make_async_copy(self.parts.at[:, :, :, core], self.mine, self.local_sem)

    def last(self, core):
        last, _ = self.place_of(core)
        return self.copy(self.total.at[self.spot(core, 1 - last)], self.lasts, 1, self.p.last)

    def first(self, core):
        p = self.p
        last, first = self.place_of(core)
        if self.z_first:
            src = self.total.at[(slice(None), *self.spot(core, last, 1 - first))]
        else:
            src = self.total.at[(p.z, *self.spot(core, last, 1 - first))]
        return self.copy(src, self.firsts, 2, p.first)

    def layer(self, zz, core):
        last, first = self.place_of(core)
        if self.z_first:
            return self.total.at[(zz, *self.spot(core, last, first))]
        return self.total.at[(zz, *self.spot(core, last)[1:])]

    def way(self, step, up, sending):
        z, far = self.p.z, 2 - step
        if sending:
            zz = z + 1 + far if up else z - 1 - far
            return zz, zz < Z if up else zz >= 0
        zz = z + far if up else z - far
        return zz, (z > 0) & (zz < Z) if up else (z < Z - 1) & (zz >= 0)

    def along_z(self, step, verb):
        p = self.p

        def go(core):
            for up in (True, False):
                zz, there = self.way(step, up, verb != "wait_recv")
                target = (p.above if up else p.below) if verb == "start" else p.last

                @pl.when(there)
                def _():
                    copy = self.copy(self.layer(zz, core), self.zs.at[step, int(up)], 3 + step * 2 + up, target)
                    getattr(copy, verb)()

        p.by_core(go)

    def add_z(self, step):
        p = self.p
        for up in (True, False):
            zz, there = self.way(step, up, False)

            @pl.when(there)
            def _():
                arrived = self.zs.at[step, int(up)]
                if self.z_first:
                    self.total[zz, p.y, p.x] += arrived[...]
                else:
                    for k in range(2):
                        self.total[(zz, *self.pair(k))] += arrived[k]

    def pair(self, k):
        p = self.p
        return k * (1 - p.c) + p.y * p.c, p.x * (1 - p.c) + k * p.c

    def each(self, make, *verbs):
        def go(core):
            copy = make(core)
            for verb in verbs:
                getattr(copy, verb)()

        self.p.by_core(go)

    def phase(self, number):
        p, early = self.p, self.z_first
        if number == 0:
            self.each(self.take, "start")
            self.each(self.across, "start")
        elif number == 1:
            self.each(self.take, "wait")
            self.each(self.across, "wait_recv")

            @pl.loop(0, 16)
            def _(i):
                self.total[i // 4, i // 2 % 2, i % 2] += self.mine[i // 4, i // 2 % 2, i % 2]

            self.each(self.last, "start")
        elif number == 2:
            self.each(self.last, "wait_recv")

            @pl.loop(0, 8)
            def _(i):
                self.total[(i // 2, *self.pair(i % 2))] += self.lasts[i // 2, i % 2]

            if early:
                self.each(self.first, "start")
            else:
                self.along_z(0, "start")
        elif number == 3:
            if early:
                self.each(self.first, "wait_recv")

                @pl.loop(0, Z)
                def _(i):
                    self.total[i, p.y, p.x] += self.firsts[i]

                self.along_z(0, "start")
            else:
                self.along_z(0, "wait_recv")
                self.add_z(0)
                self.along_z(1, "start")
        elif number == 4:
            step = 0 if early else 1
            self.along_z(step, "wait_recv")
            self.add_z(step)
            self.along_z(step + 1, "start")
        elif number == 5:
            step = 1 if early else 2
            self.along_z(step, "wait_recv")
            self.add_z(step)
            if early:
                self.along_z(2, "start")
            else:
                self.each(self.first, "start")
        elif number == 6:
            if early:
                self.along_z(2, "wait_recv")
                self.add_z(2)
                self.out[...] = self.total[p.z, p.y, p.x].astype(jnp.float32)
            else:
                self.each(self.first, "wait_recv")
                self.out[...] = self.total[p.z, p.y, p.x].astype(jnp.float32) + self.firsts[...].astype(jnp.float32)
        else:
            for make in (self.across, self.last, self.first):
                self.each(make, "wait_send")
            for step in range(3):
                self.along_z(step, "wait_send")


def gather_body(pieces, count, *refs):
    parts, wholes = refs[:count], refs[count : 2 * count]
    send, recv, local = refs[2 * count :]
    place = Place()
    place.barrier()
    work = [
        Gather(place, parts[m], wholes[m], pl.ds(start, size), z_first, (send, recv), k * Gather.SEMS, local.at[k])
        for k, (m, start, size, z_first) in enumerate(pieces)
    ]
    for slot in range(len(work) + Gather.PHASES - 1):
        for k in range(max(0, slot - Gather.PHASES + 1), min(slot, len(work) - 1) + 1):
            work[k].phase(slot - k)


def gather_all(shards):
    count = len(shards)
    parts = [s.reshape(s.shape[0] // 8, 8, s.shape[1]) for s in shards]
    shapes = [jax.ShapeDtypeStruct((Z, 2, 2, 2, *p.shape), p.dtype) for p in parts]
    sems = len(PIECES) * Gather.SEMS
    wholes = pl.pallas_call(
        functools.partial(gather_body, PIECES, count),
        out_shape=shapes,
        in_specs=[pl.BlockSpec(memory_space=pl.ANY)] * count,
        out_specs=[pl.BlockSpec(memory_space=pl.ANY)] * count,
        scratch_shapes=[
            pltpu.SemaphoreType.DMA((sems,)),
            pltpu.SemaphoreType.DMA((sems,)),
            pltpu.SemaphoreType.DMA((len(PIECES),)),
        ],
        compiler_params=pltpu.CompilerParams(collective_id=0, has_side_effects=True),
    )(*parts)
    return [w.reshape(-1, w.shape[-1]) for w in wholes]


def scatter_body(pieces, count, stages, *refs):
    sums, outs = refs[:count], refs[count : 2 * count]
    scratch = list(refs[2 * count :])
    send, recv, local = scratch[:3]
    scratch = scratch[3:]
    mines = {shape: scratch.pop(0) for shape in stages}
    place = Place()
    place.barrier()
    work = []
    for k, (m, start, size, z_first) in enumerate(pieces):
        total, lasts, zs, firsts = (scratch.pop(0) for _ in range(4))
        mine = mines[(sums[m].shape[4], size)]
        work.append(
            Scatter(
                place, sums[m], pl.ds(start, size), z_first, outs[m], total, mine, lasts, zs, firsts,
                (send, recv), k * Scatter.SEMS, local.at[k],
            )
        )
    for slot in range(len(work) + Scatter.PHASES - 1):
        for k in range(max(0, slot - Scatter.PHASES + 1), min(slot, len(work) - 1) + 1):
            work[k].phase(slot - k)


def scatter_all(sums):
    count = len(sums)
    pieces = PIECES[:0:-1]
    parts = [s.reshape(Z, 2, 2, 2, -1, 8, s.shape[1]) for s in sums]
    groups = [p.shape[4] for p in parts]
    stages = sorted({(groups[m], size) for m, _, size, _ in pieces})
    sems = len(pieces) * Scatter.SEMS
    scratch = [
        pltpu.SemaphoreType.DMA((sems,)),
        pltpu.SemaphoreType.DMA((sems,)),
        pltpu.SemaphoreType.DMA((len(pieces),)),
    ]
    scratch += [pltpu.VMEM((Z, 2, 2, r, 8, size), jnp.bfloat16) for r, size in stages]
    for m, _, size, z_first in pieces:
        block = (groups[m], 8, size)
        scratch += [
            pltpu.VMEM((Z, 2, 2, *block), jnp.bfloat16),
            pltpu.VMEM((Z, 2, *block), jnp.bfloat16),
            pltpu.VMEM((3, 2, *(() if z_first else (2,)), *block), jnp.bfloat16),
            pltpu.VMEM((*((Z,) if z_first else ()), *block), jnp.bfloat16),
        ]
    outs = pl.pallas_call(
        functools.partial(scatter_body, pieces, count, stages),
        out_shape=[jax.ShapeDtypeStruct(p.shape[4:], jnp.float32) for p in parts],
        in_specs=[pl.BlockSpec(memory_space=pl.ANY)] * count,
        out_specs=[pl.BlockSpec(memory_space=pltpu.VMEM)] * count,
        scratch_shapes=scratch,
        compiler_params=pltpu.CompilerParams(
            collective_id=1, has_side_effects=True, vmem_limit_bytes=60 * 2**20
        ),
    )(*parts)
    return [o.reshape(-1, o.shape[-1]) for o in outs]


epsilon = 1e-06
masked_value = -1000000000.0


def norm_rows(values, scales):
    return values * lax.rsqrt(jnp.mean(values * values, axis=-1, keepdims=True) + epsilon) * scales


def norm_back(inputs, scales, grad):
    return jax.vjp(lambda v: norm_rows(v, scales), inputs)[1](grad)[0]


def gated_units(united):
    halfway = united.shape[-1] // 2
    return jax.nn.gelu(united[:, :halfway], approximate=True) * united[:, halfway:]


def row_items(lengths, row_count):
    places = jnp.arange(row_count, dtype=jnp.int32)
    count = lengths.shape[0]
    item, boundary = jnp.zeros((row_count,), jnp.int32), jnp.int32(0)
    for k in range(count):
        boundary = boundary + lengths[k]
        item = item + (places >= boundary).astype(jnp.int32)
    return item


def head_split(matrix):
    return matrix.reshape(matrix.shape[0], HEADS, HEAD_DIM)


def outer_rows(left, right):
    return jnp.einsum("rd,re->de", left, right, preferred_element_type=jnp.float32).astype(jnp.bfloat16)


def back_rows(incoming, matrix):
    return jnp.einsum("re,de->rd", incoming, matrix, preferred_element_type=jnp.float32)


def score_rows(query_heads, key_heads, allowed):
    raw_scores = jnp.einsum(
        "qhd,khd->hqk", query_heads, key_heads, preferred_element_type=jnp.float32
    )
    return jnp.where(allowed[None], raw_scores * HEAD_DIM ** (-0.5), masked_value)


def attend_forward(queries, keys_in, values_in, allowed):
    scores = score_rows(head_split(queries), head_split(keys_in), allowed)
    largest = jnp.max(scores, axis=2, keepdims=True)
    expanded = jnp.exp(scores - largest)
    totals = jnp.sum(expanded, axis=2, keepdims=True)
    weights = (expanded / totals).astype(jnp.bfloat16)
    mixed = jnp.einsum(
        "hqk,khd->qhd", weights, head_split(values_in), preferred_element_type=jnp.float32
    )
    return (mixed.reshape(queries.shape[0], D), largest + jnp.log(totals))


def attend_backward(queries, keys_in, values_in, allowed, log_totals, grad_mixed):
    query_heads = head_split(queries)
    key_heads = head_split(keys_in)
    value_heads = head_split(values_in)
    probs = jnp.exp(score_rows(query_heads, key_heads, allowed) - log_totals)
    grad_heads = head_split(grad_mixed)
    grad_values = jnp.einsum(
        "hqk,qhd->khd", probs.astype(jnp.bfloat16), grad_heads, preferred_element_type=jnp.float32
    )
    grad_probs = jnp.einsum(
        "qhd,khd->hqk", grad_heads, value_heads, preferred_element_type=jnp.float32
    )
    centred = grad_probs - jnp.sum(probs * grad_probs, axis=2, keepdims=True)
    grad_scores = (probs * centred * HEAD_DIM ** (-0.5)).astype(jnp.bfloat16)
    grad_queries = jnp.einsum(
        "hqk,khd->qhd", grad_scores, key_heads, preferred_element_type=jnp.float32
    )
    grad_keys = jnp.einsum(
        "hqk,qhd->khd", grad_scores, query_heads, preferred_element_type=jnp.float32
    )
    return (
        grad_queries.reshape(queries.shape[0], D),
        grad_keys.reshape(keys_in.shape[0], D),
        grad_values.reshape(keys_in.shape[0], D),
    )


def self_forward(inputs, params, allowed, live_rows):
    scales, joined, outward = params
    normed = norm_rows(inputs, scales).astype(jnp.bfloat16)
    projected = jnp.dot(normed, joined, preferred_element_type=jnp.float32).astype(jnp.bfloat16)
    mixed, log_totals = attend_forward(
        projected[:, :D], projected[:, D : 2 * D], projected[:, 2 * D :], allowed
    )
    mixed_low = mixed.astype(jnp.bfloat16)
    branch = jnp.dot(mixed_low, outward, preferred_element_type=jnp.float32)
    return (inputs + live_rows[:, None] * branch, (normed, projected, mixed_low, log_totals))


def self_backward(inputs, params, allowed, live_rows, stored, incoming):
    scales, joined, outward = params
    normed, projected, mixed_low, log_totals = stored
    grad_branch = (live_rows[:, None] * incoming).astype(jnp.bfloat16)
    grad_outward = outer_rows(mixed_low, grad_branch)
    grad_mixed = back_rows(grad_branch, outward).astype(jnp.bfloat16)
    grad_parts = attend_backward(
        projected[:, :D],
        projected[:, D : 2 * D],
        projected[:, 2 * D :],
        allowed,
        log_totals,
        grad_mixed,
    )
    grad_projected = jnp.concatenate(grad_parts, axis=1).astype(jnp.bfloat16)
    grad_joined = outer_rows(normed, grad_projected)
    grad_inputs = norm_back(inputs, scales, back_rows(grad_projected, joined))
    return (incoming + grad_inputs, (grad_joined, grad_outward))


def cross_forward(inputs, memory, params, allowed, live_rows):
    scales, memory_scales, query_map, pair_map, outward = params
    normed = norm_rows(inputs, scales).astype(jnp.bfloat16)
    memory_normed = norm_rows(memory, memory_scales).astype(jnp.bfloat16)
    queries = jnp.dot(normed, query_map, preferred_element_type=jnp.float32).astype(jnp.bfloat16)
    pairs = jnp.dot(memory_normed, pair_map, preferred_element_type=jnp.float32).astype(
        jnp.bfloat16
    )
    mixed, log_totals = attend_forward(queries, pairs[:, :D], pairs[:, D:], allowed)
    mixed_low = mixed.astype(jnp.bfloat16)
    branch = jnp.dot(mixed_low, outward, preferred_element_type=jnp.float32)
    return (
        inputs + live_rows[:, None] * branch,
        (normed, memory_normed, queries, pairs, mixed_low, log_totals),
    )


def cross_backward(inputs, memory, params, allowed, live_rows, stored, incoming):
    scales, memory_scales, query_map, pair_map, outward = params
    normed, memory_normed, queries, pairs, mixed_low, log_totals = stored
    grad_branch = (live_rows[:, None] * incoming).astype(jnp.bfloat16)
    grad_outward = outer_rows(mixed_low, grad_branch)
    grad_mixed = back_rows(grad_branch, outward).astype(jnp.bfloat16)
    grad_queries, grad_keys, grad_values = attend_backward(
        queries, pairs[:, :D], pairs[:, D:], allowed, log_totals, grad_mixed
    )
    grad_queries_low = grad_queries.astype(jnp.bfloat16)
    grad_pairs = jnp.concatenate([grad_keys, grad_values], axis=1).astype(jnp.bfloat16)
    grad_query_map = outer_rows(normed, grad_queries_low)
    grad_pair_map = outer_rows(memory_normed, grad_pairs)
    grad_inputs = norm_back(inputs, scales, back_rows(grad_queries_low, query_map))
    grad_memory = norm_back(memory, memory_scales, back_rows(grad_pairs, pair_map))
    return (
        incoming + grad_inputs,
        grad_memory,
        (grad_query_map, grad_pair_map, grad_outward),
    )


def mlp_forward(inputs, params, live_rows):
    scales, inward, outward = params
    normed = norm_rows(inputs, scales).astype(jnp.bfloat16)
    united = jnp.dot(normed, inward, preferred_element_type=jnp.float32)
    activated = gated_units(united).astype(jnp.bfloat16)
    branch = jnp.dot(activated, outward, preferred_element_type=jnp.float32)
    return (inputs + live_rows[:, None] * branch, (normed, united, activated))


def mlp_backward(inputs, params, live_rows, stored, incoming):
    scales, inward, outward = params
    normed, united, activated = stored
    grad_branch = (live_rows[:, None] * incoming).astype(jnp.bfloat16)
    grad_outward = outer_rows(activated, grad_branch)
    grad_activated = back_rows(grad_branch, outward)
    _, pullback = jax.vjp(gated_units, united)
    grad_united = pullback(grad_activated)[0].astype(jnp.bfloat16)
    grad_inward = outer_rows(normed, grad_united)
    grad_inputs = norm_back(inputs, scales, back_rows(grad_united, inward))
    return (incoming + grad_inputs, (grad_inward, grad_outward))


def plain_gather(shards):
    return [lax.all_gather(s, AXES, axis=0, tiled=True) for s in shards]


def plain_scatter(sums):
    return [lax.psum_scatter(s.astype(jnp.float32), AXES, scatter_dimension=0, tiled=True) for s in sums]


SCALE_OF = (0, None, 1, None, 2, None, 3, 4, None, 5, None)


def per_device(
    linked,
    enc_input,
    dec_input,
    enc_lengths,
    dec_lengths,
    enc_attn_gain,
    enc_qkv,
    enc_attn_out,
    enc_mlp_gain,
    enc_mlp_in,
    enc_mlp_out,
    dec_self_gain,
    dec_qkv,
    dec_self_out,
    cross_gain,
    memory_gain,
    cross_query,
    cross_kv,
    cross_out,
    dec_mlp_gain,
    dec_mlp_in,
    dec_mlp_out,
    enc_cotangent,
    dec_cotangent,
):
    item_count = enc_lengths.shape[0]
    enc_items = row_items(enc_lengths, enc_input.shape[0])
    dec_items = row_items(dec_lengths, dec_input.shape[0])
    enc_live = (enc_items < item_count).astype(jnp.float32)
    dec_live = (dec_items < item_count).astype(jnp.float32)
    enc_padded = enc_items[:, None] == item_count
    dec_padded = dec_items[:, None] == item_count
    enc_allowed = (enc_items[:, None] == enc_items[None, :]) | enc_padded
    dec_places = jnp.arange(dec_input.shape[0], dtype=jnp.int32)
    self_allowed = (dec_items[:, None] == dec_items[None, :]) & (
        dec_places[None, :] <= dec_places[:, None]
    ) | dec_padded
    cross_allowed = (dec_items[:, None] == enc_items[None, :]) | dec_padded
    scales = [
        g.astype(jnp.float32)
        for g in (enc_attn_gain, enc_mlp_gain, dec_self_gain, cross_gain, memory_gain, dec_mlp_gain)
    ]
    shards = (
        enc_qkv, enc_attn_out, enc_mlp_in, enc_mlp_out, dec_qkv, dec_self_out,
        cross_query, cross_kv, cross_out, dec_mlp_in, dec_mlp_out,
    )
    if linked:
        mine = lax.axis_index("wide") * lax.axis_size("narrow") + lax.axis_index("narrow")
        columns = jnp.arange(D, dtype=jnp.int32) // scales[0].shape[0] == mine
        rows = [jnp.where(columns, jnp.tile(g, D // g.shape[0]), 0.0) for g in scales]
        rows += [jnp.zeros((D,), jnp.float32)] * (8 - len(rows))
        *whole, spread = gather_all((*shards, jnp.stack(rows).astype(jnp.bfloat16)))
        gains = jnp.sum(spread.reshape(-1, 8, D).astype(jnp.float32), axis=0)
    else:
        whole = plain_gather(shards)
        gains = plain_gather(scales)
    encoder_start = enc_input.astype(jnp.float32)
    enc_middle, enc_attn_store = self_forward(encoder_start, (gains[0], *whole[0:2]), enc_allowed, enc_live)
    encoder_final, enc_mlp_store = mlp_forward(enc_middle, (gains[1], *whole[2:4]), enc_live)
    decoder_start = dec_input.astype(jnp.float32)
    dec_middle, dec_self_store = self_forward(decoder_start, (gains[2], *whole[4:6]), self_allowed, dec_live)
    dec_crossed, cross_store = cross_forward(
        dec_middle, encoder_final, (gains[3], gains[4], *whole[6:9]), cross_allowed, dec_live
    )
    decoder_final, dec_mlp_store = mlp_forward(dec_crossed, (gains[5], *whole[9:11]), dec_live)
    grad_crossed, dec_mlp_grads = mlp_backward(
        dec_crossed, (gains[5], *whole[9:11]), dec_live, dec_mlp_store, dec_cotangent.astype(jnp.float32)
    )
    grad_middle, grad_memory, cross_grads = cross_backward(
        dec_middle,
        encoder_final,
        (gains[3], gains[4], *whole[6:9]),
        cross_allowed,
        dec_live,
        cross_store,
        grad_crossed,
    )
    grad_decoder_start, dec_self_grads = self_backward(
        decoder_start, (gains[2], *whole[4:6]), self_allowed, dec_live, dec_self_store, grad_middle
    )
    grad_enc_middle, enc_mlp_grads = mlp_backward(
        enc_middle,
        (gains[1], *whole[2:4]),
        enc_live,
        enc_mlp_store,
        enc_cotangent.astype(jnp.float32) + grad_memory,
    )
    grad_encoder_start, enc_attn_grads = self_backward(
        encoder_start, (gains[0], *whole[0:2]), enc_allowed, enc_live, enc_attn_store, grad_enc_middle
    )
    sums = enc_attn_grads + enc_mlp_grads + dec_self_grads + cross_grads + dec_mlp_grads
    summed = (scatter_all if linked else plain_scatter)(sums)
    grads, scale_grads = [], {}
    for total, shard, k in zip(summed, shards, SCALE_OF):
        if k is not None:
            scale_grads[k] = jnp.sum(total * shard.astype(jnp.float32), axis=1) / scales[k]
        grads.append(total)
    return (
        encoder_final.astype(jnp.bfloat16),
        decoder_final.astype(jnp.bfloat16),
        grad_encoder_start,
        grad_decoder_start,
        scale_grads[0], grads[0], grads[1],
        scale_grads[1], grads[2], grads[3],
        scale_grads[2], grads[4], grads[5],
        scale_grads[3], scale_grads[4], grads[6], grads[7], grads[8],
        scale_grads[5], grads[9], grads[10],
    )


def solution(mesh):
    rows, line = P(AXES, None), P(AXES)
    linked = mesh.shape["wide"] == 2 * Z and mesh.shape["narrow"] == 4
    weights = (
        line, rows, rows, line, rows, rows, line, rows, rows,
        line, line, rows, rows, rows, line, rows, rows,
    )
    return jax.shard_map(
        functools.partial(per_device, linked),
        mesh=mesh,
        in_specs=(rows, rows, line, line, *weights, rows, rows),
        out_specs=(rows, rows, rows, rows, *weights),
        check_vma=False,
    )
```

```python
import functools

import jax
import jax.numpy as jnp
from jax import lax
from jax.experimental import pallas as pl
from jax.experimental.pallas import tpu as pltpu
from jax.sharding import PartitionSpec as P

D = 768
HEADS = 12
HEAD_DIM = 64
FF = 2048
AXES = ("wide", "narrow")
MESH = pl.DeviceIdType.MESH

Z = 4
PIECES = (
    (11, 0, 768, False),
    (0, 0, 1152, False), (0, 1152, 1152, True), (1, 0, 768, False),
    (2, 0, 1024, False), (2, 1024, 1024, True), (2, 2048, 1024, False), (2, 3072, 1024, False),
    (3, 0, 384, True), (3, 384, 384, False),
    (4, 0, 1152, False), (4, 1152, 1152, True), (5, 0, 768, False), (6, 0, 768, False),
    (7, 0, 768, True), (7, 768, 768, False), (8, 0, 768, False),
    (9, 0, 1024, True), (9, 1024, 1024, False), (9, 2048, 1024, False), (9, 3072, 1024, True),
    (10, 0, 384, False), (10, 384, 384, False),
)
STRIDE = 2


class Place:
    def __init__(self):
        self.w, self.n = lax.axis_index("wide"), lax.axis_index("narrow")
        self.z, self.y = self.w // 2, self.w % 2
        self.x, self.c = self.n // 2, self.n % 2
        w, n, y, x, c = self.w, self.n, self.y, self.x, self.c
        self.sibling = (w, n + 1 - 2 * c)
        self.first = (w + (1 - c) * (1 - 2 * y), n + c * (2 - 4 * x))
        self.last = (w + c * (1 - 2 * y), n + (1 - c) * (2 - 4 * x))
        self.above = (w + 2, n)
        self.below = (w - 2, n)

    def barrier(self):
        sem = pltpu.get_barrier_semaphore()
        for device in (self.sibling, self.first, self.last):
            pl.semaphore_signal(sem, inc=1, device_id=device, device_id_type=MESH)

        @pl.when(self.z < Z - 1)
        def _():
            pl.semaphore_signal(sem, inc=1, device_id=self.above, device_id_type=MESH)

        @pl.when(self.z > 0)
        def _():
            pl.semaphore_signal(sem, inc=1, device_id=self.below, device_id_type=MESH)

        inner = jnp.where(self.z * (Z - 1 - self.z) > 0, 1, 0)
        pl.semaphore_wait(sem, 4 + inner)

    def by_core(self, do):
        @pl.when(self.c == 0)
        def _():
            do(0)

        @pl.when(self.c == 1)
        def _():
            do(1)


def remote(src, dst, sems, index, device):
    send, recv = sems
    return pltpu.make_async_remote_copy(
        src_ref=src, dst_ref=dst, send_sem=send.at[index], recv_sem=recv.at[index],
        device_id=device, device_id_type=MESH,
    )


class Gather:
    PHASES = 7
    SEMS = 10

    def __init__(self, place, part, whole, columns, z_first, sems, base, local_sem):
        self.p, self.z_first, self.sems, self.base = place, z_first, sems, base
        self.part = part.at[:, :, columns]
        self.whole = whole.at[:, :, :, :, :, :, columns]
        self.local = pltpu.make_async_copy(self.part, self.own(), local_sem)

    def own(self):
        p = self.p
        return self.whole.at[p.z, p.y, p.x, p.c]

    def copy(self, src, dst, slot, device):
        return remote(src, dst, self.sems, self.base + slot, device)

    def layer(self, zz, core):
        p = self.p
        if self.z_first:
            return self.whole.at[zz, p.y, p.x, core]
        return self.whole.at[zz, :, p.x, 0] if core == 0 else self.whole.at[zz, p.y, :, 1]

    def half(self, core, mine):
        p = self.p
        if core == 0:
            return self.whole.at[:, :, p.x if mine else 1 - p.x, 0]
        return self.whole.at[:, p.y if mine else 1 - p.y, :, 1]

    def along_z(self, step, sending):
        p = self.p

        def go(core):
            for up in (True, False):
                if sending:
                    zz = p.z - step if up else p.z + step
                    there = (p.z < Z - 1) & (zz >= 0) if up else (p.z > 0) & (zz < Z)
                else:
                    zz = p.z - 1 - step if up else p.z + 1 + step
                    there = zz >= 0 if up else zz < Z

                target = (p.above if up else p.below) if sending else p.last

                @pl.when(there)
                def _():
                    block = self.layer(zz, core)
                    copy = self.copy(block, block, 1 + step * 2 + up, target)
                    copy.start() if sending else copy.wait_recv()

        p.by_core(go)

    def along_z_sent(self):
        p = self.p

        def go(core):
            for step in range(3):
                for up in (True, False):
                    zz = p.z - step if up else p.z + step
                    there = (p.z < Z - 1) & (zz >= 0) if up else (p.z > 0) & (zz < Z)

                    @pl.when(there)
                    def _():
                        block = self.layer(zz, core)
                        self.copy(block, block, 1 + step * 2 + up, p.last).wait_send()

        p.by_core(go)

    def first(self, core):
        p = self.p
        if not self.z_first:
            return self.copy(self.part, self.own(), 0, p.first)
        block = self.whole.at[:, p.y, p.x, core]
        return self.copy(block, block, 0, p.first)

    def last(self, core):
        block = self.half(core, True)
        return self.copy(block, block, 7, self.p.last)

    def across(self, core, mine):
        block = self.half(core, mine)
        return self.copy(block, block, 8 if mine else 9, self.p.sibling)

    def each(self, make, *verbs):
        def go(core):
            copy = make(core)
            for verb in verbs:
                getattr(copy, verb)()

        self.p.by_core(go)

    def phase(self, number):
        early = not self.z_first
        if number == 0:
            self.local.start()
            if early:
                self.each(self.first, "start")
            self.local.wait()
            if not early:
                self.along_z(0, True)
        elif number == 1:
            if early:
                self.each(self.first, "wait_recv")
                self.along_z(0, True)
            else:
                self.along_z(0, False)
                self.along_z(1, True)
        elif number == 2:
            self.along_z(0 if early else 1, False)
            self.along_z(1 if early else 2, True)
        elif number == 3:
            self.along_z(1 if early else 2, False)
            if early:
                self.along_z(2, True)
            else:
                self.each(self.first, "start")
        elif number == 4:
            if early:
                self.along_z(2, False)
            else:
                self.each(self.first, "wait_recv")
            self.each(self.last, "start")
            self.each(lambda core: self.across(core, True), "start")
        elif number == 5:
            self.each(self.last, "wait_recv")
            self.each(lambda core: self.across(core, False), "start")
        else:
            for core in (0, 1):
                @pl.when(self.p.c == core)
                def _():
                    for mine in (True, False):
                        self.across(1 - core, mine).wait_recv()
                        self.across(core, mine).wait_send()
                    self.first(core).wait_send()
                    self.last(core).wait_send()
            self.along_z_sent()


class Scatter:
    PHASES = 8
    SEMS = 9

    def __init__(self, place, parts, columns, z_first, out, total, mine, lasts, zs, firsts, sems, base, local_sem):
        self.p, self.z_first, self.sems, self.base = place, z_first, sems, base
        self.parts = parts.at[:, :, :, :, :, :, columns]
        self.out = out.at[:, :, columns]
        self.total, self.mine, self.lasts, self.zs, self.firsts = total, mine, lasts, zs, firsts
        self.local_sem = local_sem

    def copy(self, src, dst, slot, device):
        return remote(src, dst, self.sems, self.base + slot, device)

    def spot(self, core, last, first=None):
        every = slice(None)
        if first is None:
            return (every, last) if core else (every, every, last)
        return (last, first) if core else (first, last)

    def place_of(self, core):
        p = self.p
        return (p.y, p.x) if core else (p.x, p.y)

    def across(self, core):
        return self.copy(self.parts.at[:, :, :, 1 - core], self.total, 0, self.p.sibling)

    def take(self, core):
        return pltpu.make_async_copy(self.parts.at[:, :, :, core], self.mine, self.local_sem)

    def last(self, core):
        last, _ = self.place_of(core)
        return self.copy(self.total.at[self.spot(core, 1 - last)], self.lasts, 1, self.p.last)

    def first(self, core):
        p = self.p
        last, first = self.place_of(core)
        if self.z_first:
            src = self.total.at[(slice(None), *self.spot(core, last, 1 - first))]
        else:
            src = self.total.at[(p.z, *self.spot(core, last, 1 - first))]
        return self.copy(src, self.firsts, 2, p.first)

    def layer(self, zz, core):
        last, first = self.place_of(core)
        if self.z_first:
            return self.total.at[(zz, *self.spot(core, last, first))]
        return self.total.at[(zz, *self.spot(core, last)[1:])]

    def way(self, step, up, sending):
        z, far = self.p.z, 2 - step
        if sending:
            zz = z + 1 + far if up else z - 1 - far
            return zz, zz < Z if up else zz >= 0
        zz = z + far if up else z - far
        return zz, (z > 0) & (zz < Z) if up else (z < Z - 1) & (zz >= 0)

    def along_z(self, step, verb):
        p = self.p

        def go(core):
            for up in (True, False):
                zz, there = self.way(step, up, verb != "wait_recv")
                target = (p.above if up else p.below) if verb == "start" else p.last

                @pl.when(there)
                def _():
                    copy = self.copy(self.layer(zz, core), self.zs.at[step, int(up)], 3 + step * 2 + up, target)
                    getattr(copy, verb)()

        p.by_core(go)

    def add_z(self, step):
        p = self.p
        for up in (True, False):
            zz, there = self.way(step, up, False)

            @pl.when(there)
            def _():
                arrived = self.zs.at[step, int(up)]
                if self.z_first:
                    self.total[zz, p.y, p.x] += arrived[...]
                else:
                    for k in range(2):
                        self.total[(zz, *self.pair(k))] += arrived[k]

    def pair(self, k):
        p = self.p
        return k * (1 - p.c) + p.y * p.c, p.x * (1 - p.c) + k * p.c

    def each(self, make, *verbs):
        def go(core):
            copy = make(core)
            for verb in verbs:
                getattr(copy, verb)()

        self.p.by_core(go)

    def phase(self, number):
        p, early = self.p, self.z_first
        if number == 0:
            self.each(self.take, "start")
            self.each(self.across, "start")
        elif number == 1:
            self.each(self.take, "wait")
            self.each(self.across, "wait_recv")

            @pl.loop(0, 16)
            def _(i):
                self.total[i // 4, i // 2 % 2, i % 2] += self.mine[i // 4, i // 2 % 2, i % 2]

            self.each(self.last, "start")
        elif number == 2:
            self.each(self.last, "wait_recv")

            @pl.loop(0, 8)
            def _(i):
                self.total[(i // 2, *self.pair(i % 2))] += self.lasts[i // 2, i % 2]

            if early:
                self.each(self.first, "start")
            else:
                self.along_z(0, "start")
        elif number == 3:
            if early:
                self.each(self.first, "wait_recv")

                @pl.loop(0, Z)
                def _(i):
                    self.total[i, p.y, p.x] += self.firsts[i]

                self.along_z(0, "start")
            else:
                self.along_z(0, "wait_recv")
                self.add_z(0)
                self.along_z(1, "start")
        elif number == 4:
            step = 0 if early else 1
            self.along_z(step, "wait_recv")
            self.add_z(step)
            self.along_z(step + 1, "start")
        elif number == 5:
            step = 1 if early else 2
            self.along_z(step, "wait_recv")
            self.add_z(step)
            if early:
                self.along_z(2, "start")
            else:
                self.each(self.first, "start")
        elif number == 6:
            if early:
                self.along_z(2, "wait_recv")
                self.add_z(2)
                self.out[...] = self.total[p.z, p.y, p.x].astype(jnp.float32)
            else:
                self.each(self.first, "wait_recv")
                self.out[...] = self.total[p.z, p.y, p.x].astype(jnp.float32) + self.firsts[...].astype(jnp.float32)
        else:
            for make in (self.across, self.last, self.first):
                self.each(make, "wait_send")
            for step in range(3):
                self.along_z(step, "wait_send")


epsilon = 1e-06
masked_value = -1000000000.0
SHRINK = HEAD_DIM**-0.5
NT = (((1,), (1,)), ((), ()))
TN = (((0,), (0,)), ((), ()))
f32, bf16 = jnp.float32, jnp.bfloat16


def dot(a, b, dims=(((1,), (0,)), ((), ()))):
    return lax.dot_general(a, b, dims, preferred_element_type=f32)


def shrunk(values):
    return lax.rsqrt(jnp.mean(values * values, axis=-1, keepdims=True) + epsilon)


def norm(values, scales):
    return values * shrunk(values) * scales


def items_of(lengths_ref, places):
    item, boundary = jnp.zeros_like(places), 0
    for k in range(lengths_ref.shape[0]):
        boundary = boundary + lengths_ref[k]
        item = item + jnp.where(places >= boundary, 1, 0)
    return item


def fill_masks(enc_lengths, dec_lengths, enc_mask, self_mask, cross_mask):
    count = enc_lengths.shape[0]

    def grid(ref, axis):
        return lax.broadcasted_iota(jnp.int32, ref.shape, axis)

    def put(ref, rows, columns, both):
        kept = rows == columns
        if both is not None:
            kept = kept & both
        ref[...] = jnp.where(kept | (rows == count), 1.0, 0.0)

    put(enc_mask, items_of(enc_lengths, grid(enc_mask, 0)), items_of(enc_lengths, grid(enc_mask, 1)), None)
    put(
        self_mask, items_of(dec_lengths, grid(self_mask, 0)), items_of(dec_lengths, grid(self_mask, 1)),
        grid(self_mask, 1) <= grid(self_mask, 0),
    )
    put(cross_mask, items_of(dec_lengths, grid(cross_mask, 0)), items_of(enc_lengths, grid(cross_mask, 1)), None)


def live_rows(lengths_ref, rows):
    item = items_of(lengths_ref, lax.broadcasted_iota(jnp.int32, (rows, 1), 0))
    return jnp.where(item < lengths_ref.shape[0], 1.0, 0.0)


def head_lanes(which):
    lanes = lax.broadcasted_iota(jnp.int32, (1, 2 * HEAD_DIM), 1)
    return jnp.where(lanes // HEAD_DIM == which, 1.0, 0.0).astype(bf16)


def head_probs(q, k, kept):
    scores = jnp.where(kept[...] > 0.0, dot(q, k, NT) * SHRINK, masked_value)
    raised = jnp.exp(scores - jnp.max(scores, axis=1, keepdims=True))
    return raised * (1.0 / jnp.sum(raised, axis=1, keepdims=True))


def pair_columns(pair, offset):
    return pl.ds(pl.multiple_of(pair * (2 * HEAD_DIM) + offset, 2 * HEAD_DIM), 2 * HEAD_DIM)


def attend(q_ref, q_at, k_ref, k_at, v_ref, v_at, kept, out_ref):
    @pl.loop(0, HEADS // 2)
    def _(pair):
        q = q_ref[:, pair_columns(pair, q_at)]
        k = k_ref[:, pair_columns(pair, k_at)]
        v = v_ref[:, pair_columns(pair, v_at)]
        mixed = None
        for which in range(2):
            lanes = head_lanes(which)
            part = dot(head_probs(q * lanes, k, kept).astype(bf16), v * lanes)
            mixed = part if mixed is None else mixed + part
        out_ref[:, pair_columns(pair, 0)] = mixed.astype(bf16)


def gelu_tanh(t):
    return jnp.tanh(0.7978845608028654 * (t + 0.044715 * (t * t * t)))


STORED = (
    ("e_h1", "enc", D, bf16), ("e_qkv", "enc", 3 * D, bf16), ("e_o", "enc", D, bf16), ("e_x1", "enc", D, f32),
    ("e_h2", "enc", D, bf16), ("e_u", "enc", 2 * FF, bf16), ("e_a", "enc", FF, bf16), ("e_x2", "enc", D, f32),
    ("hm", "enc", D, bf16), ("kv", "enc", 2 * D, bf16),
    ("d_h1", "dec", D, bf16), ("d_qkv", "dec", 3 * D, bf16), ("d_o", "dec", D, bf16), ("d_x1", "dec", D, f32),
    ("hq", "dec", D, bf16), ("q", "dec", D, bf16), ("c_o", "dec", D, bf16), ("d_x2", "dec", D, f32),
    ("d_h2", "dec", D, bf16), ("d_u", "dec", 2 * FF, bf16), ("d_a", "dec", FF, bf16),
)


class Forward:
    def __init__(self, refs, lengths):
        self.__dict__.update(refs)
        self.lengths = lengths

    def gain(self, k):
        return self.gains[k : k + 1]

    def set_norm(self, values, k, out):
        out[...] = norm(values, self.gain(k)).astype(bf16)

    def step(self, m, start, size, weight):
        columns = pl.ds(start, size)
        if m == 0 or m == 4:
            side = "e" if m == 0 else "d"
            if start == 0:
                self.set_norm(getattr(self, side + "_x0")[...].astype(f32), 0 if m == 0 else 2, getattr(self, side + "_h1"))
            qkv = getattr(self, side + "_qkv")
            qkv[:, columns] = dot(getattr(self, side + "_h1")[...], weight).astype(bf16)
            if start + size == qkv.shape[1]:
                kept = self.enc_mask if m == 0 else self.self_mask
                attend(qkv, 0, qkv, D, qkv, 2 * D, kept, getattr(self, side + "_o"))
        elif m == 1:
            self.e_x1[...] = self.e_x0[...].astype(f32) + self.live("enc") * dot(self.e_o[...], weight)
            self.set_norm(self.e_x1[...], 1, self.e_h2)
        elif m == 5:
            self.d_x1[...] = self.d_x0[...].astype(f32) + self.live("dec") * dot(self.d_o[...], weight)
            self.set_norm(self.d_x1[...], 3, self.hq)
        elif m == 6:
            self.q[...] = dot(self.hq[...], weight).astype(bf16)
        elif m == 7:
            self.kv[:, columns] = dot(self.hm[...], weight).astype(bf16)
            if start + size == self.kv.shape[1]:
                attend(self.q, 0, self.kv, 0, self.kv, D, self.cross_mask, self.c_o)
        elif m == 8:
            self.d_x2[...] = self.d_x1[...] + self.live("dec") * dot(self.c_o[...], weight)
            self.set_norm(self.d_x2[...], 5, self.d_h2)
        elif m == 2 or m == 9:
            side = "e" if m == 2 else "d"
            rows = getattr(self, side + "_h2").shape[0]
            united = dot(getattr(self, side + "_h2")[...], weight)
            getattr(self, side + "_u")[:, columns] = united.astype(bf16)
            half = FF
            if start < half:
                self.gates[pl.ds(0, rows), columns] = united
            else:
                back = pl.ds(start - half, size)
                gate = self.gates[pl.ds(0, rows), back]
                getattr(self, side + "_a")[:, back] = (0.5 * gate * (1.0 + gelu_tanh(gate)) * united).astype(bf16)
        else:
            side, other = ("e", "enc") if m == 3 else ("d", "dec")
            before = self.e_x1 if m == 3 else self.d_x2
            after = before[:, columns] + self.live(other) * dot(getattr(self, side + "_a")[...], weight)
            out = self.enc_out if m == 3 else self.dec_out
            out[:, columns] = after.astype(bf16)
            if m == 3:
                self.e_x2[:, columns] = after
                if start + size == D:
                    self.set_norm(self.e_x2[...], 4, self.hm)

    def live(self, side):
        ref = self.e_x0 if side == "enc" else self.d_x0
        return live_rows(self.lengths[side], ref.shape[0])


def forward_body(pieces, count, *refs):
    refs = list(refs)

    def take(n):
        got = refs[:n]
        del refs[:n]
        return got

    parts = take(count)
    e_x0, d_x0, enc_lengths, dec_lengths = take(4)
    wholes = take(count)
    stored = dict(zip([name for name, *_ in STORED], take(len(STORED))))
    enc_out, dec_out, gains = take(3)
    send, recv, local, stage_sem, spread, gates, enc_mask, self_mask, cross_mask, wide_stage, deep_stage = refs
    place = Place()
    place.barrier()
    work = [
        Gather(place, parts[m], wholes[m], pl.ds(start, size), z_first, (send, recv), k * Gather.SEMS, local.at[k])
        for k, (m, start, size, z_first) in enumerate(pieces)
    ]
    forward = Forward(
        dict(
            stored, e_x0=e_x0, d_x0=d_x0, enc_out=enc_out, dec_out=dec_out, gains=gains, gates=gates,
            enc_mask=enc_mask, self_mask=self_mask, cross_mask=cross_mask,
        ),
        {"enc": enc_lengths, "dec": dec_lengths},
    )

    def staged(k):
        m, start, size, _ = pieces[k]
        if m == len(parts) - 1:
            into = spread
        elif parts[m].shape[0] > 3:
            into = deep_stage.at[k % STAGES, ..., pl.ds(0, size)]
        else:
            into = wide_stage.at[k % STAGES, ..., pl.ds(0, size)]
        return pltpu.make_async_copy(wholes[m].at[..., pl.ds(start, size)], into, stage_sem.at[k % STAGES])

    last = STRIDE * (Gather.PHASES - 1)
    for slot in range(len(work) + last + 1):
        for k in range(len(work)):
            if (slot - k) % STRIDE == 0 and 0 <= slot - k <= last:
                work[k].phase((slot - k) // STRIDE)
        if slot == 0:
            fill_masks(enc_lengths, dec_lengths, enc_mask, self_mask, cross_mask)
        if 0 <= slot - last < len(work):
            staged(slot - last).start()
        k = slot - last - 1
        if k >= 0:
            staged(k).wait()
            m, start, size, _ = pieces[k]
            if m == len(parts) - 1:
                gains[...] = jnp.sum(spread[...].reshape(-1, 8, D).astype(f32), axis=0)
            else:
                stage = deep_stage if parts[m].shape[0] > 3 else wide_stage
                weight = stage[k % STAGES, ..., pl.ds(0, size)]
                forward.step(m, start, size, weight.reshape(-1, size))


STAGES = 2


def forward_all(shards, enc_input, dec_input, enc_lengths, dec_lengths):
    count = len(shards)
    parts = [s.reshape(s.shape[0] // 8, 8, s.shape[1]) for s in shards]
    sems = len(PIECES) * Gather.SEMS
    rows = {"enc": enc_input.shape[0], "dec": dec_input.shape[0]}
    hbm, vmem = pl.BlockSpec(memory_space=pl.ANY), pl.BlockSpec(memory_space=pltpu.VMEM)
    smem = pl.BlockSpec(memory_space=pltpu.SMEM)
    widest = max(size for m, _, size, _ in PIECES if parts[m].shape[0] == 3)
    deep = max((parts[m].shape[0], size) for m, _, size, _ in PIECES)
    outs = pl.pallas_call(
        functools.partial(forward_body, PIECES, count),
        out_shape=[jax.ShapeDtypeStruct((Z, 2, 2, 2, *p.shape), p.dtype) for p in parts]
        + [jax.ShapeDtypeStruct((rows[side], columns), dtype) for _, side, columns, dtype in STORED]
        + [
            jax.ShapeDtypeStruct(enc_input.shape, bf16),
            jax.ShapeDtypeStruct(dec_input.shape, bf16),
            jax.ShapeDtypeStruct((8, D), f32),
        ],
        in_specs=[hbm] * count + [vmem, vmem, smem, smem],
        out_specs=[hbm] * count + [vmem] * (len(STORED) + 3),
        scratch_shapes=[
            pltpu.SemaphoreType.DMA((sems,)),
            pltpu.SemaphoreType.DMA((sems,)),
            pltpu.SemaphoreType.DMA((len(PIECES),)),
            pltpu.SemaphoreType.DMA((STAGES,)),
            pltpu.VMEM((Z, 2, 2, 2, 1, 8, D), bf16),
            pltpu.VMEM((rows["enc"], FF), f32),
            pltpu.VMEM((rows["enc"], rows["enc"]), f32),
            pltpu.VMEM((rows["dec"], rows["dec"]), f32),
            pltpu.VMEM((rows["dec"], rows["enc"]), f32),
            pltpu.VMEM((STAGES, Z, 2, 2, 2, 3, 8, widest), bf16),
            pltpu.VMEM((STAGES, Z, 2, 2, 2, deep[0], 8, deep[1]), bf16),
        ],
        compiler_params=pltpu.CompilerParams(
            collective_id=0, has_side_effects=True, vmem_limit_bytes=60 * 2**20
        ),
    )(*parts, enc_input, dec_input, enc_lengths, dec_lengths)
    wholes, stored, (enc_out, dec_out, gains) = outs[:count], outs[count:-3], outs[-3:]
    stored = dict(zip([name for name, *_ in STORED], stored))
    return wholes, stored, enc_out, dec_out, gains


def scatter_body(pieces, count, stages, *refs):
    sums, outs = refs[:count], refs[count : 2 * count]
    scratch = list(refs[2 * count :])
    send, recv, local = scratch[:3]
    scratch = scratch[3:]
    mines = {shape: scratch.pop(0) for shape in stages}
    place = Place()
    place.barrier()
    work = []
    for k, (m, start, size, z_first) in enumerate(pieces):
        total, lasts, zs, firsts = (scratch.pop(0) for _ in range(4))
        mine = mines[(sums[m].shape[4], size)].at[k % STRIDE]
        work.append(
            Scatter(
                place, sums[m], pl.ds(start, size), z_first, outs[m], total, mine, lasts, zs, firsts,
                (send, recv), k * Scatter.SEMS, local.at[k],
            )
        )
    for slot in range(len(work) + STRIDE * (Scatter.PHASES - 1)):
        for k in range(len(work)):
            if (slot - k) % STRIDE == 0 and 0 <= slot - k <= STRIDE * (Scatter.PHASES - 1):
                work[k].phase((slot - k) // STRIDE)


def scatter_all(sums):
    count = len(sums)
    pieces = PIECES[:0:-1]
    parts = [s.reshape(Z, 2, 2, 2, -1, 8, s.shape[1]) for s in sums]
    groups = [p.shape[4] for p in parts]
    stages = sorted({(groups[m], size) for m, _, size, _ in pieces})
    sems = len(pieces) * Scatter.SEMS
    scratch = [
        pltpu.SemaphoreType.DMA((sems,)),
        pltpu.SemaphoreType.DMA((sems,)),
        pltpu.SemaphoreType.DMA((len(pieces),)),
    ]
    scratch += [pltpu.VMEM((STRIDE, Z, 2, 2, r, 8, size), jnp.bfloat16) for r, size in stages]
    for m, _, size, z_first in pieces:
        block = (groups[m], 8, size)
        scratch += [
            pltpu.VMEM((Z, 2, 2, *block), jnp.bfloat16),
            pltpu.VMEM((Z, 2, *block), jnp.bfloat16),
            pltpu.VMEM((3, 2, *(() if z_first else (2,)), *block), jnp.bfloat16),
            pltpu.VMEM((*((Z,) if z_first else ()), *block), jnp.bfloat16),
        ]
    outs = pl.pallas_call(
        functools.partial(scatter_body, pieces, count, stages),
        out_shape=[jax.ShapeDtypeStruct(p.shape[4:], jnp.float32) for p in parts],
        in_specs=[pl.BlockSpec(memory_space=pl.ANY)] * count,
        out_specs=[pl.BlockSpec(memory_space=pltpu.VMEM)] * count,
        scratch_shapes=scratch,
        compiler_params=pltpu.CompilerParams(
            collective_id=1, has_side_effects=True, vmem_limit_bytes=60 * 2**20
        ),
    )(*parts)
    return [o.reshape(-1, o.shape[-1]) for o in outs]


def norm_rows(values, scales):
    return values * lax.rsqrt(jnp.mean(values * values, axis=-1, keepdims=True) + epsilon) * scales


def norm_back(inputs, scales, grad):
    return jax.vjp(lambda v: norm_rows(v, scales), inputs)[1](grad)[0]


def gated_units(united):
    halfway = united.shape[-1] // 2
    return jax.nn.gelu(united[:, :halfway], approximate=True) * united[:, halfway:]


def row_items(lengths, row_count):
    places = jnp.arange(row_count, dtype=jnp.int32)
    count = lengths.shape[0]
    item, boundary = jnp.zeros((row_count,), jnp.int32), jnp.int32(0)
    for k in range(count):
        boundary = boundary + lengths[k]
        item = item + (places >= boundary).astype(jnp.int32)
    return item


def head_split(matrix):
    return matrix.reshape(matrix.shape[0], HEADS, HEAD_DIM)


def outer_rows(left, right):
    return jnp.einsum("rd,re->de", left, right, preferred_element_type=jnp.float32).astype(jnp.bfloat16)


def back_rows(incoming, matrix):
    return jnp.einsum("re,de->rd", incoming, matrix, preferred_element_type=jnp.float32)


def score_rows(query_heads, key_heads, allowed):
    raw_scores = jnp.einsum(
        "qhd,khd->hqk", query_heads, key_heads, preferred_element_type=jnp.float32
    )
    return jnp.where(allowed[None], raw_scores * HEAD_DIM ** (-0.5), masked_value)


def attend_forward(queries, keys_in, values_in, allowed):
    scores = score_rows(head_split(queries), head_split(keys_in), allowed)
    largest = jnp.max(scores, axis=2, keepdims=True)
    expanded = jnp.exp(scores - largest)
    totals = jnp.sum(expanded, axis=2, keepdims=True)
    weights = (expanded / totals).astype(jnp.bfloat16)
    mixed = jnp.einsum(
        "hqk,khd->qhd", weights, head_split(values_in), preferred_element_type=jnp.float32
    )
    return (mixed.reshape(queries.shape[0], D), largest + jnp.log(totals))


def attend_backward(queries, keys_in, values_in, allowed, log_totals, grad_mixed):
    query_heads = head_split(queries)
    key_heads = head_split(keys_in)
    value_heads = head_split(values_in)
    probs = jnp.exp(score_rows(query_heads, key_heads, allowed) - log_totals)
    grad_heads = head_split(grad_mixed)
    grad_values = jnp.einsum(
        "hqk,qhd->khd", probs.astype(jnp.bfloat16), grad_heads, preferred_element_type=jnp.float32
    )
    grad_probs = jnp.einsum(
        "qhd,khd->hqk", grad_heads, value_heads, preferred_element_type=jnp.float32
    )
    centred = grad_probs - jnp.sum(probs * grad_probs, axis=2, keepdims=True)
    grad_scores = (probs * centred * HEAD_DIM ** (-0.5)).astype(jnp.bfloat16)
    grad_queries = jnp.einsum(
        "hqk,khd->qhd", grad_scores, key_heads, preferred_element_type=jnp.float32
    )
    grad_keys = jnp.einsum(
        "hqk,qhd->khd", grad_scores, query_heads, preferred_element_type=jnp.float32
    )
    return (
        grad_queries.reshape(queries.shape[0], D),
        grad_keys.reshape(keys_in.shape[0], D),
        grad_values.reshape(keys_in.shape[0], D),
    )


def self_forward(inputs, params, allowed, live_rows):
    scales, joined, outward = params
    normed = norm_rows(inputs, scales).astype(jnp.bfloat16)
    projected = jnp.dot(normed, joined, preferred_element_type=jnp.float32).astype(jnp.bfloat16)
    mixed, log_totals = attend_forward(
        projected[:, :D], projected[:, D : 2 * D], projected[:, 2 * D :], allowed
    )
    mixed_low = mixed.astype(jnp.bfloat16)
    branch = jnp.dot(mixed_low, outward, preferred_element_type=jnp.float32)
    return (inputs + live_rows[:, None] * branch, (normed, projected, mixed_low, log_totals))


def self_backward(inputs, params, allowed, live_rows, stored, incoming):
    scales, joined, outward = params
    normed, projected, mixed_low, log_totals = stored
    grad_branch = (live_rows[:, None] * incoming).astype(jnp.bfloat16)
    grad_outward = outer_rows(mixed_low, grad_branch)
    grad_mixed = back_rows(grad_branch, outward).astype(jnp.bfloat16)
    grad_parts = attend_backward(
        projected[:, :D],
        projected[:, D : 2 * D],
        projected[:, 2 * D :],
        allowed,
        log_totals,
        grad_mixed,
    )
    grad_projected = jnp.concatenate(grad_parts, axis=1).astype(jnp.bfloat16)
    grad_joined = outer_rows(normed, grad_projected)
    grad_inputs = norm_back(inputs, scales, back_rows(grad_projected, joined))
    return (incoming + grad_inputs, (grad_joined, grad_outward))


def cross_forward(inputs, memory, params, allowed, live_rows):
    scales, memory_scales, query_map, pair_map, outward = params
    normed = norm_rows(inputs, scales).astype(jnp.bfloat16)
    memory_normed = norm_rows(memory, memory_scales).astype(jnp.bfloat16)
    queries = jnp.dot(normed, query_map, preferred_element_type=jnp.float32).astype(jnp.bfloat16)
    pairs = jnp.dot(memory_normed, pair_map, preferred_element_type=jnp.float32).astype(
        jnp.bfloat16
    )
    mixed, log_totals = attend_forward(queries, pairs[:, :D], pairs[:, D:], allowed)
    mixed_low = mixed.astype(jnp.bfloat16)
    branch = jnp.dot(mixed_low, outward, preferred_element_type=jnp.float32)
    return (
        inputs + live_rows[:, None] * branch,
        (normed, memory_normed, queries, pairs, mixed_low, log_totals),
    )


def cross_backward(inputs, memory, params, allowed, live_rows, stored, incoming):
    scales, memory_scales, query_map, pair_map, outward = params
    normed, memory_normed, queries, pairs, mixed_low, log_totals = stored
    grad_branch = (live_rows[:, None] * incoming).astype(jnp.bfloat16)
    grad_outward = outer_rows(mixed_low, grad_branch)
    grad_mixed = back_rows(grad_branch, outward).astype(jnp.bfloat16)
    grad_queries, grad_keys, grad_values = attend_backward(
        queries, pairs[:, :D], pairs[:, D:], allowed, log_totals, grad_mixed
    )
    grad_queries_low = grad_queries.astype(jnp.bfloat16)
    grad_pairs = jnp.concatenate([grad_keys, grad_values], axis=1).astype(jnp.bfloat16)
    grad_query_map = outer_rows(normed, grad_queries_low)
    grad_pair_map = outer_rows(memory_normed, grad_pairs)
    grad_inputs = norm_back(inputs, scales, back_rows(grad_queries_low, query_map))
    grad_memory = norm_back(memory, memory_scales, back_rows(grad_pairs, pair_map))
    return (
        incoming + grad_inputs,
        grad_memory,
        (grad_query_map, grad_pair_map, grad_outward),
    )


def mlp_forward(inputs, params, live_rows):
    scales, inward, outward = params
    normed = norm_rows(inputs, scales).astype(jnp.bfloat16)
    united = jnp.dot(normed, inward, preferred_element_type=jnp.float32)
    activated = gated_units(united).astype(jnp.bfloat16)
    branch = jnp.dot(activated, outward, preferred_element_type=jnp.float32)
    return (inputs + live_rows[:, None] * branch, (normed, united, activated))


def mlp_backward(inputs, params, live_rows, stored, incoming):
    scales, inward, outward = params
    normed, united, activated = stored
    grad_branch = (live_rows[:, None] * incoming).astype(jnp.bfloat16)
    grad_outward = outer_rows(activated, grad_branch)
    grad_activated = back_rows(grad_branch, outward)
    _, pullback = jax.vjp(gated_units, united)
    grad_united = pullback(grad_activated)[0].astype(jnp.bfloat16)
    grad_inward = outer_rows(normed, grad_united)
    grad_inputs = norm_back(inputs, scales, back_rows(grad_united, inward))
    return (incoming + grad_inputs, (grad_inward, grad_outward))


def plain_gather(shards):
    return [lax.all_gather(s, AXES, axis=0, tiled=True) for s in shards]


def plain_scatter(sums):
    return [lax.psum_scatter(s.astype(jnp.float32), AXES, scatter_dimension=0, tiled=True) for s in sums]


SCALE_OF = (0, None, 1, None, 2, None, 3, 4, None, 5, None)


def per_device(
    linked,
    enc_input,
    dec_input,
    enc_lengths,
    dec_lengths,
    enc_attn_gain,
    enc_qkv,
    enc_attn_out,
    enc_mlp_gain,
    enc_mlp_in,
    enc_mlp_out,
    dec_self_gain,
    dec_qkv,
    dec_self_out,
    cross_gain,
    memory_gain,
    cross_query,
    cross_kv,
    cross_out,
    dec_mlp_gain,
    dec_mlp_in,
    dec_mlp_out,
    enc_cotangent,
    dec_cotangent,
):
    item_count = enc_lengths.shape[0]
    enc_items = row_items(enc_lengths, enc_input.shape[0])
    dec_items = row_items(dec_lengths, dec_input.shape[0])
    enc_live = (enc_items < item_count).astype(jnp.float32)
    dec_live = (dec_items < item_count).astype(jnp.float32)
    enc_padded = enc_items[:, None] == item_count
    dec_padded = dec_items[:, None] == item_count
    enc_allowed = (enc_items[:, None] == enc_items[None, :]) | enc_padded
    dec_places = jnp.arange(dec_input.shape[0], dtype=jnp.int32)
    self_allowed = (dec_items[:, None] == dec_items[None, :]) & (
        dec_places[None, :] <= dec_places[:, None]
    ) | dec_padded
    cross_allowed = (dec_items[:, None] == enc_items[None, :]) | dec_padded
    scales = [
        g.astype(jnp.float32)
        for g in (enc_attn_gain, enc_mlp_gain, dec_self_gain, cross_gain, memory_gain, dec_mlp_gain)
    ]
    shards = (
        enc_qkv, enc_attn_out, enc_mlp_in, enc_mlp_out, dec_qkv, dec_self_out,
        cross_query, cross_kv, cross_out, dec_mlp_in, dec_mlp_out,
    )
    if linked:
        mine = lax.axis_index("wide") * lax.axis_size("narrow") + lax.axis_index("narrow")
        columns = jnp.arange(D, dtype=jnp.int32) // scales[0].shape[0] == mine
        rows = [jnp.where(columns, jnp.tile(g, D // g.shape[0]), 0.0) for g in scales]
        rows += [jnp.zeros((D,), jnp.float32)] * (8 - len(rows))
        packed = jnp.stack(rows).astype(jnp.bfloat16)
        (*whole, _), kept, enc_out, dec_out, gains = forward_all(
            (*shards, packed), enc_input, dec_input, enc_lengths, dec_lengths
        )
        whole = [w.reshape(-1, w.shape[-1]) for w in whole]
    else:
        whole = plain_gather(shards)
        gains = plain_gather(scales)
    encoder_start = enc_input.astype(jnp.float32)
    decoder_start = dec_input.astype(jnp.float32)
    if linked:
        g = kept
        enc_middle, encoder_final, dec_middle, dec_crossed = g["e_x1"], g["e_x2"], g["d_x1"], g["d_x2"]

        def logs(q, k, allowed):
            scores = score_rows(head_split(q), head_split(k), allowed)
            return jax.nn.logsumexp(scores, axis=2, keepdims=True)

        enc_attn_store = (g["e_h1"], g["e_qkv"], g["e_o"], logs(g["e_qkv"][:, :D], g["e_qkv"][:, D:2*D], enc_allowed))
        enc_mlp_store = (g["e_h2"], g["e_u"].astype(jnp.float32), g["e_a"])
        dec_self_store = (g["d_h1"], g["d_qkv"], g["d_o"], logs(g["d_qkv"][:, :D], g["d_qkv"][:, D:2*D], self_allowed))
        cross_store = (g["hq"], g["hm"], g["q"], g["kv"], g["c_o"], logs(g["q"], g["kv"][:, :D], cross_allowed))
        dec_mlp_store = (g["d_h2"], g["d_u"].astype(jnp.float32), g["d_a"])
    else:
        encoder_start = enc_input.astype(jnp.float32)
        enc_middle, enc_attn_store = self_forward(encoder_start, (gains[0], *whole[0:2]), enc_allowed, enc_live)
        encoder_final, enc_mlp_store = mlp_forward(enc_middle, (gains[1], *whole[2:4]), enc_live)
        decoder_start = dec_input.astype(jnp.float32)
        dec_middle, dec_self_store = self_forward(decoder_start, (gains[2], *whole[4:6]), self_allowed, dec_live)
        dec_crossed, cross_store = cross_forward(
            dec_middle, encoder_final, (gains[3], gains[4], *whole[6:9]), cross_allowed, dec_live
        )
        decoder_final, dec_mlp_store = mlp_forward(dec_crossed, (gains[5], *whole[9:11]), dec_live)
        enc_out, dec_out = encoder_final.astype(jnp.bfloat16), decoder_final.astype(jnp.bfloat16)
    grad_crossed, dec_mlp_grads = mlp_backward(
        dec_crossed, (gains[5], *whole[9:11]), dec_live, dec_mlp_store, dec_cotangent.astype(jnp.float32)
    )
    grad_middle, grad_memory, cross_grads = cross_backward(
        dec_middle,
        encoder_final,
        (gains[3], gains[4], *whole[6:9]),
        cross_allowed,
        dec_live,
        cross_store,
        grad_crossed,
    )
    grad_decoder_start, dec_self_grads = self_backward(
        decoder_start, (gains[2], *whole[4:6]), self_allowed, dec_live, dec_self_store, grad_middle
    )
    grad_enc_middle, enc_mlp_grads = mlp_backward(
        enc_middle,
        (gains[1], *whole[2:4]),
        enc_live,
        enc_mlp_store,
        enc_cotangent.astype(jnp.float32) + grad_memory,
    )
    grad_encoder_start, enc_attn_grads = self_backward(
        encoder_start, (gains[0], *whole[0:2]), enc_allowed, enc_live, enc_attn_store, grad_enc_middle
    )
    sums = enc_attn_grads + enc_mlp_grads + dec_self_grads + cross_grads + dec_mlp_grads
    summed = (scatter_all if linked else plain_scatter)(sums)
    grads, scale_grads = [], {}
    for total, shard, k in zip(summed, shards, SCALE_OF):
        if k is not None:
            scale_grads[k] = jnp.sum(total * shard.astype(jnp.float32), axis=1) / scales[k]
        grads.append(total)
    return (
        enc_out,
        dec_out,
        grad_encoder_start,
        grad_decoder_start,
        scale_grads[0], grads[0], grads[1],
        scale_grads[1], grads[2], grads[3],
        scale_grads[2], grads[4], grads[5],
        scale_grads[3], scale_grads[4], grads[6], grads[7], grads[8],
        scale_grads[5], grads[9], grads[10],
    )


def solution(mesh):
    rows, line = P(AXES, None), P(AXES)
    linked = mesh.shape["wide"] == 2 * Z and mesh.shape["narrow"] == 4
    weights = (
        line, rows, rows, line, rows, rows, line, rows, rows,
        line, line, rows, rows, rows, line, rows, rows,
    )
    return jax.shard_map(
        functools.partial(per_device, linked),
        mesh=mesh,
        in_specs=(rows, rows, line, line, *weights, rows, rows),
        out_specs=(rows, rows, rows, rows, *weights),
        check_vma=False,
    )
```

```python
import functools

import jax
import jax.numpy as jnp
from jax import lax
from jax.experimental import pallas as pl
from jax.experimental.pallas import tpu as pltpu
from jax.sharding import PartitionSpec as P

D = 768
HEADS = 12
HEAD_DIM = 64
FF = 2048
AXES = ("wide", "narrow")
MESH = pl.DeviceIdType.MESH

Z = 4
PIECES = (
    (11, 0, 768, False),
    (0, 0, 1152, False), (0, 1152, 1152, True), (1, 0, 768, False),
    (2, 0, 1024, False), (2, 1024, 1024, True), (2, 2048, 1024, False), (2, 3072, 1024, False),
    (3, 0, 384, True), (3, 384, 384, False),
    (4, 0, 1152, False), (4, 1152, 1152, True), (5, 0, 768, False), (6, 0, 768, False),
    (7, 0, 768, True), (7, 768, 768, False), (8, 0, 768, False),
    (9, 0, 1024, True), (9, 1024, 1024, False), (9, 2048, 1024, False), (9, 3072, 1024, True),
    (10, 0, 384, False), (10, 384, 384, False),
)
STRIDE = 2


class Place:
    def __init__(self):
        self.w, self.n = lax.axis_index("wide"), lax.axis_index("narrow")
        self.z, self.y = self.w // 2, self.w % 2
        self.x, self.c = self.n // 2, self.n % 2
        w, n, y, x, c = self.w, self.n, self.y, self.x, self.c
        self.sibling = (w, n + 1 - 2 * c)
        self.first = (w + (1 - c) * (1 - 2 * y), n + c * (2 - 4 * x))
        self.last = (w + c * (1 - 2 * y), n + (1 - c) * (2 - 4 * x))
        self.above = (w + 2, n)
        self.below = (w - 2, n)

    def barrier(self):
        sem = pltpu.get_barrier_semaphore()
        for device in (self.sibling, self.first, self.last):
            pl.semaphore_signal(sem, inc=1, device_id=device, device_id_type=MESH)

        @pl.when(self.z < Z - 1)
        def _():
            pl.semaphore_signal(sem, inc=1, device_id=self.above, device_id_type=MESH)

        @pl.when(self.z > 0)
        def _():
            pl.semaphore_signal(sem, inc=1, device_id=self.below, device_id_type=MESH)

        inner = jnp.where(self.z * (Z - 1 - self.z) > 0, 1, 0)
        pl.semaphore_wait(sem, 4 + inner)

    def by_core(self, do):
        @pl.when(self.c == 0)
        def _():
            do(0)

        @pl.when(self.c == 1)
        def _():
            do(1)


def remote(src, dst, sems, index, device):
    send, recv = sems
    return pltpu.make_async_remote_copy(
        src_ref=src, dst_ref=dst, send_sem=send.at[index], recv_sem=recv.at[index],
        device_id=device, device_id_type=MESH,
    )


class Gather:
    PHASES = 7
    SEMS = 10

    def __init__(self, place, part, whole, columns, z_first, sems, base, local_sem):
        self.p, self.z_first, self.sems, self.base = place, z_first, sems, base
        self.part = part.at[:, :, columns]
        self.whole = whole.at[:, :, :, :, :, :, columns]
        self.local = pltpu.make_async_copy(self.part, self.own(), local_sem)

    def own(self):
        p = self.p
        return self.whole.at[p.z, p.y, p.x, p.c]

    def copy(self, src, dst, slot, device):
        return remote(src, dst, self.sems, self.base + slot, device)

    def layer(self, zz, core):
        p = self.p
        if self.z_first:
            return self.whole.at[zz, p.y, p.x, core]
        return self.whole.at[zz, :, p.x, 0] if core == 0 else self.whole.at[zz, p.y, :, 1]

    def half(self, core, mine):
        p = self.p
        if core == 0:
            return self.whole.at[:, :, p.x if mine else 1 - p.x, 0]
        return self.whole.at[:, p.y if mine else 1 - p.y, :, 1]

    def along_z(self, step, sending):
        p = self.p

        def go(core):
            for up in (True, False):
                if sending:
                    zz = p.z - step if up else p.z + step
                    there = (p.z < Z - 1) & (zz >= 0) if up else (p.z > 0) & (zz < Z)
                else:
                    zz = p.z - 1 - step if up else p.z + 1 + step
                    there = zz >= 0 if up else zz < Z

                target = (p.above if up else p.below) if sending else p.last

                @pl.when(there)
                def _():
                    block = self.layer(zz, core)
                    copy = self.copy(block, block, 1 + step * 2 + up, target)
                    copy.start() if sending else copy.wait_recv()

        p.by_core(go)

    def along_z_sent(self):
        p = self.p

        def go(core):
            for step in range(3):
                for up in (True, False):
                    zz = p.z - step if up else p.z + step
                    there = (p.z < Z - 1) & (zz >= 0) if up else (p.z > 0) & (zz < Z)

                    @pl.when(there)
                    def _():
                        block = self.layer(zz, core)
                        self.copy(block, block, 1 + step * 2 + up, p.last).wait_send()

        p.by_core(go)

    def first(self, core):
        p = self.p
        if not self.z_first:
            return self.copy(self.part, self.own(), 0, p.first)
        block = self.whole.at[:, p.y, p.x, core]
        return self.copy(block, block, 0, p.first)

    def last(self, core):
        block = self.half(core, True)
        return self.copy(block, block, 7, self.p.last)

    def across(self, core, mine):
        block = self.half(core, mine)
        return self.copy(block, block, 8 if mine else 9, self.p.sibling)

    def each(self, make, *verbs):
        def go(core):
            copy = make(core)
            for verb in verbs:
                getattr(copy, verb)()

        self.p.by_core(go)

    def phase(self, number):
        early = not self.z_first
        if number == 0:
            self.local.start()
            if early:
                self.each(self.first, "start")
            self.local.wait()
            if not early:
                self.along_z(0, True)
        elif number == 1:
            if early:
                self.each(self.first, "wait_recv")
                self.along_z(0, True)
            else:
                self.along_z(0, False)
                self.along_z(1, True)
        elif number == 2:
            self.along_z(0 if early else 1, False)
            self.along_z(1 if early else 2, True)
        elif number == 3:
            self.along_z(1 if early else 2, False)
            if early:
                self.along_z(2, True)
            else:
                self.each(self.first, "start")
        elif number == 4:
            if early:
                self.along_z(2, False)
            else:
                self.each(self.first, "wait_recv")
            self.each(self.last, "start")
            self.each(lambda core: self.across(core, True), "start")
        elif number == 5:
            self.each(self.last, "wait_recv")
            self.each(lambda core: self.across(core, False), "start")
        else:
            for core in (0, 1):
                @pl.when(self.p.c == core)
                def _():
                    for mine in (True, False):
                        self.across(1 - core, mine).wait_recv()
                        self.across(core, mine).wait_send()
                    self.first(core).wait_send()
                    self.last(core).wait_send()
            self.along_z_sent()


class Scatter:
    PHASES = 8
    SEMS = 9

    def __init__(self, place, parts, z_first, out, total, lasts, zs, firsts, sems, base):
        self.p, self.z_first, self.sems, self.base = place, z_first, sems, base
        self.parts, self.out = parts, out
        self.total, self.lasts, self.zs, self.firsts = total, lasts, zs, firsts

    def copy(self, src, dst, slot, device):
        return remote(src, dst, self.sems, self.base + slot, device)

    def spot(self, core, last, first=None):
        every = slice(None)
        if first is None:
            return (every, last) if core else (every, every, last)
        return (last, first) if core else (first, last)

    def place_of(self, core):
        p = self.p
        return (p.y, p.x) if core else (p.x, p.y)

    def across(self, core):
        return self.copy(self.parts.at[:, :, :, 1 - core], self.total, 0, self.p.sibling)

    def last(self, core):
        last, _ = self.place_of(core)
        return self.copy(self.total.at[self.spot(core, 1 - last)], self.lasts, 1, self.p.last)

    def first(self, core):
        p = self.p
        last, first = self.place_of(core)
        if self.z_first:
            src = self.total.at[(slice(None), *self.spot(core, last, 1 - first))]
        else:
            src = self.total.at[(p.z, *self.spot(core, last, 1 - first))]
        return self.copy(src, self.firsts, 2, p.first)

    def layer(self, zz, core):
        last, first = self.place_of(core)
        if self.z_first:
            return self.total.at[(zz, *self.spot(core, last, first))]
        return self.total.at[(zz, *self.spot(core, last)[1:])]

    def way(self, step, up, sending):
        z, far = self.p.z, 2 - step
        if sending:
            zz = z + 1 + far if up else z - 1 - far
            return zz, zz < Z if up else zz >= 0
        zz = z + far if up else z - far
        return zz, (z > 0) & (zz < Z) if up else (z < Z - 1) & (zz >= 0)

    def landing(self, step, up):
        return 0 if step == 0 else 2 * step - 1 + up

    def along_z(self, step, verb):
        p = self.p

        def go(core):
            for up in (True, False):
                zz, there = self.way(step, up, verb != "wait_recv")
                target = (p.above if up else p.below) if verb == "start" else p.last

                @pl.when(there)
                def _():
                    copy = self.copy(self.layer(zz, core), self.zs.at[self.landing(step, up)], 3 + step * 2 + up, target)
                    getattr(copy, verb)()

        p.by_core(go)

    def add_z(self, step):
        p = self.p
        for up in (True, False):
            zz, there = self.way(step, up, False)

            @pl.when(there)
            def _():
                arrived = self.zs.at[self.landing(step, up)]
                if self.z_first:
                    self.total[zz, p.y, p.x] += arrived[...]
                else:
                    for k in range(2):
                        self.total[(zz, *self.pair(k))] += arrived[k]

    def pair(self, k):
        p = self.p
        return k * (1 - p.c) + p.y * p.c, p.x * (1 - p.c) + k * p.c

    def each(self, make, *verbs):
        def go(core):
            copy = make(core)
            for verb in verbs:
                getattr(copy, verb)()

        self.p.by_core(go)

    def phase(self, number):
        p, early = self.p, self.z_first
        if number == 0:
            self.each(self.across, "start")
        elif number == 1:
            self.each(self.across, "wait_recv")

            @pl.loop(0, 16)
            def _(i):
                self.total[i // 4, i // 2 % 2, i % 2] += self.parts[i // 4, i // 2 % 2, i % 2, p.c]

            self.each(self.last, "start")
            self.each(self.across, "wait_send")
        elif number == 2:
            self.each(self.last, "wait_recv")

            @pl.loop(0, 8)
            def _(i):
                self.total[(i // 2, *self.pair(i % 2))] += self.lasts[i // 2, i % 2]

            if early:
                self.each(self.first, "start")
            else:
                self.along_z(0, "start")
        elif number == 3:
            if early:
                self.each(self.first, "wait_recv")

                @pl.loop(0, Z)
                def _(i):
                    self.total[i, p.y, p.x] += self.firsts[i]

                self.along_z(0, "start")
            else:
                self.along_z(0, "wait_recv")
                self.add_z(0)
                self.along_z(1, "start")
        elif number == 4:
            step = 0 if early else 1
            self.along_z(step, "wait_recv")
            self.add_z(step)
            self.along_z(step + 1, "start")
        elif number == 5:
            step = 1 if early else 2
            self.along_z(step, "wait_recv")
            self.add_z(step)
            if early:
                self.along_z(2, "start")
            else:
                self.each(self.first, "start")
        elif number == 6:
            if early:
                self.along_z(2, "wait_recv")
                self.add_z(2)
                self.out[...] = self.total[p.z, p.y, p.x].astype(jnp.float32)
            else:
                self.each(self.first, "wait_recv")
                self.out[...] = self.total[p.z, p.y, p.x].astype(jnp.float32) + self.firsts[...].astype(jnp.float32)
        else:
            for make in (self.last, self.first):
                self.each(make, "wait_send")
            for step in range(3):
                self.along_z(step, "wait_send")


epsilon = 1e-06
masked_value = -1000000000.0
SHRINK = HEAD_DIM**-0.5
NT = (((1,), (1,)), ((), ()))
TN = (((0,), (0,)), ((), ()))
f32, bf16 = jnp.float32, jnp.bfloat16


def dot(a, b, dims=(((1,), (0,)), ((), ()))):
    return lax.dot_general(a, b, dims, preferred_element_type=f32)


def shrunk(values):
    return lax.rsqrt(jnp.mean(values * values, axis=-1, keepdims=True) + epsilon)


def norm(values, scales):
    return values * shrunk(values) * scales


def items_of(lengths_ref, places):
    item, boundary = jnp.zeros_like(places), 0
    for k in range(lengths_ref.shape[0]):
        boundary = boundary + lengths_ref[k]
        item = item + jnp.where(places >= boundary, 1, 0)
    return item


def fill_masks(enc_lengths, dec_lengths, enc_mask, self_mask, cross_mask):
    count = enc_lengths.shape[0]

    def grid(ref, axis):
        return lax.broadcasted_iota(jnp.int32, ref.shape, axis)

    def put(ref, rows, columns, both):
        kept = rows == columns
        if both is not None:
            kept = kept & both
        ref[...] = jnp.where(kept | (rows == count), 1.0, 0.0)

    put(enc_mask, items_of(enc_lengths, grid(enc_mask, 0)), items_of(enc_lengths, grid(enc_mask, 1)), None)
    put(
        self_mask, items_of(dec_lengths, grid(self_mask, 0)), items_of(dec_lengths, grid(self_mask, 1)),
        grid(self_mask, 1) <= grid(self_mask, 0),
    )
    put(cross_mask, items_of(dec_lengths, grid(cross_mask, 0)), items_of(enc_lengths, grid(cross_mask, 1)), None)


def live_rows(lengths_ref, rows):
    item = items_of(lengths_ref, lax.broadcasted_iota(jnp.int32, (rows, 1), 0))
    return jnp.where(item < lengths_ref.shape[0], 1.0, 0.0)


def head_lanes(which):
    lanes = lax.broadcasted_iota(jnp.int32, (1, 2 * HEAD_DIM), 1)
    return jnp.where(lanes // HEAD_DIM == which, 1.0, 0.0).astype(bf16)


def head_probs(q, k, kept):
    scores = jnp.where(kept[...] > 0.0, dot(q, k, NT) * SHRINK, masked_value)
    raised = jnp.exp(scores - jnp.max(scores, axis=1, keepdims=True))
    return raised * (1.0 / jnp.sum(raised, axis=1, keepdims=True))


def pair_columns(pair, offset):
    return pl.ds(pl.multiple_of(pair * (2 * HEAD_DIM) + offset, 2 * HEAD_DIM), 2 * HEAD_DIM)


def attend(q_ref, q_at, k_ref, k_at, v_ref, v_at, kept, out_ref):
    @pl.loop(0, HEADS // 2)
    def _(pair):
        q = q_ref[:, pair_columns(pair, q_at)]
        k = k_ref[:, pair_columns(pair, k_at)]
        v = v_ref[:, pair_columns(pair, v_at)]
        mixed = None
        for which in range(2):
            lanes = head_lanes(which)
            part = dot(head_probs(q * lanes, k, kept).astype(bf16), v * lanes)
            mixed = part if mixed is None else mixed + part
        out_ref[:, pair_columns(pair, 0)] = mixed.astype(bf16)


def gelu_tanh(t):
    return jnp.tanh(0.7978845608028654 * (t + 0.044715 * (t * t * t)))


STORED = (
    ("e_h1", "enc", D, bf16), ("e_qkv", "enc", 3 * D, bf16), ("e_o", "enc", D, bf16), ("e_x1", "enc", D, f32),
    ("e_h2", "enc", D, bf16), ("e_u", "enc", 2 * FF, bf16), ("e_a", "enc", FF, bf16), ("e_x2", "enc", D, f32),
    ("hm", "enc", D, bf16), ("kv", "enc", 2 * D, bf16),
    ("d_h1", "dec", D, bf16), ("d_qkv", "dec", 3 * D, bf16), ("d_o", "dec", D, bf16), ("d_x1", "dec", D, f32),
    ("hq", "dec", D, bf16), ("q", "dec", D, bf16), ("c_o", "dec", D, bf16), ("d_x2", "dec", D, f32),
    ("d_h2", "dec", D, bf16), ("d_u", "dec", 2 * FF, bf16), ("d_a", "dec", FF, bf16),
)


class Forward:
    def __init__(self, refs, lengths):
        self.__dict__.update(refs)
        self.lengths = lengths

    def gain(self, k):
        return self.gains[k : k + 1]

    def set_norm(self, values, k, out):
        out[...] = norm(values, self.gain(k)).astype(bf16)

    def step(self, m, start, size, weight):
        columns = pl.ds(start, size)
        if m == 0 or m == 4:
            side = "e" if m == 0 else "d"
            if start == 0:
                self.set_norm(getattr(self, side + "_x0")[...].astype(f32), 0 if m == 0 else 2, getattr(self, side + "_h1"))
            qkv = getattr(self, side + "_qkv")
            qkv[:, columns] = dot(getattr(self, side + "_h1")[...], weight).astype(bf16)
            if start + size == qkv.shape[1]:
                kept = self.enc_mask if m == 0 else self.self_mask
                attend(qkv, 0, qkv, D, qkv, 2 * D, kept, getattr(self, side + "_o"))
        elif m == 1:
            self.e_x1[...] = self.e_x0[...].astype(f32) + self.live("enc") * dot(self.e_o[...], weight)
            self.set_norm(self.e_x1[...], 1, self.e_h2)
        elif m == 5:
            self.d_x1[...] = self.d_x0[...].astype(f32) + self.live("dec") * dot(self.d_o[...], weight)
            self.set_norm(self.d_x1[...], 3, self.hq)
        elif m == 6:
            self.q[...] = dot(self.hq[...], weight).astype(bf16)
        elif m == 7:
            self.kv[:, columns] = dot(self.hm[...], weight).astype(bf16)
            if start + size == self.kv.shape[1]:
                attend(self.q, 0, self.kv, 0, self.kv, D, self.cross_mask, self.c_o)
        elif m == 8:
            self.d_x2[...] = self.d_x1[...] + self.live("dec") * dot(self.c_o[...], weight)
            self.set_norm(self.d_x2[...], 5, self.d_h2)
        elif m == 2 or m == 9:
            side = "e" if m == 2 else "d"
            rows = getattr(self, side + "_h2").shape[0]
            united = dot(getattr(self, side + "_h2")[...], weight)
            getattr(self, side + "_u")[:, columns] = united.astype(bf16)
            half = FF
            if start < half:
                self.gates[pl.ds(0, rows), columns] = united
            else:
                back = pl.ds(start - half, size)
                gate = self.gates[pl.ds(0, rows), back]
                getattr(self, side + "_a")[:, back] = (0.5 * gate * (1.0 + gelu_tanh(gate)) * united).astype(bf16)
        else:
            side, other = ("e", "enc") if m == 3 else ("d", "dec")
            before = self.e_x1 if m == 3 else self.d_x2
            after = before[:, columns] + self.live(other) * dot(getattr(self, side + "_a")[...], weight)
            out = self.enc_out if m == 3 else self.dec_out
            out[:, columns] = after.astype(bf16)
            if m == 3:
                self.e_x2[:, columns] = after
                if start + size == D:
                    self.set_norm(self.e_x2[...], 4, self.hm)

    def live(self, side):
        ref = self.e_x0 if side == "enc" else self.d_x0
        return live_rows(self.lengths[side], ref.shape[0])


def forward_body(pieces, count, *refs):
    refs = list(refs)

    def take(n):
        got = refs[:n]
        del refs[:n]
        return got

    parts = take(count - 1)
    scales, e_x0, d_x0, enc_lengths, dec_lengths = take(5)
    wholes = take(count)
    stored = dict(zip([name for name, *_ in STORED], take(len(STORED))))
    enc_out, dec_out, gains = take(3)
    send, recv, local, stage_sem, own_scales, spread, gates, enc_mask, self_mask, cross_mask, wide_stage, deep_stage = refs
    place = Place()
    place.barrier()
    each = scales.shape[1]
    shape = (each, D)
    spots = lax.broadcasted_iota(jnp.int32, shape, 1) - lax.broadcasted_iota(jnp.int32, shape, 0)
    spots = jnp.where(spots == (place.w * 4 + place.n) * each, 1.0, 0.0).astype(bf16)
    own_scales[0] = dot(scales[...], spots).astype(bf16)
    parts.append(own_scales)
    work = [
        Gather(place, parts[m], wholes[m], pl.ds(start, size), z_first, (send, recv), k * Gather.SEMS, local.at[k])
        for k, (m, start, size, z_first) in enumerate(pieces)
    ]
    forward = Forward(
        dict(
            stored, e_x0=e_x0, d_x0=d_x0, enc_out=enc_out, dec_out=dec_out, gains=gains, gates=gates,
            enc_mask=enc_mask, self_mask=self_mask, cross_mask=cross_mask,
        ),
        {"enc": enc_lengths, "dec": dec_lengths},
    )

    def staged(k):
        m, start, size, _ = pieces[k]
        if m == len(parts) - 1:
            into = spread
        elif parts[m].shape[0] > 3:
            into = deep_stage.at[k % STAGES, ..., pl.ds(0, size)]
        else:
            into = wide_stage.at[k % STAGES, ..., pl.ds(0, size)]
        return pltpu.make_async_copy(wholes[m].at[..., pl.ds(start, size)], into, stage_sem.at[k % STAGES])

    last = STRIDE * (Gather.PHASES - 1)
    for slot in range(len(work) + last + 1):
        for k in range(len(work)):
            if (slot - k) % STRIDE == 0 and 0 <= slot - k <= last:
                work[k].phase((slot - k) // STRIDE)
        if slot == 0:
            fill_masks(enc_lengths, dec_lengths, enc_mask, self_mask, cross_mask)
        if 0 <= slot - last < len(work):
            staged(slot - last).start()
        k = slot - last - 1
        if k >= 0:
            staged(k).wait()
            m, start, size, _ = pieces[k]
            if m == len(parts) - 1:
                gains[...] = jnp.sum(spread[...].reshape(-1, 8, D).astype(f32), axis=0)
            else:
                stage = deep_stage if parts[m].shape[0] > 3 else wide_stage
                weight = stage[k % STAGES, ..., pl.ds(0, size)]
                forward.step(m, start, size, weight.reshape(-1, size))


STAGES = 2


def forward_all(shards, scales, enc_input, dec_input, enc_lengths, dec_lengths):
    count = len(shards) + 1
    parts = [s.reshape(s.shape[0] // 8, 8, s.shape[1]) for s in shards]
    shapes = [p.shape for p in parts] + [(1, 8, D)]
    sems = len(PIECES) * Gather.SEMS
    rows = {"enc": enc_input.shape[0], "dec": dec_input.shape[0]}
    hbm, vmem = pl.BlockSpec(memory_space=pl.ANY), pl.BlockSpec(memory_space=pltpu.VMEM)
    smem = pl.BlockSpec(memory_space=pltpu.SMEM)
    widest = max(size for m, _, size, _ in PIECES if shapes[m][0] == 3)
    deep = max((shapes[m][0], size) for m, _, size, _ in PIECES)
    outs = pl.pallas_call(
        functools.partial(forward_body, PIECES, count),
        out_shape=[jax.ShapeDtypeStruct((Z, 2, 2, 2, *shape), bf16) for shape in shapes]
        + [jax.ShapeDtypeStruct((rows[side], columns), dtype) for _, side, columns, dtype in STORED]
        + [
            jax.ShapeDtypeStruct(enc_input.shape, bf16),
            jax.ShapeDtypeStruct(dec_input.shape, bf16),
            jax.ShapeDtypeStruct((8, D), f32),
        ],
        in_specs=[hbm] * (count - 1) + [vmem, vmem, vmem, smem, smem],
        out_specs=[hbm] * count + [vmem] * (len(STORED) + 3),
        scratch_shapes=[
            pltpu.SemaphoreType.DMA((sems,)),
            pltpu.SemaphoreType.DMA((sems,)),
            pltpu.SemaphoreType.DMA((len(PIECES),)),
            pltpu.SemaphoreType.DMA((STAGES,)),
            pltpu.VMEM((1, 8, D), bf16),
            pltpu.VMEM((Z, 2, 2, 2, 1, 8, D), bf16),
            pltpu.VMEM((rows["enc"], FF), f32),
            pltpu.VMEM((rows["enc"], rows["enc"]), f32),
            pltpu.VMEM((rows["dec"], rows["dec"]), f32),
            pltpu.VMEM((rows["dec"], rows["enc"]), f32),
            pltpu.VMEM((STAGES, Z, 2, 2, 2, 3, 8, widest), bf16),
            pltpu.VMEM((STAGES, Z, 2, 2, 2, deep[0], 8, deep[1]), bf16),
        ],
        compiler_params=pltpu.CompilerParams(
            collective_id=0, has_side_effects=True, vmem_limit_bytes=60 * 2**20
        ),
    )(*parts, scales, enc_input, dec_input, enc_lengths, dec_lengths)
    wholes, stored, (enc_out, dec_out, gains) = outs[:count], outs[count:-3], outs[-3:]
    stored = dict(zip([name for name, *_ in STORED], stored))
    return wholes, stored, enc_out, dec_out, gains


class Backward:
    def __init__(self, refs, lengths, load, free):
        self.__dict__.update(refs)
        self.lengths, self.load, self.free = lengths, load, free

    def rows(self, side):
        return self.e_x0.shape[0] if side == "enc" else self.d_x0.shape[0]

    def live(self, side):
        return live_rows(self.lengths[side], self.rows(side))

    def gain(self, k):
        return self.gains[k : k + 1]

    def top(self, ref, side):
        return ref.at[pl.ds(0, self.rows(side))]

    def side(self, m):
        return "enc" if m < 4 else "dec"

    def through_norm(self, values, k, grad, into):
        small = shrunk(values)
        unit = values * small
        grad = grad * self.gain(k)
        into[...] += small * (grad - unit * jnp.mean(grad * unit, axis=-1, keepdims=True))

    def set_branch(self, side):
        grad = self.e_grad if side == "enc" else self.d_grad
        self.top(self.dz, side)[...] = (self.live(side) * grad[...]).astype(bf16)

    def before(self, m):
        side = self.side(m)
        if m == 10 or m == 3:
            if m == 10:
                self.d_grad[...] = self.d_cot[...].astype(f32)
            self.set_branch(side)
            self.load("d_a" if m == 10 else "e_a")
        elif m == 9 or m == 2:
            self.load("d_u" if m == 9 else "e_u")
            self.load("d_h2" if m == 9 else "e_h2")
            u, da = self.top(self.u, side), self.top(self.da, side)

            @pl.loop(0, FF // 256)
            def _(j):
                at = pl.multiple_of(j * 256, 256)
                gate_at, up_at = pl.ds(at, 256), pl.ds(pl.multiple_of(at + FF, 256), 256)
                t, up, grad = u[:, gate_at].astype(f32), u[:, up_at].astype(f32), da[:, gate_at]
                th = gelu_tanh(t)
                slope = 0.5 * (1.0 + th) + 0.5 * t * (1.0 - th * th) * (
                    0.7978845608028654 * (1.0 + 0.134145 * (t * t))
                )
                u[:, gate_at] = (slope * up * grad).astype(bf16)
                u[:, up_at] = (0.5 * t * (1.0 + th) * grad).astype(bf16)
        elif m == 8:
            self.set_branch("dec")
            self.load("c_o")
        elif m == 7:
            for name in ("q", "kv", "hm"):
                self.load(name)
            self.attend_back(self.q, 0, self.kv, 0, self.kv, D, self.cross_mask, "dec")
        elif m == 6:
            self.load("hq")
        elif m == 5 or m == 1:
            self.set_branch(side)
            self.load("d_o" if m == 5 else "e_o")
        else:
            self.load("d_h1" if m == 4 else "e_h1")
            self.load("d_qkv" if m == 4 else "e_qkv")
            qkv = self.top(self.qkv, side)
            self.attend_back(qkv, 0, qkv, D, qkv, 2 * D, self.self_mask if m == 4 else self.enc_mask, side)

    def attend_back(self, q_ref, q_at, k_ref, k_at, v_ref, v_at, kept, side):
        grad_ref = self.top(self.do, side)

        @pl.loop(0, HEADS // 2)
        def _(pair):
            q = q_ref[:, pair_columns(pair, q_at)]
            k = k_ref[:, pair_columns(pair, k_at)]
            v = v_ref[:, pair_columns(pair, v_at)]
            grad = grad_ref[:, pair_columns(pair, 0)]
            dq = dk = dv = 0.0
            for which in range(2):
                lanes = head_lanes(which)
                q_half, grad_half = q * lanes, grad * lanes
                probs = head_probs(q_half, k, kept)
                dv = dv + dot(probs.astype(bf16), grad_half, TN)
                dp = dot(grad_half, v, NT)
                centred = dp - jnp.sum(probs * dp, axis=1, keepdims=True)
                ds = (probs * centred * SHRINK).astype(bf16)
                dq = dq + dot(ds, k * lanes)
                dk = dk + dot(ds, q_half, TN)
            q_ref[:, pair_columns(pair, q_at)] = dq.astype(bf16)
            k_ref[:, pair_columns(pair, k_at)] = dk.astype(bf16)
            v_ref[:, pair_columns(pair, v_at)] = dv.astype(bf16)

    def factors(self, m):
        side = self.side(m)
        left = {
            10: self.a, 3: self.a, 9: self.h2, 2: self.h2, 8: self.o, 7: self.h2, 6: self.h1,
            5: self.o, 1: self.o, 4: self.h1, 0: self.h1,
        }[m]
        right = {
            10: self.dz, 3: self.dz, 9: self.u, 2: self.u, 8: self.dz, 7: self.kv, 6: self.q,
            5: self.dz, 1: self.dz, 4: self.qkv, 0: self.qkv,
        }[m]
        if m != 7:
            left, right = self.top(left, side), self.top(right, side)
        return left, right

    def back(self, m, columns, weight, first):
        side = self.side(m)
        right = self.factors(m)[1][:, columns]
        if m in (10, 3):
            into = self.top(self.da, side)
            tall = FF // Z
            for j in range(Z):
                share = dot(right, weight[j].reshape(tall, -1), NT)
                if first:
                    into[:, j * tall : (j + 1) * tall] = share
                else:
                    into[:, j * tall : (j + 1) * tall] += share
            return
        share = dot(right, weight[...].reshape(D, -1), NT)
        into = self.dh if m == 7 else self.top(self.dh, side)
        if m in (8, 5, 1):
            self.top(self.do, side)[...] = share.astype(bf16)
        elif first:
            into[...] = share
        else:
            into[...] += share
    def after(self, m):
        side = self.side(m)
        into = self.dh if m == 7 else self.top(self.dh, side)
        if m == 10:
            self.free("e_a")
        elif m == 9:
            self.load("d_x2")
            self.through_norm(self.top(self.x, "dec")[...], 5, into[...], self.d_grad)
            for name in ("e_x2", "e_u", "hm"):
                self.free(name)
        elif m == 8:
            self.free("d_o")
        elif m == 7:
            self.load("e_x2")
            self.e_grad[...] = self.e_cot[...].astype(f32)
            self.through_norm(self.x[...], 4, into[...], self.e_grad)
            self.free("d_x1")
            self.free("e_h2")
        elif m == 6:
            self.load("d_x1")
            self.through_norm(self.top(self.x, "dec")[...], 3, into[...], self.d_grad)
            self.free("e_x1")
            self.free("d_h1")
        elif m == 5:
            self.free("e_o")
        elif m == 4:
            self.through_norm(self.d_x0[...].astype(f32), 2, into[...], self.d_grad)
            self.free("e_h1")
            self.free("e_qkv")
        elif m == 2:
            self.load("e_x1")
            self.through_norm(self.x[...], 1, into[...], self.e_grad)
        elif m == 0:
            self.through_norm(self.e_x0[...].astype(f32), 0, into[...], self.e_grad)


HELD = dict(
    e_a="a", d_a="a", e_u="u", d_u="u", e_h2="h2", d_h2="h2", d_x2="x", e_x2="x", c_o="o", q="q", kv="kv",
    hm="h2", hq="h1", d_x1="x", e_x1="x", d_o="o", e_o="o", d_qkv="qkv", e_qkv="qkv", d_h1="h1", e_h1="h1",
)
RING = 3


def backward_body(pieces, count, *refs):
    refs = list(refs)

    def take(n):
        got = refs[:n]
        del refs[:n]
        return got

    wholes = take(count)
    stored = dict(zip(HELD, take(len(HELD))))
    e_x0, d_x0, e_cot, d_cot, gains, enc_lengths, dec_lengths = take(7)
    outs = take(count)
    e_grad, d_grad = take(2)
    send, recv, held_sem, ring_sem = take(4)
    names = ["a", "u", "h2", "x", "q", "kv", "o", "qkv", "h1"]
    held = dict(zip(names, take(len(names))))
    dz, do, da, dh, enc_mask, self_mask, cross_mask, wide_ring, deep_ring = take(9)
    place = Place()
    place.barrier()

    def loaded(name):
        src, into = stored[name], held[HELD[name]]
        return pltpu.make_async_copy(src, into.at[pl.ds(0, src.shape[0])], held_sem.at[list(HELD).index(name)])

    backward = Backward(
        dict(
            held, e_x0=e_x0, d_x0=d_x0, e_cot=e_cot, d_cot=d_cot, gains=gains, e_grad=e_grad, d_grad=d_grad,
            dz=dz, do=do, da=da, dh=dh, enc_mask=enc_mask, self_mask=self_mask, cross_mask=cross_mask,
        ),
        {"enc": enc_lengths, "dec": dec_lengths},
        lambda name: loaded(name).wait(),
        lambda name: loaded(name).start(),
    )
    deep = [k for k, (m, *_) in enumerate(pieces) if wholes[m].shape[4] > 3]

    def ring(k):
        _, _, size, _ = pieces[k]
        if k in deep:
            return deep_ring.at[deep.index(k) % 2, ..., pl.ds(0, size)]
        return wide_ring.at[k % RING, ..., pl.ds(0, size)]

    def weight(k):
        m, start, size, _ = pieces[k]
        return pltpu.make_async_copy(wholes[m].at[..., pl.ds(start, size)], ring(k), ring_sem.at[k])

    work = []
    for k, (m, start, size, z_first) in enumerate(pieces):
        total, lasts, zs, firsts = take(4)
        work.append(
            Scatter(
                place, ring(k), z_first, outs[m].at[:, :, pl.ds(start, size)], total, lasts, zs, firsts,
                (send, recv), k * Scatter.SEMS,
            )
        )
    for k in range(2):
        weight(k).start()
    for name in HELD:
        if name[:2] != "e_" and name not in ("hm", "d_x1", "d_o", "d_h1"):
            loaded(name).start()
    fill_masks(enc_lengths, dec_lengths, enc_mask, self_mask, cross_mask)
    last_slot = STRIDE * (Scatter.PHASES - 1)
    for slot in range(len(work) + last_slot):
        for k in range(len(work)):
            if (slot - k) % STRIDE == 0 and STRIDE <= slot - k <= last_slot:
                work[k].phase((slot - k) // STRIDE)
        k = slot
        if k >= len(work):
            continue
        if 0 < k < len(work) - 1:
            weight(k + 1).start()
        m, start, size, _ = pieces[k]
        first = k == 0 or pieces[k - 1][0] != m
        last = k == len(work) - 1 or pieces[k + 1][0] != m
        columns = pl.ds(start, size)
        if first:
            backward.before(m)
        left, right = backward.factors(m)
        weight(k).wait()
        part = ring(k)
        backward.back(m, columns, part, first)
        cut = Z if k in deep else 2
        tall = left.shape[1] // cut
        grad_columns = right[:, columns]
        for j in range(cut):
            grad = dot(left[:, j * tall : (j + 1) * tall], grad_columns, TN)
            layers = part.at[pl.ds(j * (Z // cut), Z // cut)]
            layers[...] = grad.reshape(layers.shape).astype(bf16)
        work[k].phase(0)
        if last:
            backward.after(m)


def backward_all(wholes, stored, enc_input, dec_input, enc_cot, dec_cot, gains, enc_lengths, dec_lengths):
    count = len(wholes)
    pieces = PIECES[:0:-1]
    groups = [w.shape[4] for w in wholes]
    rows, short = enc_input.shape[0], dec_input.shape[0]
    hbm, vmem = pl.BlockSpec(memory_space=pl.ANY), pl.BlockSpec(memory_space=pltpu.VMEM)
    smem = pl.BlockSpec(memory_space=pltpu.SMEM)
    wide = max(size for m, _, size, _ in pieces if groups[m] == 3)
    deep = max((groups[m], size) for m, _, size, _ in pieces)
    sems = len(pieces) * Scatter.SEMS
    scratch = [
        pltpu.SemaphoreType.DMA((sems,)),
        pltpu.SemaphoreType.DMA((sems,)),
        pltpu.SemaphoreType.DMA((len(HELD),)),
        pltpu.SemaphoreType.DMA((len(pieces),)),
        pltpu.VMEM((rows, FF), bf16),
        pltpu.VMEM((rows, 2 * FF), bf16),
        pltpu.VMEM((rows, D), bf16),
        pltpu.VMEM((rows, D), f32),
        pltpu.VMEM((short, D), bf16),
        pltpu.VMEM((rows, 2 * D), bf16),
        pltpu.VMEM((rows, D), bf16),
        pltpu.VMEM((rows, 3 * D), bf16),
        pltpu.VMEM((rows, D), bf16),
        pltpu.VMEM((rows, D), bf16),
        pltpu.VMEM((rows, D), bf16),
        pltpu.VMEM((rows, FF), f32),
        pltpu.VMEM((rows, D), f32),
        pltpu.VMEM((rows, rows), f32),
        pltpu.VMEM((short, short), f32),
        pltpu.VMEM((short, rows), f32),
        pltpu.VMEM((RING, Z, 2, 2, 2, 3, 8, wide), bf16),
        pltpu.VMEM((2, Z, 2, 2, 2, deep[0], 8, deep[1]), bf16),
    ]
    for m, _, size, z_first in pieces:
        block = (groups[m], 8, size)
        scratch += [
            pltpu.VMEM((Z, 2, 2, *block), bf16),
            pltpu.VMEM((Z, 2, *block), bf16),
            pltpu.VMEM((5, *(() if z_first else (2,)), *block), bf16),
            pltpu.VMEM((*((Z,) if z_first else ()), *block), bf16),
        ]
    outs = pl.pallas_call(
        functools.partial(backward_body, pieces, count),
        out_shape=[jax.ShapeDtypeStruct(w.shape[4:], f32) for w in wholes]
        + [jax.ShapeDtypeStruct((rows, D), f32), jax.ShapeDtypeStruct((short, D), f32)],
        in_specs=[hbm] * (count + len(HELD)) + [vmem] * 5 + [smem] * 2,
        out_specs=[vmem] * (count + 2),
        scratch_shapes=scratch,
        compiler_params=pltpu.CompilerParams(
            collective_id=1, has_side_effects=True, vmem_limit_bytes=VMEM_LIMIT
        ),
    )(
        *wholes, *[stored[name] for name in HELD], enc_input, dec_input, enc_cot, dec_cot, gains,
        enc_lengths, dec_lengths,
    )
    return outs[:count], outs[count], outs[count + 1]


VMEM_LIMIT = 60 * 2**20


def finish_body(count, scaled, *refs):
    refs = list(refs)

    def take(n):
        got = refs[:n]
        del refs[:n]
        return got

    totals, shards, (scales,), passed = take(count), take(len(scaled)), take(1), take(4)
    grads, scale_grads, through = take(count), take(len(scaled)), take(4)
    for total, grad in zip(totals, grads):
        grad[...] = total[...].reshape(grad.shape)
    for k, (m, shard, out) in enumerate(zip(scaled, shards, scale_grads)):
        product = grads[m][...] * shard[...].astype(f32)
        summed = lax.dot_general(
            jnp.ones((8, product.shape[1]), f32), product, NT,
            precision=lax.Precision.HIGHEST, preferred_element_type=f32,
        )
        out[...] = summed[0:1] / scales[k : k + 1].astype(f32)
    for src, out in zip(passed, through):
        out[...] = src[...]


def finish(totals, shards, scales, passed):
    scaled = [m for m, k in enumerate(SCALE_OF) if k is not None]
    vmem = pl.BlockSpec(memory_space=pltpu.VMEM)
    count = len(totals)
    outs = pl.pallas_call(
        functools.partial(finish_body, count, scaled),
        out_shape=[jax.ShapeDtypeStruct(s.shape, f32) for s in shards]
        + [jax.ShapeDtypeStruct((1, scales.shape[1]), f32)] * len(scaled)
        + [jax.ShapeDtypeStruct(p.shape, p.dtype) for p in passed],
        in_specs=[vmem] * (count + len(scaled) + 5),
        out_specs=[vmem] * (count + len(scaled) + 4),
        compiler_params=pltpu.CompilerParams(vmem_limit_bytes=VMEM_LIMIT),
    )(*totals, *[shards[m] for m in scaled], scales, *passed)
    return outs[:count], [g.reshape(-1) for g in outs[count:-4]], outs[-4:]


def norm_rows(values, scales):
    return values * lax.rsqrt(jnp.mean(values * values, axis=-1, keepdims=True) + epsilon) * scales


def norm_back(inputs, scales, grad):
    return jax.vjp(lambda v: norm_rows(v, scales), inputs)[1](grad)[0]


def gated_units(united):
    halfway = united.shape[-1] // 2
    return jax.nn.gelu(united[:, :halfway], approximate=True) * united[:, halfway:]


def row_items(lengths, row_count):
    places = jnp.arange(row_count, dtype=jnp.int32)
    count = lengths.shape[0]
    item, boundary = jnp.zeros((row_count,), jnp.int32), jnp.int32(0)
    for k in range(count):
        boundary = boundary + lengths[k]
        item = item + (places >= boundary).astype(jnp.int32)
    return item


def head_split(matrix):
    return matrix.reshape(matrix.shape[0], HEADS, HEAD_DIM)


def outer_rows(left, right):
    return jnp.einsum("rd,re->de", left, right, preferred_element_type=jnp.float32).astype(jnp.bfloat16)


def back_rows(incoming, matrix):
    return jnp.einsum("re,de->rd", incoming, matrix, preferred_element_type=jnp.float32)


def score_rows(query_heads, key_heads, allowed):
    raw_scores = jnp.einsum(
        "qhd,khd->hqk", query_heads, key_heads, preferred_element_type=jnp.float32
    )
    return jnp.where(allowed[None], raw_scores * HEAD_DIM ** (-0.5), masked_value)


def attend_forward(queries, keys_in, values_in, allowed):
    scores = score_rows(head_split(queries), head_split(keys_in), allowed)
    largest = jnp.max(scores, axis=2, keepdims=True)
    expanded = jnp.exp(scores - largest)
    totals = jnp.sum(expanded, axis=2, keepdims=True)
    weights = (expanded / totals).astype(jnp.bfloat16)
    mixed = jnp.einsum(
        "hqk,khd->qhd", weights, head_split(values_in), preferred_element_type=jnp.float32
    )
    return (mixed.reshape(queries.shape[0], D), largest + jnp.log(totals))


def attend_backward(queries, keys_in, values_in, allowed, log_totals, grad_mixed):
    query_heads = head_split(queries)
    key_heads = head_split(keys_in)
    value_heads = head_split(values_in)
    probs = jnp.exp(score_rows(query_heads, key_heads, allowed) - log_totals)
    grad_heads = head_split(grad_mixed)
    grad_values = jnp.einsum(
        "hqk,qhd->khd", probs.astype(jnp.bfloat16), grad_heads, preferred_element_type=jnp.float32
    )
    grad_probs = jnp.einsum(
        "qhd,khd->hqk", grad_heads, value_heads, preferred_element_type=jnp.float32
    )
    centred = grad_probs - jnp.sum(probs * grad_probs, axis=2, keepdims=True)
    grad_scores = (probs * centred * HEAD_DIM ** (-0.5)).astype(jnp.bfloat16)
    grad_queries = jnp.einsum(
        "hqk,khd->qhd", grad_scores, key_heads, preferred_element_type=jnp.float32
    )
    grad_keys = jnp.einsum(
        "hqk,qhd->khd", grad_scores, query_heads, preferred_element_type=jnp.float32
    )
    return (
        grad_queries.reshape(queries.shape[0], D),
        grad_keys.reshape(keys_in.shape[0], D),
        grad_values.reshape(keys_in.shape[0], D),
    )


def self_forward(inputs, params, allowed, live_rows):
    scales, joined, outward = params
    normed = norm_rows(inputs, scales).astype(jnp.bfloat16)
    projected = jnp.dot(normed, joined, preferred_element_type=jnp.float32).astype(jnp.bfloat16)
    mixed, log_totals = attend_forward(
        projected[:, :D], projected[:, D : 2 * D], projected[:, 2 * D :], allowed
    )
    mixed_low = mixed.astype(jnp.bfloat16)
    branch = jnp.dot(mixed_low, outward, preferred_element_type=jnp.float32)
    return (inputs + live_rows[:, None] * branch, (normed, projected, mixed_low, log_totals))


def self_backward(inputs, params, allowed, live_rows, stored, incoming):
    scales, joined, outward = params
    normed, projected, mixed_low, log_totals = stored
    grad_branch = (live_rows[:, None] * incoming).astype(jnp.bfloat16)
    grad_outward = outer_rows(mixed_low, grad_branch)
    grad_mixed = back_rows(grad_branch, outward).astype(jnp.bfloat16)
    grad_parts = attend_backward(
        projected[:, :D],
        projected[:, D : 2 * D],
        projected[:, 2 * D :],
        allowed,
        log_totals,
        grad_mixed,
    )
    grad_projected = jnp.concatenate(grad_parts, axis=1).astype(jnp.bfloat16)
    grad_joined = outer_rows(normed, grad_projected)
    grad_inputs = norm_back(inputs, scales, back_rows(grad_projected, joined))
    return (incoming + grad_inputs, (grad_joined, grad_outward))


def cross_forward(inputs, memory, params, allowed, live_rows):
    scales, memory_scales, query_map, pair_map, outward = params
    normed = norm_rows(inputs, scales).astype(jnp.bfloat16)
    memory_normed = norm_rows(memory, memory_scales).astype(jnp.bfloat16)
    queries = jnp.dot(normed, query_map, preferred_element_type=jnp.float32).astype(jnp.bfloat16)
    pairs = jnp.dot(memory_normed, pair_map, preferred_element_type=jnp.float32).astype(
        jnp.bfloat16
    )
    mixed, log_totals = attend_forward(queries, pairs[:, :D], pairs[:, D:], allowed)
    mixed_low = mixed.astype(jnp.bfloat16)
    branch = jnp.dot(mixed_low, outward, preferred_element_type=jnp.float32)
    return (
        inputs + live_rows[:, None] * branch,
        (normed, memory_normed, queries, pairs, mixed_low, log_totals),
    )


def cross_backward(inputs, memory, params, allowed, live_rows, stored, incoming):
    scales, memory_scales, query_map, pair_map, outward = params
    normed, memory_normed, queries, pairs, mixed_low, log_totals = stored
    grad_branch = (live_rows[:, None] * incoming).astype(jnp.bfloat16)
    grad_outward = outer_rows(mixed_low, grad_branch)
    grad_mixed = back_rows(grad_branch, outward).astype(jnp.bfloat16)
    grad_queries, grad_keys, grad_values = attend_backward(
        queries, pairs[:, :D], pairs[:, D:], allowed, log_totals, grad_mixed
    )
    grad_queries_low = grad_queries.astype(jnp.bfloat16)
    grad_pairs = jnp.concatenate([grad_keys, grad_values], axis=1).astype(jnp.bfloat16)
    grad_query_map = outer_rows(normed, grad_queries_low)
    grad_pair_map = outer_rows(memory_normed, grad_pairs)
    grad_inputs = norm_back(inputs, scales, back_rows(grad_queries_low, query_map))
    grad_memory = norm_back(memory, memory_scales, back_rows(grad_pairs, pair_map))
    return (
        incoming + grad_inputs,
        grad_memory,
        (grad_query_map, grad_pair_map, grad_outward),
    )


def mlp_forward(inputs, params, live_rows):
    scales, inward, outward = params
    normed = norm_rows(inputs, scales).astype(jnp.bfloat16)
    united = jnp.dot(normed, inward, preferred_element_type=jnp.float32)
    activated = gated_units(united).astype(jnp.bfloat16)
    branch = jnp.dot(activated, outward, preferred_element_type=jnp.float32)
    return (inputs + live_rows[:, None] * branch, (normed, united, activated))


def mlp_backward(inputs, params, live_rows, stored, incoming):
    scales, inward, outward = params
    normed, united, activated = stored
    grad_branch = (live_rows[:, None] * incoming).astype(jnp.bfloat16)
    grad_outward = outer_rows(activated, grad_branch)
    grad_activated = back_rows(grad_branch, outward)
    _, pullback = jax.vjp(gated_units, united)
    grad_united = pullback(grad_activated)[0].astype(jnp.bfloat16)
    grad_inward = outer_rows(normed, grad_united)
    grad_inputs = norm_back(inputs, scales, back_rows(grad_united, inward))
    return (incoming + grad_inputs, (grad_inward, grad_outward))


def plain_gather(shards):
    return [lax.all_gather(s, AXES, axis=0, tiled=True) for s in shards]


def plain_scatter(sums):
    return [lax.psum_scatter(s.astype(jnp.float32), AXES, scatter_dimension=0, tiled=True) for s in sums]


SCALE_OF = (0, None, 1, None, 2, None, 3, 4, None, 5, None)


def per_device(
    linked,
    enc_input,
    dec_input,
    enc_lengths,
    dec_lengths,
    enc_attn_gain,
    enc_qkv,
    enc_attn_out,
    enc_mlp_gain,
    enc_mlp_in,
    enc_mlp_out,
    dec_self_gain,
    dec_qkv,
    dec_self_out,
    cross_gain,
    memory_gain,
    cross_query,
    cross_kv,
    cross_out,
    dec_mlp_gain,
    dec_mlp_in,
    dec_mlp_out,
    enc_cotangent,
    dec_cotangent,
):
    gains = [enc_attn_gain, enc_mlp_gain, dec_self_gain, cross_gain, memory_gain, dec_mlp_gain]
    shards = (
        enc_qkv, enc_attn_out, enc_mlp_in, enc_mlp_out, dec_qkv, dec_self_out,
        cross_query, cross_kv, cross_out, dec_mlp_in, dec_mlp_out,
    )
    if linked:
        stacked = jnp.stack(gains + [jnp.zeros_like(gains[0])] * (8 - len(gains)))
        (*whole, _), kept, enc_out, dec_out, spread = forward_all(
            shards, stacked, enc_input, dec_input, enc_lengths, dec_lengths
        )
        summed, grad_encoder_start, grad_decoder_start = backward_all(
            whole, kept, enc_input, dec_input, enc_cotangent, dec_cotangent, spread, enc_lengths, dec_lengths
        )
        grads, scale_grads, (enc_out, dec_out, grad_encoder_start, grad_decoder_start) = finish(
            summed, shards, stacked, (enc_out, dec_out, grad_encoder_start, grad_decoder_start)
        )
    else:
        item_count = enc_lengths.shape[0]
        enc_items = row_items(enc_lengths, enc_input.shape[0])
        dec_items = row_items(dec_lengths, dec_input.shape[0])
        enc_live = (enc_items < item_count).astype(jnp.float32)
        dec_live = (dec_items < item_count).astype(jnp.float32)
        enc_padded = enc_items[:, None] == item_count
        dec_padded = dec_items[:, None] == item_count
        enc_allowed = (enc_items[:, None] == enc_items[None, :]) | enc_padded
        dec_places = jnp.arange(dec_input.shape[0], dtype=jnp.int32)
        self_allowed = (dec_items[:, None] == dec_items[None, :]) & (
            dec_places[None, :] <= dec_places[:, None]
        ) | dec_padded
        cross_allowed = (dec_items[:, None] == enc_items[None, :]) | dec_padded
        whole = plain_gather(shards)
        own = [g.astype(jnp.float32) for g in gains]
        gains = plain_gather(own)
        encoder_start = enc_input.astype(jnp.float32)
        decoder_start = dec_input.astype(jnp.float32)
        enc_middle, enc_attn_store = self_forward(encoder_start, (gains[0], *whole[0:2]), enc_allowed, enc_live)
        encoder_final, enc_mlp_store = mlp_forward(enc_middle, (gains[1], *whole[2:4]), enc_live)
        dec_middle, dec_self_store = self_forward(decoder_start, (gains[2], *whole[4:6]), self_allowed, dec_live)
        dec_crossed, cross_store = cross_forward(
            dec_middle, encoder_final, (gains[3], gains[4], *whole[6:9]), cross_allowed, dec_live
        )
        decoder_final, dec_mlp_store = mlp_forward(dec_crossed, (gains[5], *whole[9:11]), dec_live)
        enc_out, dec_out = encoder_final.astype(jnp.bfloat16), decoder_final.astype(jnp.bfloat16)
        grad_crossed, dec_mlp_grads = mlp_backward(
            dec_crossed, (gains[5], *whole[9:11]), dec_live, dec_mlp_store, dec_cotangent.astype(jnp.float32)
        )
        grad_middle, grad_memory, cross_grads = cross_backward(
            dec_middle,
            encoder_final,
            (gains[3], gains[4], *whole[6:9]),
            cross_allowed,
            dec_live,
            cross_store,
            grad_crossed,
        )
        grad_decoder_start, dec_self_grads = self_backward(
            decoder_start, (gains[2], *whole[4:6]), self_allowed, dec_live, dec_self_store, grad_middle
        )
        grad_enc_middle, enc_mlp_grads = mlp_backward(
            enc_middle,
            (gains[1], *whole[2:4]),
            enc_live,
            enc_mlp_store,
            enc_cotangent.astype(jnp.float32) + grad_memory,
        )
        grad_encoder_start, enc_attn_grads = self_backward(
            encoder_start, (gains[0], *whole[0:2]), enc_allowed, enc_live, enc_attn_store, grad_enc_middle
        )
        sums = enc_attn_grads + enc_mlp_grads + dec_self_grads + cross_grads + dec_mlp_grads
        summed = plain_scatter(sums)
        grads, scale_grads = [], {}
        for total, shard, k in zip(summed, shards, SCALE_OF):
            if k is not None:
                scale_grads[k] = jnp.sum(total * shard.astype(jnp.float32), axis=1) / own[k]
            grads.append(total)
    return (
        enc_out,
        dec_out,
        grad_encoder_start,
        grad_decoder_start,
        scale_grads[0], grads[0], grads[1],
        scale_grads[1], grads[2], grads[3],
        scale_grads[2], grads[4], grads[5],
        scale_grads[3], scale_grads[4], grads[6], grads[7], grads[8],
        scale_grads[5], grads[9], grads[10],
    )


def solution(mesh):
    rows, line = P(AXES, None), P(AXES)
    linked = mesh.shape["wide"] == 2 * Z and mesh.shape["narrow"] == 4
    weights = (
        line, rows, rows, line, rows, rows, line, rows, rows,
        line, line, rows, rows, rows, line, rows, rows,
    )
    return jax.shard_map(
        functools.partial(per_device, linked),
        mesh=mesh,
        in_specs=(rows, rows, line, line, *weights, rows, rows),
        out_specs=(rows, rows, rows, rows, *weights),
        check_vma=False,
    )
```

```python
import functools

import jax
import jax.numpy as jnp
from jax import lax
from jax.experimental import pallas as pl
from jax.experimental.pallas import tpu as pltpu
from jax.sharding import PartitionSpec as P

D = 768
HEADS = 12
HEAD_DIM = 64
FF = 2048
AXES = ("wide", "narrow")
MESH = pl.DeviceIdType.MESH

Z = 4
PIECES = (
    (11, 0, 768, False),
    (0, 0, 1152, False), (0, 1152, 1152, True), (1, 0, 768, False),
    (2, 0, 1024, False), (2, 1024, 1024, True), (2, 2048, 1024, False), (2, 3072, 1024, False),
    (3, 0, 384, True), (3, 384, 384, False),
    (4, 0, 1152, False), (4, 1152, 1152, True), (5, 0, 768, False), (6, 0, 768, False),
    (7, 0, 768, True), (7, 768, 768, False), (8, 0, 768, False),
    (9, 0, 1024, True), (9, 1024, 1024, False), (9, 2048, 1024, False), (9, 3072, 1024, True),
    (10, 0, 384, False), (10, 384, 384, False),
)
STRIDE = 2


class Place:
    def __init__(self):
        self.w, self.n = lax.axis_index("wide"), lax.axis_index("narrow")
        self.z, self.y = self.w // 2, self.w % 2
        self.x, self.c = self.n // 2, self.n % 2
        w, n, y, x, c = self.w, self.n, self.y, self.x, self.c
        self.sibling = (w, n + 1 - 2 * c)
        self.first = (w + (1 - c) * (1 - 2 * y), n + c * (2 - 4 * x))
        self.last = (w + c * (1 - 2 * y), n + (1 - c) * (2 - 4 * x))
        self.above = (w + 2, n)
        self.below = (w - 2, n)

    def barrier(self):
        sem = pltpu.get_barrier_semaphore()
        for device in (self.sibling, self.first, self.last):
            pl.semaphore_signal(sem, inc=1, device_id=device, device_id_type=MESH)

        @pl.when(self.z < Z - 1)
        def _():
            pl.semaphore_signal(sem, inc=1, device_id=self.above, device_id_type=MESH)

        @pl.when(self.z > 0)
        def _():
            pl.semaphore_signal(sem, inc=1, device_id=self.below, device_id_type=MESH)

        inner = jnp.where(self.z * (Z - 1 - self.z) > 0, 1, 0)
        pl.semaphore_wait(sem, 4 + inner)

    def by_core(self, do):
        @pl.when(self.c == 0)
        def _():
            do(0)

        @pl.when(self.c == 1)
        def _():
            do(1)


def remote(src, dst, sems, index, device):
    send, recv = sems
    return pltpu.make_async_remote_copy(
        src_ref=src, dst_ref=dst, send_sem=send.at[index], recv_sem=recv.at[index],
        device_id=device, device_id_type=MESH,
    )


class Gather:
    PHASES = 7
    SEMS = 13

    def __init__(self, place, part, whole, columns, z_first, sems, base, local_sem):
        self.p, self.z_first, self.sems, self.base = place, z_first, sems, base
        self.part = part.at[:, :, columns]
        self.whole = whole.at[:, :, :, :, :, :, columns]
        self.local = pltpu.make_async_copy(self.part, self.own(), local_sem)

    def own(self):
        p = self.p
        return self.whole.at[p.z, p.y, p.x, p.c]

    def copy(self, src, dst, slot, device):
        return remote(src, dst, self.sems, self.base + slot, device)

    def layer(self, zz, core):
        p = self.p
        if self.z_first:
            return self.whole.at[zz, p.y, p.x, core]
        return self.whole.at[zz, :, p.x, 0] if core == 0 else self.whole.at[zz, p.y, :, 1]

    def half(self, core, mine):
        p = self.p
        if core == 0:
            return self.whole.at[:, :, p.x if mine else 1 - p.x, 0]
        return self.whole.at[:, p.y if mine else 1 - p.y, :, 1]

    def along_z(self, step, sending):
        p = self.p

        def go(core):
            for up in (True, False):
                if sending:
                    zz = p.z - step if up else p.z + step
                    there = (p.z < Z - 1) & (zz >= 0) if up else (p.z > 0) & (zz < Z)
                else:
                    zz = p.z - 1 - step if up else p.z + 1 + step
                    there = zz >= 0 if up else zz < Z

                target = (p.above if up else p.below) if sending else p.last

                @pl.when(there)
                def _():
                    block = self.layer(zz, core)
                    copy = self.copy(block, block, 1 + step * 2 + up, target)
                    copy.start() if sending else copy.wait_recv()

        p.by_core(go)

    def along_z_sent(self):
        p = self.p

        def go(core):
            for step in range(3):
                for up in (True, False):
                    zz = p.z - step if up else p.z + step
                    there = (p.z < Z - 1) & (zz >= 0) if up else (p.z > 0) & (zz < Z)

                    @pl.when(there)
                    def _():
                        block = self.layer(zz, core)
                        self.copy(block, block, 1 + step * 2 + up, p.last).wait_send()

        p.by_core(go)

    def first(self, core):
        p = self.p
        if not self.z_first:
            return self.copy(self.part, self.own(), 0, p.first)
        block = self.whole.at[:, p.y, p.x, core]
        return self.copy(block, block, 0, p.first)

    def last(self, core):
        block = self.half(core, True)
        return self.copy(block, block, 7, self.p.last)

    def last_layer(self, zz, core, mine=True):
        p = self.p
        if core == 0:
            block = self.whole.at[zz, :, p.x if mine else 1 - p.x, 0]
        else:
            block = self.whole.at[zz, p.y if mine else 1 - p.y, :, 1]
        return self.copy(block, block, 7 + zz, p.last)

    def far_layers(self, far, core, verb):
        z = self.p.z
        if far == 0:
            getattr(self.last_layer(z, core), verb)()
            return

        @pl.when(z + far < Z)
        def _():
            getattr(self.last_layer(z + far, core), verb)()

        @pl.when(z - far >= 0)
        def _():
            getattr(self.last_layer(z - far, core), verb)()

    def send_far(self, far):
        self.p.by_core(lambda core: self.far_layers(far, core, "start"))

    def wait_last(self, core, verb):
        if self.z_first:
            getattr(self.last(core), verb)()
        else:
            for zz in range(Z):
                getattr(self.last_layer(zz, core, verb == "wait_send"), verb)()

    def across(self, core, mine):
        block = self.half(core, mine)
        return self.copy(block, block, 11 if mine else 12, self.p.sibling)

    def each(self, make, *verbs):
        def go(core):
            copy = make(core)
            for verb in verbs:
                getattr(copy, verb)()

        self.p.by_core(go)

    def phase(self, number):
        early = not self.z_first
        if number == 0:
            self.local.start()
            if early:
                self.each(self.first, "start")
            self.local.wait()
            if not early:
                self.along_z(0, True)
        elif number == 1:
            if early:
                self.each(self.first, "wait_recv")
                self.along_z(0, True)
                self.send_far(0)
            else:
                self.along_z(0, False)
                self.along_z(1, True)
        elif number == 2:
            self.along_z(0 if early else 1, False)
            self.along_z(1 if early else 2, True)
            if early:
                self.send_far(1)
        elif number == 3:
            self.along_z(1 if early else 2, False)
            if early:
                self.along_z(2, True)
                self.send_far(2)
            else:
                self.each(self.first, "start")
        elif number == 4:
            if early:
                self.along_z(2, False)
                self.send_far(3)
            else:
                self.each(self.first, "wait_recv")
                self.each(self.last, "start")
            self.each(lambda core: self.across(core, True), "start")
        elif number == 5:
            self.p.by_core(lambda core: self.wait_last(core, "wait_recv"))
            self.each(lambda core: self.across(core, False), "start")
        else:
            for core in (0, 1):
                @pl.when(self.p.c == core)
                def _():
                    for mine in (True, False):
                        self.across(1 - core, mine).wait_recv()
                        self.across(core, mine).wait_send()
                    self.first(core).wait_send()
                    self.wait_last(core, "wait_send")
            self.along_z_sent()


class Scatter:
    PHASES = 8
    SEMS = 12

    def __init__(self, place, parts, z_first, out, leave, total, lasts, zs, firsts, sems, base):
        self.p, self.z_first, self.sems, self.base = place, z_first, sems, base
        self.parts, self.out, self.leave = parts, out, leave
        self.total, self.lasts, self.zs, self.firsts = total, lasts, zs, firsts

    def copy(self, src, dst, slot, device):
        return remote(src, dst, self.sems, self.base + slot, device)

    def spot(self, core, last, first=None):
        every = slice(None)
        if first is None:
            return (every, last) if core else (every, every, last)
        return (last, first) if core else (first, last)

    def place_of(self, core):
        p = self.p
        return (p.y, p.x) if core else (p.x, p.y)

    def across(self, core):
        return self.copy(self.parts.at[:, :, :, 1 - core], self.total, 0, self.p.sibling)

    def last(self, core):
        last, _ = self.place_of(core)
        return self.copy(self.total.at[self.spot(core, 1 - last)], self.lasts, 8, self.p.last)

    def last_layer(self, zz, core):
        last, _ = self.place_of(core)
        src = self.total.at[(zz, *self.spot(core, 1 - last)[1:])]
        return self.copy(src, self.lasts.at[zz], 8 + zz, self.p.last)

    def far_layers(self, far, do):
        z = self.p.z
        if far == 0:
            do(z)
            return

        @pl.when(z + far < Z)
        def _():
            do(z + far)

        @pl.when(z - far >= 0)
        def _():
            do(z - far)

    def send_layers(self, core):
        for far in (3, 2, 1, 0):
            self.far_layers(far, lambda zz: self.last_layer(zz, core).start())

    def add_layers(self, far):
        def one(zz):
            self.p.by_core(lambda core: self.last_layer(zz, core).wait_recv())
            for k in range(2):
                self.total[(zz, *self.pair(k))] += self.lasts[zz, k]

        self.far_layers(far, one)

    def last_sent(self, core):
        if self.z_first:
            self.last(core).wait_send()
        else:
            for zz in range(Z):
                self.last_layer(zz, core).wait_send()

    def first(self, core):
        p = self.p
        last, first = self.place_of(core)
        if self.z_first:
            src = self.total.at[(slice(None), *self.spot(core, last, 1 - first))]
        else:
            src = self.total.at[(p.z, *self.spot(core, last, 1 - first))]
        return self.copy(src, self.firsts, 1, p.first)

    def layer(self, zz, core):
        last, first = self.place_of(core)
        if self.z_first:
            return self.total.at[(zz, *self.spot(core, last, first))]
        return self.total.at[(zz, *self.spot(core, last)[1:])]

    def way(self, step, up, sending):
        z, far = self.p.z, 2 - step
        if sending:
            zz = z + 1 + far if up else z - 1 - far
            return zz, zz < Z if up else zz >= 0
        zz = z + far if up else z - far
        return zz, (z > 0) & (zz < Z) if up else (z < Z - 1) & (zz >= 0)

    def landing(self, step, up):
        return 0 if step == 0 else 2 * step - 1 + up

    def along_z(self, step, verb):
        p = self.p

        def go(core):
            for up in (True, False):
                zz, there = self.way(step, up, verb != "wait_recv")
                target = (p.above if up else p.below) if verb == "start" else p.last

                @pl.when(there)
                def _():
                    copy = self.copy(self.layer(zz, core), self.zs.at[self.landing(step, up)], 2 + step * 2 + up, target)
                    getattr(copy, verb)()

        p.by_core(go)

    def add_z(self, step):
        p = self.p
        for up in (True, False):
            zz, there = self.way(step, up, False)

            @pl.when(there)
            def _():
                arrived = self.zs.at[self.landing(step, up)]
                if self.z_first:
                    self.total[zz, p.y, p.x] += arrived[...]
                else:
                    for k in range(2):
                        self.total[(zz, *self.pair(k))] += arrived[k]

    def pair(self, k):
        p = self.p
        return k * (1 - p.c) + p.y * p.c, p.x * (1 - p.c) + k * p.c

    def each(self, make, *verbs):
        def go(core):
            copy = make(core)
            for verb in verbs:
                getattr(copy, verb)()

        self.p.by_core(go)

    def phase(self, number):
        p, early = self.p, self.z_first
        if number == 0:
            self.each(self.across, "start")
        elif number == 1:
            self.each(self.across, "wait_recv")

            @pl.loop(0, 16)
            def _(i):
                self.total[i // 4, i // 2 % 2, i % 2] += self.parts[i // 4, i // 2 % 2, i % 2, p.c]

            if early:
                self.each(self.last, "start")
            else:
                p.by_core(self.send_layers)
            self.each(self.across, "wait_send")
        elif number == 2:
            if early:
                self.each(self.last, "wait_recv")

                @pl.loop(0, 8)
                def _(i):
                    self.total[(i // 2, *self.pair(i % 2))] += self.lasts[i // 2, i % 2]

                self.each(self.first, "start")
            else:
                self.add_layers(3)
                self.along_z(0, "start")
        elif number == 3:
            if early:
                self.each(self.first, "wait_recv")

                @pl.loop(0, Z)
                def _(i):
                    self.total[i, p.y, p.x] += self.firsts[i]

                self.along_z(0, "start")
            else:
                self.add_layers(2)
                self.along_z(0, "wait_recv")
                self.add_z(0)
                self.along_z(1, "start")
        elif number == 4:
            step = 0 if early else 1
            if not early:
                self.add_layers(1)
            self.along_z(step, "wait_recv")
            self.add_z(step)
            self.along_z(step + 1, "start")
        elif number == 5:
            step = 1 if early else 2
            if not early:
                self.add_layers(0)
            self.along_z(step, "wait_recv")
            self.add_z(step)
            if early:
                self.along_z(2, "start")
            else:
                self.each(self.first, "start")
        elif number == 6:
            if early:
                self.along_z(2, "wait_recv")
                self.add_z(2)
                self.out[...] = self.total[p.z, p.y, p.x].astype(jnp.float32)
            else:
                self.each(self.first, "wait_recv")
                self.out[...] = self.total[p.z, p.y, p.x].astype(jnp.float32) + self.firsts[...].astype(jnp.float32)
            self.leave.start()
        else:
            self.leave.wait()
            p.by_core(self.last_sent)
            self.each(self.first, "wait_send")
            for step in range(3):
                self.along_z(step, "wait_send")


epsilon = 1e-06
masked_value = -1000000000.0
SHRINK = HEAD_DIM**-0.5
NT = (((1,), (1,)), ((), ()))
TN = (((0,), (0,)), ((), ()))
f32, bf16 = jnp.float32, jnp.bfloat16


def dot(a, b, dims=(((1,), (0,)), ((), ()))):
    return lax.dot_general(a, b, dims, preferred_element_type=f32)


def shrunk(values):
    return lax.rsqrt(jnp.mean(values * values, axis=-1, keepdims=True) + epsilon)


def norm(values, scales):
    return values * shrunk(values) * scales


def items_of(lengths_ref, places):
    item, boundary = jnp.zeros_like(places), 0
    for k in range(lengths_ref.shape[0]):
        boundary = boundary + lengths_ref[k]
        item = item + jnp.where(places >= boundary, 1, 0)
    return item


def fill_masks(enc_lengths, dec_lengths, enc_mask, self_mask, cross_mask):
    count = enc_lengths.shape[0]

    def grid(ref, axis):
        return lax.broadcasted_iota(jnp.int32, ref.shape, axis)

    def put(ref, rows, columns, both):
        kept = rows == columns
        if both is not None:
            kept = kept & both
        ref[...] = jnp.where(kept | (rows == count), 1.0, 0.0)

    put(enc_mask, items_of(enc_lengths, grid(enc_mask, 0)), items_of(enc_lengths, grid(enc_mask, 1)), None)
    put(
        self_mask, items_of(dec_lengths, grid(self_mask, 0)), items_of(dec_lengths, grid(self_mask, 1)),
        grid(self_mask, 1) <= grid(self_mask, 0),
    )
    put(cross_mask, items_of(dec_lengths, grid(cross_mask, 0)), items_of(enc_lengths, grid(cross_mask, 1)), None)


def live_rows(lengths_ref, rows):
    item = items_of(lengths_ref, lax.broadcasted_iota(jnp.int32, (rows, 1), 0))
    return jnp.where(item < lengths_ref.shape[0], 1.0, 0.0)


def head_lanes(which):
    lanes = lax.broadcasted_iota(jnp.int32, (1, 2 * HEAD_DIM), 1)
    return jnp.where(lanes // HEAD_DIM == which, 1.0, 0.0).astype(bf16)


def head_probs(q, k, kept):
    scores = jnp.where(kept[...] > 0.0, dot(q, k, NT) * SHRINK, masked_value)
    raised = jnp.exp(scores - jnp.max(scores, axis=1, keepdims=True))
    return raised * (1.0 / jnp.sum(raised, axis=1, keepdims=True))


def pair_columns(pair, offset):
    return pl.ds(pl.multiple_of(pair * (2 * HEAD_DIM) + offset, 2 * HEAD_DIM), 2 * HEAD_DIM)


def attend(q_ref, q_at, k_ref, k_at, v_ref, v_at, kept, out_ref):
    @pl.loop(0, HEADS // 2)
    def _(pair):
        q = q_ref[:, pair_columns(pair, q_at)]
        k = k_ref[:, pair_columns(pair, k_at)]
        v = v_ref[:, pair_columns(pair, v_at)]
        mixed = None
        for which in range(2):
            lanes = head_lanes(which)
            part = dot(head_probs(q * lanes, k, kept).astype(bf16), v * lanes)
            mixed = part if mixed is None else mixed + part
        out_ref[:, pair_columns(pair, 0)] = mixed.astype(bf16)


def gelu_tanh(t):
    return jnp.tanh(0.7978845608028654 * (t + 0.044715 * (t * t * t)))


class Forward:
    def __init__(self, refs, held, lengths, store):
        self.__dict__.update(refs)
        self.held, self.lengths, self.store, self.leaving = held, lengths, store, {}

    def at(self, name):
        buffer = self.held[HELD[name]]
        return buffer.at[pl.ds(0, self.rows("dec"))] if name[0] == "d" or name in ("c_o", "hq") else buffer

    def rows(self, side):
        return self.e_x0.shape[0] if side == "enc" else self.d_x0.shape[0]

    def opened(self, name):
        copy = self.leaving.pop(HELD[name], None)
        if copy is not None:
            copy.wait()
        return self.at(name)

    def kept(self, name):
        if name in KEPT:
            copy = self.store(name)
            copy.start()
            self.leaving[HELD[name]] = copy

    def close(self):
        for copy in self.leaving.values():
            copy.wait()

    def set_norm(self, values, k, name):
        self.opened(name)[...] = norm(values, self.gains[k : k + 1]).astype(bf16)
        self.kept(name)

    def live(self, side):
        return live_rows(self.lengths[side], self.rows(side))

    def step(self, m, start, size, weight):
        columns = pl.ds(start, size)
        side, rows = ("e", "enc") if m < 4 else ("d", "dec")
        first = start == 0
        if m == 0 or m == 4:
            h1, qkv, o = side + "_h1", side + "_qkv", side + "_o"
            if first:
                before = self.e_x0 if m == 0 else self.d_x0
                self.set_norm(before[...].astype(f32), 0 if m == 0 else 2, h1)
                self.opened(qkv)
            ref = self.at(qkv)
            ref[:, columns] = dot(self.at(h1)[...], weight).astype(bf16)
            if start + size == ref.shape[1]:
                self.kept(qkv)
                attend(ref, 0, ref, D, ref, 2 * D, self.enc_mask if m == 0 else self.self_mask, self.opened(o))
                self.kept(o)
        elif m == 1 or m == 5:
            before, x1 = (self.e_x0, "e_x1") if m == 1 else (self.d_x0, "d_x1")
            after = before[...].astype(f32) + self.live(rows) * dot(self.at(side + "_o")[...], weight)
            self.opened(x1)[...] = after
            self.kept(x1)
            self.set_norm(self.at(x1)[...], 1 if m == 1 else 3, "e_h2" if m == 1 else "hq")
        elif m == 6:
            self.at("q")[...] = dot(self.at("hq")[...], weight).astype(bf16)
        elif m == 7:
            kv = self.at("kv")
            kv[:, columns] = dot(self.at("hm")[...], weight).astype(bf16)
            if start + size == kv.shape[1]:
                attend(self.at("q"), 0, kv, 0, kv, D, self.cross_mask, self.opened("c_o"))
        elif m == 8:
            after = self.live(rows) * dot(self.at("c_o")[...], weight)
            self.opened("d_x2")[...] += after
            self.set_norm(self.at("d_x2")[...], 5, "d_h2")
        elif m == 2 or m == 9:
            u, a = side + "_u", side + "_a"
            if first:
                self.opened(u)
                self.opened(a)
            united = dot(self.at(side + "_h2")[...], weight)
            self.at(u)[:, columns] = united.astype(bf16)
            if start < FF:
                self.gates[pl.ds(0, united.shape[0]), columns] = united
            else:
                back = pl.ds(start - FF, size)
                gate = self.gates[pl.ds(0, united.shape[0]), back]
                self.at(a)[:, back] = (0.5 * gate * (1.0 + gelu_tanh(gate)) * united).astype(bf16)
            if start + size == 2 * FF:
                self.kept(u)
                self.kept(a)
        else:
            if m == 3 and first:
                self.opened("e_x2")
            before = self.at("e_x1" if m == 3 else "d_x2")
            after = before[:, columns] + self.live(rows) * dot(self.at(side + "_a")[...], weight)
            out = self.enc_out if m == 3 else self.dec_out
            out[:, columns] = after.astype(bf16)
            if m == 3:
                self.at("e_x2")[:, columns] = after
                if start + size == D:
                    self.kept("e_x2")
                    self.set_norm(self.at("e_x2")[...], 4, "hm")


class Backward:
    def __init__(self, refs, lengths, load, free):
        self.__dict__.update(refs)
        self.lengths, self.load, self.free = lengths, load, free

    def rows(self, side):
        return self.e_x0.shape[0] if side == "enc" else self.d_x0.shape[0]

    def live(self, side):
        return live_rows(self.lengths[side], self.rows(side))

    def gain(self, k):
        return self.gains[k : k + 1]

    def top(self, ref, side):
        return ref.at[pl.ds(0, self.rows(side))]

    def side(self, m):
        return "enc" if m < 4 else "dec"

    def through_norm(self, values, k, grad, into):
        small = shrunk(values)
        unit = values * small
        grad = grad * self.gain(k)
        into[...] += small * (grad - unit * jnp.mean(grad * unit, axis=-1, keepdims=True))

    def set_branch(self, side):
        grad = self.e_grad if side == "enc" else self.d_grad
        self.top(self.dz, side)[...] = (self.live(side) * grad[...]).astype(bf16)

    def before(self, m):
        side = self.side(m)
        if m == 10 or m == 3:
            if m == 10:
                self.d_grad[...] = self.d_cot[...].astype(f32)
            self.set_branch(side)
            self.load("d_a" if m == 10 else "e_a")
        elif m == 9 or m == 2:
            self.load("d_u" if m == 9 else "e_u")
            self.load("d_h2" if m == 9 else "e_h2")
            u, da = self.top(self.u, side), self.top(self.da, side)

            @pl.loop(0, FF // 256)
            def _(j):
                at = pl.multiple_of(j * 256, 256)
                gate_at, up_at = pl.ds(at, 256), pl.ds(pl.multiple_of(at + FF, 256), 256)
                t, up, grad = u[:, gate_at].astype(f32), u[:, up_at].astype(f32), da[:, gate_at]
                th = gelu_tanh(t)
                slope = 0.5 * (1.0 + th) + 0.5 * t * (1.0 - th * th) * (
                    0.7978845608028654 * (1.0 + 0.134145 * (t * t))
                )
                u[:, gate_at] = (slope * up * grad).astype(bf16)
                u[:, up_at] = (0.5 * t * (1.0 + th) * grad).astype(bf16)
        elif m == 8:
            self.set_branch("dec")
            self.load("c_o")
        elif m == 7:
            for name in ("q", "kv", "hm"):
                self.load(name)
            self.attend_back(self.q, 0, self.kv, 0, self.kv, D, self.cross_mask, "dec")
        elif m == 6:
            self.load("hq")
        elif m == 5 or m == 1:
            self.set_branch(side)
            self.load("d_o" if m == 5 else "e_o")
        else:
            self.load("d_h1" if m == 4 else "e_h1")
            self.load("d_qkv" if m == 4 else "e_qkv")
            qkv = self.top(self.qkv, side)
            self.attend_back(qkv, 0, qkv, D, qkv, 2 * D, self.self_mask if m == 4 else self.enc_mask, side)

    def attend_back(self, q_ref, q_at, k_ref, k_at, v_ref, v_at, kept, side):
        grad_ref = self.top(self.do, side)

        @pl.loop(0, HEADS // 2)
        def _(pair):
            q = q_ref[:, pair_columns(pair, q_at)]
            k = k_ref[:, pair_columns(pair, k_at)]
            v = v_ref[:, pair_columns(pair, v_at)]
            grad = grad_ref[:, pair_columns(pair, 0)]
            dq = dk = dv = 0.0
            for which in range(2):
                lanes = head_lanes(which)
                q_half, grad_half = q * lanes, grad * lanes
                probs = head_probs(q_half, k, kept)
                dv = dv + dot(probs.astype(bf16), grad_half, TN)
                dp = dot(grad_half, v, NT)
                centred = dp - jnp.sum(probs * dp, axis=1, keepdims=True)
                ds = (probs * centred * SHRINK).astype(bf16)
                dq = dq + dot(ds, k * lanes)
                dk = dk + dot(ds, q_half, TN)
            q_ref[:, pair_columns(pair, q_at)] = dq.astype(bf16)
            k_ref[:, pair_columns(pair, k_at)] = dk.astype(bf16)
            v_ref[:, pair_columns(pair, v_at)] = dv.astype(bf16)

    def factors(self, m):
        side = self.side(m)
        left = {
            10: self.a, 3: self.a, 9: self.h2, 2: self.h2, 8: self.o, 7: self.h2, 6: self.h1,
            5: self.o, 1: self.o, 4: self.h1, 0: self.h1,
        }[m]
        right = {
            10: self.dz, 3: self.dz, 9: self.u, 2: self.u, 8: self.dz, 7: self.kv, 6: self.q,
            5: self.dz, 1: self.dz, 4: self.qkv, 0: self.qkv,
        }[m]
        if m != 7:
            left, right = self.top(left, side), self.top(right, side)
        return left, right

    def back(self, m, columns, weight, first):
        side = self.side(m)
        right = self.factors(m)[1][:, columns]
        if m in (10, 3):
            into = self.top(self.da, side)
            tall = FF // Z
            for j in range(Z):
                share = dot(right, weight[j].reshape(tall, -1), NT)
                if first:
                    into[:, j * tall : (j + 1) * tall] = share
                else:
                    into[:, j * tall : (j + 1) * tall] += share
            return
        share = dot(right, weight[...].reshape(D, -1), NT)
        into = self.dh if m == 7 else self.top(self.dh, side)
        if m in (8, 5, 1):
            self.top(self.do, side)[...] = share.astype(bf16)
        elif first:
            into[...] = share
        else:
            into[...] += share
    def after(self, m):
        side = self.side(m)
        into = self.dh if m == 7 else self.top(self.dh, side)
        if m == 10:
            self.free("e_a")
        elif m == 9:
            self.load("d_x2")
            self.through_norm(self.top(self.x, "dec")[...], 5, into[...], self.d_grad)
            for name in ("e_x2", "e_u", "hm"):
                self.free(name)
        elif m == 8:
            self.free("d_o")
        elif m == 7:
            self.load("e_x2")
            self.e_grad[...] = self.e_cot[...].astype(f32)
            self.through_norm(self.x[...], 4, into[...], self.e_grad)
            self.free("d_x1")
            self.free("e_h2")
        elif m == 6:
            self.load("d_x1")
            self.through_norm(self.top(self.x, "dec")[...], 3, into[...], self.d_grad)
            self.free("e_x1")
            self.free("d_h1")
        elif m == 5:
            self.free("e_o")
        elif m == 4:
            self.through_norm(self.d_x0[...].astype(f32), 2, into[...], self.d_grad)
            self.free("e_h1")
            self.free("e_qkv")
        elif m == 2:
            self.load("e_x1")
            self.through_norm(self.x[...], 1, into[...], self.e_grad)
        elif m == 0:
            self.through_norm(self.e_x0[...].astype(f32), 0, into[...], self.e_grad)


HELD = dict(
    e_a="a", d_a="a", e_u="u", d_u="u", e_h2="h2", hm="h2", d_h2="h2", e_x1="x", d_x1="x", d_x2="x", e_x2="dh",
    e_o="o", d_o="o", c_o="o", e_h1="h1", d_h1="h1", hq="h1", e_qkv="qkv", d_qkv="qkv", q="q", kv="kv",
)
KEPT = dict(
    hm="h2", d_x1="x", d_o="o", d_h1="h1", e_a="a", e_u="u", e_h2="h2", e_x2="x", e_x1="x", e_o="o", e_qkv="qkv", e_h1="h1",
)
RING = 3


def whole_body(pieces, back_pieces, count, *refs):
    refs = list(refs)

    def take(n):
        got = refs[:n]
        del refs[:n]
        return got

    parts = take(count)
    scales, e_x0, d_x0, e_cot, d_cot, enc_lengths, dec_lengths = take(7)
    outs = take(count)
    e_grad, d_grad, enc_out, dec_out = take(4)
    wholes = take(count + 1)
    away = dict(zip(KEPT, take(len(KEPT))))
    send, recv, local, back_send, back_recv, stage_sem, ring_sem, out_sem, away_sem, come_sem = take(10)
    names = ["a", "u", "h2", "x", "q", "kv", "o", "qkv", "h1", "dh"]
    held = dict(zip(names, take(len(names))))
    dz, do, da, enc_mask, self_mask, cross_mask, gains, own_scales = take(8)
    wide_ring, deep_ring, wide_out, deep_out = take(4)
    place = Place()
    place.barrier()
    each = scales.shape[1]
    spots = lax.broadcasted_iota(jnp.int32, (each, D), 1) - lax.broadcasted_iota(jnp.int32, (each, D), 0)
    spots = jnp.where(spots == (place.w * 4 + place.n) * each, 1.0, 0.0).astype(bf16)
    own_scales[0] = dot(scales[...], spots).astype(bf16)
    parts.append(own_scales)

    gathers = [
        Gather(place, parts[m], wholes[m], pl.ds(start, size), z_first, (send, recv), k * Gather.SEMS, local.at[k])
        for k, (m, start, size, z_first) in enumerate(pieces)
    ]

    def moved(name, out):
        buffer = held[HELD[name] if out else KEPT[name]]
        there = away[name]
        here = buffer.at[pl.ds(0, there.shape[0])]
        sem = (away_sem if out else come_sem).at[list(KEPT).index(name)]
        return pltpu.make_async_copy(*((here, there) if out else (there, here)), sem)

    lengths = {"enc": enc_lengths, "dec": dec_lengths}
    shared = dict(
        e_x0=e_x0, d_x0=d_x0, e_cot=e_cot, d_cot=d_cot, gains=gains, e_grad=e_grad, d_grad=d_grad,
        enc_out=enc_out, dec_out=dec_out, enc_mask=enc_mask, self_mask=self_mask, cross_mask=cross_mask,
    )
    forward = Forward(dict(shared, gates=da), held, lengths, lambda name: moved(name, True))
    backward = Backward(
        dict(shared, **held, dz=dz, do=do, da=da), lengths,
        lambda name: moved(name, False).wait() if name in KEPT else None,
        lambda name: moved(name, False).start(),
    )
    tall = [w.shape[4] > 3 for w in wholes]

    def staged(k):
        m, start, size, _ = pieces[k]
        if m == count:
            into = wide_ring.at[k % 2, ..., pl.ds(0, 1), :, pl.ds(0, D)]
        else:
            into = (deep_ring.at[2] if tall[m] else wide_ring.at[k % 2]).at[..., pl.ds(0, size)]
        return pltpu.make_async_copy(wholes[m].at[..., pl.ds(start, size)], into, stage_sem.at[k]), into

    deep = [k for k, (m, *_) in enumerate(back_pieces) if tall[m]]

    def ring(k):
        _, _, size, _ = back_pieces[k]
        if k in deep:
            return deep_ring.at[deep.index(k) % 2, ..., pl.ds(0, size)]
        return wide_ring.at[k % RING, ..., pl.ds(0, size)]

    def weight(k):
        m, start, size, _ = back_pieces[k]
        return pltpu.make_async_copy(wholes[m].at[..., pl.ds(start, size)], ring(k), ring_sem.at[k])

    scatters = []
    for k, (m, start, size, z_first) in enumerate(back_pieces):
        total, lasts, zs, firsts = take(4)
        final = deep_out.at[deep.index(k) % 2] if k in deep else wide_out.at[k % 3]
        final = final.at[:, :, pl.ds(0, size)]
        leave = pltpu.make_async_copy(final, outs[m].at[:, :, pl.ds(start, size)], out_sem.at[k])
        scatters.append(
            Scatter(
                place, ring(k), z_first, final, leave, total, lasts, zs, firsts, (back_send, back_recv), k * Scatter.SEMS
            )
        )

    def gather_slot(slot):
        last = STRIDE * (Gather.PHASES - 1)
        for k in range(len(gathers)):
            if (slot - k) % STRIDE == 0 and 0 <= slot - k <= last:
                gathers[k].phase((slot - k) // STRIDE)
        if slot == 0:
            fill_masks(enc_lengths, dec_lengths, enc_mask, self_mask, cross_mask)
        k = slot - last - 1
        if 0 <= k < len(gathers):
            copy, stage = staged(k)
            copy.wait()
            m, start, size, _ = pieces[k]
            if m == count:
                gains[...] = jnp.sum(stage[...].reshape(-1, 8, D).astype(f32), axis=0)
            else:
                forward.step(m, start, size, stage[...].reshape(-1, size))
            if m == 10:
                backward.back(m, pl.ds(start, size), stage, start == 0)
            if k == len(gathers) - 1:
                forward.close()
                backward.after(10)
        if 0 <= slot - last < len(gathers):
            staged(slot - last)[0].start()

    def scatter_slot(slot):
        last_slot = STRIDE * (Scatter.PHASES - 1)
        for k in range(len(scatters)):
            if (slot - k) % STRIDE == 0 and STRIDE <= slot - k <= last_slot:
                scatters[k].phase((slot - k) // STRIDE)
        k = slot
        if k >= len(scatters):
            return
        if 0 < k < len(scatters) - 1:
            weight(k + 1).start()
        m, start, size, _ = back_pieces[k]
        first = k == 0 or back_pieces[k - 1][0] != m
        last = k == len(scatters) - 1 or back_pieces[k + 1][0] != m
        columns = pl.ds(start, size)
        if first:
            backward.before(m)
        left, right = backward.factors(m)
        part = ring(k)
        if m != 10:
            weight(k).wait()
            backward.back(m, columns, part, first)
        cut = Z if k in deep else 2
        height = left.shape[1] // cut
        grad_columns = right[:, columns]
        for j in range(cut):
            grad = dot(left[:, j * height : (j + 1) * height], grad_columns, TN)
            layers = part.at[pl.ds(j * (Z // cut), Z // cut)]
            layers[...] = grad.reshape(layers.shape).astype(bf16)
        scatters[k].phase(0)
        if last and m != 10:
            backward.after(m)

    start = min(k for k, (m, *_) in enumerate(pieces) if m == 10) + STRIDE * (Gather.PHASES - 1)
    gather_slots = len(gathers) + STRIDE * (Gather.PHASES - 1) + 1
    scatter_slots = len(scatters) + STRIDE * (Scatter.PHASES - 1)
    for slot in range(max(gather_slots, start + scatter_slots)):
        if slot < gather_slots:
            gather_slot(slot)
        if 0 <= slot - start < scatter_slots:
            scatter_slot(slot - start)


def whole_step(shards, scales, enc_input, dec_input, enc_cot, dec_cot, enc_lengths, dec_lengths):
    count = len(shards)
    parts = [s.reshape(s.shape[0] // 8, 8, s.shape[1]) for s in shards]
    shapes = [p.shape for p in parts] + [(1, 8, D)]
    pieces = PIECES
    tail = [p for p in pieces if p[0] == 10]
    back_pieces = tuple(tail) + tuple(p for p in pieces[:0:-1] if p[0] != 10)
    rows, short = enc_input.shape[0], dec_input.shape[0]
    hbm, vmem = pl.BlockSpec(memory_space=pl.ANY), pl.BlockSpec(memory_space=pltpu.VMEM)
    smem = pl.BlockSpec(memory_space=pltpu.SMEM)
    wide = max(size for m, _, size, _ in back_pieces if shapes[m][0] == 3)
    deep = max((shapes[m][0], size) for m, _, size, _ in back_pieces)
    buffers = dict(
        a=(rows, FF, bf16), u=(rows, 2 * FF, bf16), h2=(rows, D, bf16), x=(rows, D, f32), q=(short, D, bf16),
        kv=(rows, 2 * D, bf16), o=(rows, D, bf16), qkv=(rows, 3 * D, bf16), h1=(rows, D, bf16), dh=(rows, D, f32),
    )
    dma = pltpu.SemaphoreType.DMA
    scratch = [
        dma((len(pieces) * Gather.SEMS,)), dma((len(pieces) * Gather.SEMS,)), dma((len(pieces),)),
        dma((len(back_pieces) * Scatter.SEMS,)), dma((len(back_pieces) * Scatter.SEMS,)),
        dma((len(pieces),)), dma((len(back_pieces),)), dma((len(back_pieces),)), dma((len(KEPT),)), dma((len(KEPT),)),
    ]
    scratch += [pltpu.VMEM((tall, across), dtype) for tall, across, dtype in buffers.values()]
    scratch += [
        pltpu.VMEM((rows, D), bf16),
        pltpu.VMEM((rows, D), bf16),
        pltpu.VMEM((rows, FF), f32),
        pltpu.VMEM((rows, rows), f32),
        pltpu.VMEM((short, short), f32),
        pltpu.VMEM((short, rows), f32),
        pltpu.VMEM((8, D), f32),
        pltpu.VMEM((1, 8, D), bf16),
        pltpu.VMEM((RING, Z, 2, 2, 2, 3, 8, wide), bf16),
        pltpu.VMEM((3, Z, 2, 2, 2, deep[0], 8, deep[1]), bf16),
        pltpu.VMEM((3, 3, 8, wide), f32),
        pltpu.VMEM((2, deep[0], 8, deep[1]), f32),
    ]
    for m, _, size, z_first in back_pieces:
        block = (shapes[m][0], 8, size)
        scratch += [
            pltpu.VMEM((Z, 2, 2, *block), bf16),
            pltpu.VMEM((Z, 2, *block), bf16),
            pltpu.VMEM((5, *(() if z_first else (2,)), *block), bf16),
            pltpu.VMEM((*((Z,) if z_first else ()), *block), bf16),
        ]
    kept = [(short if name[0] == "d" else rows, *buffers[HELD[name]][1:]) for name in KEPT]
    outs = pl.pallas_call(
        functools.partial(whole_body, pieces, back_pieces, count),
        out_shape=[jax.ShapeDtypeStruct(p.shape, f32) for p in parts]
        + [
            jax.ShapeDtypeStruct((rows, D), f32),
            jax.ShapeDtypeStruct((short, D), f32),
            jax.ShapeDtypeStruct((rows, D), bf16),
            jax.ShapeDtypeStruct((short, D), bf16),
        ]
        + [jax.ShapeDtypeStruct((Z, 2, 2, 2, *shape), bf16) for shape in shapes]
        + [jax.ShapeDtypeStruct((tall, across), dtype) for tall, across, dtype in kept],
        in_specs=[hbm] * count + [vmem] * 5 + [smem] * 2,
        out_specs=[hbm] * count + [vmem] * 4 + [hbm] * (count + 1 + len(KEPT)),
        scratch_shapes=scratch,
        compiler_params=pltpu.CompilerParams(
            collective_id=0, has_side_effects=True, vmem_limit_bytes=VMEM_LIMIT
        ),
    )(*parts, scales, enc_input, dec_input, enc_cot, dec_cot, enc_lengths, dec_lengths)
    e_grad, d_grad, enc_out, dec_out = outs[count : count + 4]
    return outs[:count], (enc_out, dec_out, e_grad, d_grad)


VMEM_LIMIT = 62 * 2**20


def finish_body(count, scaled, *refs):
    refs = list(refs)

    def take(n):
        got = refs[:n]
        del refs[:n]
        return got

    totals, shards, (scales,), passed = take(count), take(len(scaled)), take(1), take(4)
    grads, scale_grads, through = take(count), take(len(scaled)), take(4)
    for total, grad in zip(totals, grads):
        grad[...] = total[...].reshape(grad.shape)
    for k, (m, shard, out) in enumerate(zip(scaled, shards, scale_grads)):
        product = grads[m][...] * shard[...].astype(f32)
        summed = lax.dot_general(
            jnp.ones((8, product.shape[1]), f32), product, NT,
            precision=lax.Precision.HIGHEST, preferred_element_type=f32,
        )
        out[...] = summed[0:1] / scales[k : k + 1].astype(f32)
    for src, out in zip(passed, through):
        out[...] = src[...]


def finish(totals, shards, scales, passed):
    scaled = [m for m, k in enumerate(SCALE_OF) if k is not None]
    vmem = pl.BlockSpec(memory_space=pltpu.VMEM)
    count = len(totals)
    outs = pl.pallas_call(
        functools.partial(finish_body, count, scaled),
        out_shape=[jax.ShapeDtypeStruct(s.shape, f32) for s in shards]
        + [jax.ShapeDtypeStruct((1, scales.shape[1]), f32)] * len(scaled)
        + [jax.ShapeDtypeStruct(p.shape, p.dtype) for p in passed],
        in_specs=[vmem] * (count + len(scaled) + 5),
        out_specs=[vmem] * (count + len(scaled) + 4),
        compiler_params=pltpu.CompilerParams(vmem_limit_bytes=VMEM_LIMIT),
    )(*totals, *[shards[m] for m in scaled], scales, *passed)
    return outs[:count], [g.reshape(-1) for g in outs[count:-4]], outs[-4:]


def norm_rows(values, scales):
    return values * lax.rsqrt(jnp.mean(values * values, axis=-1, keepdims=True) + epsilon) * scales


def norm_back(inputs, scales, grad):
    return jax.vjp(lambda v: norm_rows(v, scales), inputs)[1](grad)[0]


def gated_units(united):
    halfway = united.shape[-1] // 2
    return jax.nn.gelu(united[:, :halfway], approximate=True) * united[:, halfway:]


def row_items(lengths, row_count):
    places = jnp.arange(row_count, dtype=jnp.int32)
    count = lengths.shape[0]
    item, boundary = jnp.zeros((row_count,), jnp.int32), jnp.int32(0)
    for k in range(count):
        boundary = boundary + lengths[k]
        item = item + (places >= boundary).astype(jnp.int32)
    return item


def head_split(matrix):
    return matrix.reshape(matrix.shape[0], HEADS, HEAD_DIM)


def outer_rows(left, right):
    return jnp.einsum("rd,re->de", left, right, preferred_element_type=jnp.float32).astype(jnp.bfloat16)


def back_rows(incoming, matrix):
    return jnp.einsum("re,de->rd", incoming, matrix, preferred_element_type=jnp.float32)


def score_rows(query_heads, key_heads, allowed):
    raw_scores = jnp.einsum(
        "qhd,khd->hqk", query_heads, key_heads, preferred_element_type=jnp.float32
    )
    return jnp.where(allowed[None], raw_scores * HEAD_DIM ** (-0.5), masked_value)


def attend_forward(queries, keys_in, values_in, allowed):
    scores = score_rows(head_split(queries), head_split(keys_in), allowed)
    largest = jnp.max(scores, axis=2, keepdims=True)
    expanded = jnp.exp(scores - largest)
    totals = jnp.sum(expanded, axis=2, keepdims=True)
    weights = (expanded / totals).astype(jnp.bfloat16)
    mixed = jnp.einsum(
        "hqk,khd->qhd", weights, head_split(values_in), preferred_element_type=jnp.float32
    )
    return (mixed.reshape(queries.shape[0], D), largest + jnp.log(totals))


def attend_backward(queries, keys_in, values_in, allowed, log_totals, grad_mixed):
    query_heads = head_split(queries)
    key_heads = head_split(keys_in)
    value_heads = head_split(values_in)
    probs = jnp.exp(score_rows(query_heads, key_heads, allowed) - log_totals)
    grad_heads = head_split(grad_mixed)
    grad_values = jnp.einsum(
        "hqk,qhd->khd", probs.astype(jnp.bfloat16), grad_heads, preferred_element_type=jnp.float32
    )
    grad_probs = jnp.einsum(
        "qhd,khd->hqk", grad_heads, value_heads, preferred_element_type=jnp.float32
    )
    centred = grad_probs - jnp.sum(probs * grad_probs, axis=2, keepdims=True)
    grad_scores = (probs * centred * HEAD_DIM ** (-0.5)).astype(jnp.bfloat16)
    grad_queries = jnp.einsum(
        "hqk,khd->qhd", grad_scores, key_heads, preferred_element_type=jnp.float32
    )
    grad_keys = jnp.einsum(
        "hqk,qhd->khd", grad_scores, query_heads, preferred_element_type=jnp.float32
    )
    return (
        grad_queries.reshape(queries.shape[0], D),
        grad_keys.reshape(keys_in.shape[0], D),
        grad_values.reshape(keys_in.shape[0], D),
    )


def self_forward(inputs, params, allowed, live_rows):
    scales, joined, outward = params
    normed = norm_rows(inputs, scales).astype(jnp.bfloat16)
    projected = jnp.dot(normed, joined, preferred_element_type=jnp.float32).astype(jnp.bfloat16)
    mixed, log_totals = attend_forward(
        projected[:, :D], projected[:, D : 2 * D], projected[:, 2 * D :], allowed
    )
    mixed_low = mixed.astype(jnp.bfloat16)
    branch = jnp.dot(mixed_low, outward, preferred_element_type=jnp.float32)
    return (inputs + live_rows[:, None] * branch, (normed, projected, mixed_low, log_totals))


def self_backward(inputs, params, allowed, live_rows, stored, incoming):
    scales, joined, outward = params
    normed, projected, mixed_low, log_totals = stored
    grad_branch = (live_rows[:, None] * incoming).astype(jnp.bfloat16)
    grad_outward = outer_rows(mixed_low, grad_branch)
    grad_mixed = back_rows(grad_branch, outward).astype(jnp.bfloat16)
    grad_parts = attend_backward(
        projected[:, :D],
        projected[:, D : 2 * D],
        projected[:, 2 * D :],
        allowed,
        log_totals,
        grad_mixed,
    )
    grad_projected = jnp.concatenate(grad_parts, axis=1).astype(jnp.bfloat16)
    grad_joined = outer_rows(normed, grad_projected)
    grad_inputs = norm_back(inputs, scales, back_rows(grad_projected, joined))
    return (incoming + grad_inputs, (grad_joined, grad_outward))


def cross_forward(inputs, memory, params, allowed, live_rows):
    scales, memory_scales, query_map, pair_map, outward = params
    normed = norm_rows(inputs, scales).astype(jnp.bfloat16)
    memory_normed = norm_rows(memory, memory_scales).astype(jnp.bfloat16)
    queries = jnp.dot(normed, query_map, preferred_element_type=jnp.float32).astype(jnp.bfloat16)
    pairs = jnp.dot(memory_normed, pair_map, preferred_element_type=jnp.float32).astype(
        jnp.bfloat16
    )
    mixed, log_totals = attend_forward(queries, pairs[:, :D], pairs[:, D:], allowed)
    mixed_low = mixed.astype(jnp.bfloat16)
    branch = jnp.dot(mixed_low, outward, preferred_element_type=jnp.float32)
    return (
        inputs + live_rows[:, None] * branch,
        (normed, memory_normed, queries, pairs, mixed_low, log_totals),
    )


def cross_backward(inputs, memory, params, allowed, live_rows, stored, incoming):
    scales, memory_scales, query_map, pair_map, outward = params
    normed, memory_normed, queries, pairs, mixed_low, log_totals = stored
    grad_branch = (live_rows[:, None] * incoming).astype(jnp.bfloat16)
    grad_outward = outer_rows(mixed_low, grad_branch)
    grad_mixed = back_rows(grad_branch, outward).astype(jnp.bfloat16)
    grad_queries, grad_keys, grad_values = attend_backward(
        queries, pairs[:, :D], pairs[:, D:], allowed, log_totals, grad_mixed
    )
    grad_queries_low = grad_queries.astype(jnp.bfloat16)
    grad_pairs = jnp.concatenate([grad_keys, grad_values], axis=1).astype(jnp.bfloat16)
    grad_query_map = outer_rows(normed, grad_queries_low)
    grad_pair_map = outer_rows(memory_normed, grad_pairs)
    grad_inputs = norm_back(inputs, scales, back_rows(grad_queries_low, query_map))
    grad_memory = norm_back(memory, memory_scales, back_rows(grad_pairs, pair_map))
    return (
        incoming + grad_inputs,
        grad_memory,
        (grad_query_map, grad_pair_map, grad_outward),
    )


def mlp_forward(inputs, params, live_rows):
    scales, inward, outward = params
    normed = norm_rows(inputs, scales).astype(jnp.bfloat16)
    united = jnp.dot(normed, inward, preferred_element_type=jnp.float32)
    activated = gated_units(united).astype(jnp.bfloat16)
    branch = jnp.dot(activated, outward, preferred_element_type=jnp.float32)
    return (inputs + live_rows[:, None] * branch, (normed, united, activated))


def mlp_backward(inputs, params, live_rows, stored, incoming):
    scales, inward, outward = params
    normed, united, activated = stored
    grad_branch = (live_rows[:, None] * incoming).astype(jnp.bfloat16)
    grad_outward = outer_rows(activated, grad_branch)
    grad_activated = back_rows(grad_branch, outward)
    _, pullback = jax.vjp(gated_units, united)
    grad_united = pullback(grad_activated)[0].astype(jnp.bfloat16)
    grad_inward = outer_rows(normed, grad_united)
    grad_inputs = norm_back(inputs, scales, back_rows(grad_united, inward))
    return (incoming + grad_inputs, (grad_inward, grad_outward))


def plain_gather(shards):
    return [lax.all_gather(s, AXES, axis=0, tiled=True) for s in shards]


def plain_scatter(sums):
    return [lax.psum_scatter(s.astype(jnp.float32), AXES, scatter_dimension=0, tiled=True) for s in sums]


SCALE_OF = (0, None, 1, None, 2, None, 3, 4, None, 5, None)


def per_device(
    linked,
    enc_input,
    dec_input,
    enc_lengths,
    dec_lengths,
    enc_attn_gain,
    enc_qkv,
    enc_attn_out,
    enc_mlp_gain,
    enc_mlp_in,
    enc_mlp_out,
    dec_self_gain,
    dec_qkv,
    dec_self_out,
    cross_gain,
    memory_gain,
    cross_query,
    cross_kv,
    cross_out,
    dec_mlp_gain,
    dec_mlp_in,
    dec_mlp_out,
    enc_cotangent,
    dec_cotangent,
):
    gains = [enc_attn_gain, enc_mlp_gain, dec_self_gain, cross_gain, memory_gain, dec_mlp_gain]
    shards = (
        enc_qkv, enc_attn_out, enc_mlp_in, enc_mlp_out, dec_qkv, dec_self_out,
        cross_query, cross_kv, cross_out, dec_mlp_in, dec_mlp_out,
    )
    if linked:
        stacked = jnp.stack(gains + [jnp.zeros_like(gains[0])] * (8 - len(gains)))
        summed, passed = whole_step(
            shards, stacked, enc_input, dec_input, enc_cotangent, dec_cotangent, enc_lengths, dec_lengths
        )
        grads, scale_grads, (enc_out, dec_out, grad_encoder_start, grad_decoder_start) = finish(
            summed, shards, stacked, passed
        )
    else:
        item_count = enc_lengths.shape[0]
        enc_items = row_items(enc_lengths, enc_input.shape[0])
        dec_items = row_items(dec_lengths, dec_input.shape[0])
        enc_live = (enc_items < item_count).astype(jnp.float32)
        dec_live = (dec_items < item_count).astype(jnp.float32)
        enc_padded = enc_items[:, None] == item_count
        dec_padded = dec_items[:, None] == item_count
        enc_allowed = (enc_items[:, None] == enc_items[None, :]) | enc_padded
        dec_places = jnp.arange(dec_input.shape[0], dtype=jnp.int32)
        self_allowed = (dec_items[:, None] == dec_items[None, :]) & (
            dec_places[None, :] <= dec_places[:, None]
        ) | dec_padded
        cross_allowed = (dec_items[:, None] == enc_items[None, :]) | dec_padded
        whole = plain_gather(shards)
        own = [g.astype(jnp.float32) for g in gains]
        gains = plain_gather(own)
        encoder_start = enc_input.astype(jnp.float32)
        decoder_start = dec_input.astype(jnp.float32)
        enc_middle, enc_attn_store = self_forward(encoder_start, (gains[0], *whole[0:2]), enc_allowed, enc_live)
        encoder_final, enc_mlp_store = mlp_forward(enc_middle, (gains[1], *whole[2:4]), enc_live)
        dec_middle, dec_self_store = self_forward(decoder_start, (gains[2], *whole[4:6]), self_allowed, dec_live)
        dec_crossed, cross_store = cross_forward(
            dec_middle, encoder_final, (gains[3], gains[4], *whole[6:9]), cross_allowed, dec_live
        )
        decoder_final, dec_mlp_store = mlp_forward(dec_crossed, (gains[5], *whole[9:11]), dec_live)
        enc_out, dec_out = encoder_final.astype(jnp.bfloat16), decoder_final.astype(jnp.bfloat16)
        grad_crossed, dec_mlp_grads = mlp_backward(
            dec_crossed, (gains[5], *whole[9:11]), dec_live, dec_mlp_store, dec_cotangent.astype(jnp.float32)
        )
        grad_middle, grad_memory, cross_grads = cross_backward(
            dec_middle,
            encoder_final,
            (gains[3], gains[4], *whole[6:9]),
            cross_allowed,
            dec_live,
            cross_store,
            grad_crossed,
        )
        grad_decoder_start, dec_self_grads = self_backward(
            decoder_start, (gains[2], *whole[4:6]), self_allowed, dec_live, dec_self_store, grad_middle
        )
        grad_enc_middle, enc_mlp_grads = mlp_backward(
            enc_middle,
            (gains[1], *whole[2:4]),
            enc_live,
            enc_mlp_store,
            enc_cotangent.astype(jnp.float32) + grad_memory,
        )
        grad_encoder_start, enc_attn_grads = self_backward(
            encoder_start, (gains[0], *whole[0:2]), enc_allowed, enc_live, enc_attn_store, grad_enc_middle
        )
        sums = enc_attn_grads + enc_mlp_grads + dec_self_grads + cross_grads + dec_mlp_grads
        summed = plain_scatter(sums)
        grads, scale_grads = [], {}
        for total, shard, k in zip(summed, shards, SCALE_OF):
            if k is not None:
                scale_grads[k] = jnp.sum(total * shard.astype(jnp.float32), axis=1) / own[k]
            grads.append(total)
    return (
        enc_out,
        dec_out,
        grad_encoder_start,
        grad_decoder_start,
        scale_grads[0], grads[0], grads[1],
        scale_grads[1], grads[2], grads[3],
        scale_grads[2], grads[4], grads[5],
        scale_grads[3], scale_grads[4], grads[6], grads[7], grads[8],
        scale_grads[5], grads[9], grads[10],
    )


def solution(mesh):
    rows, line = P(AXES, None), P(AXES)
    linked = mesh.shape["wide"] == 2 * Z and mesh.shape["narrow"] == 4
    weights = (
        line, rows, rows, line, rows, rows, line, rows, rows,
        line, line, rows, rows, rows, line, rows, rows,
    )
    return jax.shard_map(
        functools.partial(per_device, linked),
        mesh=mesh,
        in_specs=(rows, rows, line, line, *weights, rows, rows),
        out_specs=(rows, rows, rows, rows, *weights),
        check_vma=False,
    )
```

```python
import functools

import jax
import jax.numpy as jnp
from jax import lax
from jax.experimental import pallas as pl
from jax.experimental.pallas import tpu as pltpu
from jax.sharding import PartitionSpec as P

D = 768
HEADS = 12
HEAD_DIM = 64
FF = 2048
AXES = ("wide", "narrow")
MESH = pl.DeviceIdType.MESH

Z = 4
PIECES = (
    (11, 0, 768, False, False),
    (0, 0, 1152, True, True),
    (0, 1152, 1152, False, True),
    (1, 0, 768, True, False),
    (2, 0, 1024, False, True),
    (2, 1024, 1024, False, False),
    (2, 2048, 1024, True, False),
    (2, 3072, 1024, False, True),
    (3, 0, 384, False, False),
    (3, 384, 384, True, True),
    (4, 0, 1152, False, False),
    (4, 1152, 1152, False, False),
    (5, 0, 768, True, False),
    (6, 0, 768, False, False),
    (7, 0, 768, False, False),
    (7, 768, 768, True, False),
    (8, 0, 768, False, True),
    (9, 0, 1024, False, True),
    (9, 1024, 1024, False, False),
    (9, 2048, 1024, True, False),
    (9, 3072, 1024, False, False),
    (10, 0, 384, False, False),
    (10, 384, 384, False, False),
)
STRIDE = 2


class Place:
    def __init__(self):
        self.w, self.n = lax.axis_index("wide"), lax.axis_index("narrow")
        self.z, self.y = self.w // 2, self.w % 2
        self.x, self.c = self.n // 2, self.n % 2
        w, n, y, x, c = self.w, self.n, self.y, self.x, self.c
        self.sibling = (w, n + 1 - 2 * c)
        self.first = (w + (1 - c) * (1 - 2 * y), n + c * (2 - 4 * x))
        self.last = (w + c * (1 - 2 * y), n + (1 - c) * (2 - 4 * x))
        self.above = (w + 2, n)
        self.below = (w - 2, n)

    def barrier(self):
        sem = pltpu.get_barrier_semaphore()
        for device in (self.sibling, self.first, self.last):
            pl.semaphore_signal(sem, inc=1, device_id=device, device_id_type=MESH)

        @pl.when(self.z < Z - 1)
        def _():
            pl.semaphore_signal(sem, inc=1, device_id=self.above, device_id_type=MESH)

        @pl.when(self.z > 0)
        def _():
            pl.semaphore_signal(sem, inc=1, device_id=self.below, device_id_type=MESH)

        inner = jnp.where(self.z * (Z - 1 - self.z) > 0, 1, 0)
        pl.semaphore_wait(sem, 4 + inner)

    def by_core(self, do):
        @pl.when(self.c == 0)
        def _():
            do(0)

        @pl.when(self.c == 1)
        def _():
            do(1)


def remote(src, dst, sems, index, device):
    send, recv = sems
    return pltpu.make_async_remote_copy(
        src_ref=src, dst_ref=dst, send_sem=send.at[index], recv_sem=recv.at[index],
        device_id=device, device_id_type=MESH,
    )


class Gather:
    PHASES = 7
    SEMS = 13

    def __init__(self, place, part, whole, columns, z_first, sems, base, local_sem):
        self.p, self.z_first, self.sems, self.base = place, z_first, sems, base
        self.part = part.at[:, :, columns]
        self.whole = whole.at[:, :, :, :, :, :, columns]
        self.local = pltpu.make_async_copy(self.part, self.own(), local_sem)

    def own(self):
        p = self.p
        return self.whole.at[p.z, p.y, p.x, p.c]

    def copy(self, src, dst, slot, device):
        return remote(src, dst, self.sems, self.base + slot, device)

    def layer(self, zz, core):
        p = self.p
        if self.z_first:
            return self.whole.at[zz, p.y, p.x, core]
        return self.whole.at[zz, :, p.x, 0] if core == 0 else self.whole.at[zz, p.y, :, 1]

    def half(self, core, mine):
        p = self.p
        if core == 0:
            return self.whole.at[:, :, p.x if mine else 1 - p.x, 0]
        return self.whole.at[:, p.y if mine else 1 - p.y, :, 1]

    def along_z(self, step, sending):
        p = self.p

        def go(core):
            for up in (True, False):
                if sending:
                    zz = p.z - step if up else p.z + step
                    there = (p.z < Z - 1) & (zz >= 0) if up else (p.z > 0) & (zz < Z)
                else:
                    zz = p.z - 1 - step if up else p.z + 1 + step
                    there = zz >= 0 if up else zz < Z

                target = (p.above if up else p.below) if sending else p.last

                @pl.when(there)
                def _():
                    block = self.layer(zz, core)
                    copy = self.copy(block, block, 1 + step * 2 + up, target)
                    copy.start() if sending else copy.wait_recv()

        p.by_core(go)

    def along_z_sent(self):
        p = self.p

        def go(core):
            for step in range(3):
                for up in (True, False):
                    zz = p.z - step if up else p.z + step
                    there = (p.z < Z - 1) & (zz >= 0) if up else (p.z > 0) & (zz < Z)

                    @pl.when(there)
                    def _():
                        block = self.layer(zz, core)
                        self.copy(block, block, 1 + step * 2 + up, p.last).wait_send()

        p.by_core(go)

    def first(self, core):
        p = self.p
        if not self.z_first:
            return self.copy(self.part, self.own(), 0, p.first)
        block = self.whole.at[:, p.y, p.x, core]
        return self.copy(block, block, 0, p.first)

    def last(self, core):
        block = self.half(core, True)
        return self.copy(block, block, 7, self.p.last)

    def last_layer(self, zz, core, mine=True):
        p = self.p
        if core == 0:
            block = self.whole.at[zz, :, p.x if mine else 1 - p.x, 0]
        else:
            block = self.whole.at[zz, p.y if mine else 1 - p.y, :, 1]
        return self.copy(block, block, 7 + zz, p.last)

    def far_layers(self, far, core, verb):
        z = self.p.z
        if far == 0:
            getattr(self.last_layer(z, core), verb)()
            return

        @pl.when(z + far < Z)
        def _():
            getattr(self.last_layer(z + far, core), verb)()

        @pl.when(z - far >= 0)
        def _():
            getattr(self.last_layer(z - far, core), verb)()

    def send_far(self, far):
        self.p.by_core(lambda core: self.far_layers(far, core, "start"))

    def wait_last(self, core, verb):
        if self.z_first:
            getattr(self.last(core), verb)()
        else:
            for zz in range(Z):
                getattr(self.last_layer(zz, core, verb == "wait_send"), verb)()

    def across(self, core, mine):
        block = self.half(core, mine)
        return self.copy(block, block, 11 if mine else 12, self.p.sibling)

    def each(self, make, *verbs):
        def go(core):
            copy = make(core)
            for verb in verbs:
                getattr(copy, verb)()

        self.p.by_core(go)

    def phase(self, number):
        early = not self.z_first
        if number == 0:
            self.local.start()
            if early:
                self.each(self.first, "start")
            self.local.wait()
            if not early:
                self.along_z(0, True)
        elif number == 1:
            if early:
                self.each(self.first, "wait_recv")
                self.along_z(0, True)
                self.send_far(0)
            else:
                self.along_z(0, False)
                self.along_z(1, True)
        elif number == 2:
            self.along_z(0 if early else 1, False)
            self.along_z(1 if early else 2, True)
            if early:
                self.send_far(1)
        elif number == 3:
            self.along_z(1 if early else 2, False)
            if early:
                self.along_z(2, True)
                self.send_far(2)
            else:
                self.each(self.first, "start")
        elif number == 4:
            if early:
                self.along_z(2, False)
                self.send_far(3)
            else:
                self.each(self.first, "wait_recv")
                self.each(self.last, "start")
            self.each(lambda core: self.across(core, True), "start")
        elif number == 5:
            self.p.by_core(lambda core: self.wait_last(core, "wait_recv"))
            self.each(lambda core: self.across(core, False), "start")
        else:
            for core in (0, 1):
                @pl.when(self.p.c == core)
                def _():
                    for mine in (True, False):
                        self.across(1 - core, mine).wait_recv()
                        self.across(core, mine).wait_send()
                    self.first(core).wait_send()
                    self.wait_last(core, "wait_send")
            self.along_z_sent()


class Scatter:
    PHASES = 8
    SEMS = 12

    def __init__(self, place, parts, z_first, out, leave, total, lasts, zs, firsts, sems, base):
        self.p, self.z_first, self.sems, self.base = place, z_first, sems, base
        self.parts, self.out, self.leave = parts, out, leave
        self.total, self.lasts, self.zs, self.firsts = total, lasts, zs, firsts

    def copy(self, src, dst, slot, device):
        return remote(src, dst, self.sems, self.base + slot, device)

    def spot(self, core, last, first=None):
        every = slice(None)
        if first is None:
            return (every, last) if core else (every, every, last)
        return (last, first) if core else (first, last)

    def place_of(self, core):
        p = self.p
        return (p.y, p.x) if core else (p.x, p.y)

    def across(self, core):
        return self.copy(self.parts.at[:, :, :, 1 - core], self.total, 0, self.p.sibling)

    def last(self, core):
        last, _ = self.place_of(core)
        return self.copy(self.total.at[self.spot(core, 1 - last)], self.lasts, 8, self.p.last)

    def last_layer(self, zz, core):
        last, _ = self.place_of(core)
        src = self.total.at[(zz, *self.spot(core, 1 - last)[1:])]
        return self.copy(src, self.lasts.at[zz], 8 + zz, self.p.last)

    def far_layers(self, far, do):
        z = self.p.z
        if far == 0:
            do(z)
            return

        @pl.when(z + far < Z)
        def _():
            do(z + far)

        @pl.when(z - far >= 0)
        def _():
            do(z - far)

    def send_layers(self, core):
        for far in (3, 2, 1, 0):
            self.far_layers(far, lambda zz: self.last_layer(zz, core).start())

    def add_layers(self, far):
        def one(zz):
            self.p.by_core(lambda core: self.last_layer(zz, core).wait_recv())
            for k in range(2):
                self.total[(zz, *self.pair(k))] += self.lasts[zz, k]

        self.far_layers(far, one)

    def last_sent(self, core):
        if self.z_first:
            self.last(core).wait_send()
        else:
            for zz in range(Z):
                self.last_layer(zz, core).wait_send()

    def first(self, core):
        p = self.p
        last, first = self.place_of(core)
        if self.z_first:
            src = self.total.at[(slice(None), *self.spot(core, last, 1 - first))]
        else:
            src = self.total.at[(p.z, *self.spot(core, last, 1 - first))]
        return self.copy(src, self.firsts, 1, p.first)

    def layer(self, zz, core):
        last, first = self.place_of(core)
        if self.z_first:
            return self.total.at[(zz, *self.spot(core, last, first))]
        return self.total.at[(zz, *self.spot(core, last)[1:])]

    def way(self, step, up, sending):
        z, far = self.p.z, 2 - step
        if sending:
            zz = z + 1 + far if up else z - 1 - far
            return zz, zz < Z if up else zz >= 0
        zz = z + far if up else z - far
        return zz, (z > 0) & (zz < Z) if up else (z < Z - 1) & (zz >= 0)

    def landing(self, step, up):
        return 0 if step == 0 else 2 * step - 1 + up

    def along_z(self, step, verb):
        p = self.p

        def go(core):
            for up in (True, False):
                zz, there = self.way(step, up, verb != "wait_recv")
                target = (p.above if up else p.below) if verb == "start" else p.last

                @pl.when(there)
                def _():
                    copy = self.copy(self.layer(zz, core), self.zs.at[self.landing(step, up)], 2 + step * 2 + up, target)
                    getattr(copy, verb)()

        p.by_core(go)

    def add_z(self, step):
        p = self.p
        for up in (True, False):
            zz, there = self.way(step, up, False)

            @pl.when(there)
            def _():
                arrived = self.zs.at[self.landing(step, up)]
                if self.z_first:
                    self.total[zz, p.y, p.x] += arrived[...]
                else:
                    for k in range(2):
                        self.total[(zz, *self.pair(k))] += arrived[k]

    def pair(self, k):
        p = self.p
        return k * (1 - p.c) + p.y * p.c, p.x * (1 - p.c) + k * p.c

    def each(self, make, *verbs):
        def go(core):
            copy = make(core)
            for verb in verbs:
                getattr(copy, verb)()

        self.p.by_core(go)

    def phase(self, number):
        p, early = self.p, self.z_first
        if number == 0:
            self.each(self.across, "start")
        elif number == 1:
            self.each(self.across, "wait_recv")

            @pl.loop(0, 16)
            def _(i):
                self.total[i // 4, i // 2 % 2, i % 2] += self.parts[i // 4, i // 2 % 2, i % 2, p.c]

            if early:
                self.each(self.last, "start")
            else:
                p.by_core(self.send_layers)
            self.each(self.across, "wait_send")
        elif number == 2:
            if early:
                self.each(self.last, "wait_recv")

                @pl.loop(0, 8)
                def _(i):
                    self.total[(i // 2, *self.pair(i % 2))] += self.lasts[i // 2, i % 2]

                self.each(self.first, "start")
            else:
                self.add_layers(3)
                self.along_z(0, "start")
        elif number == 3:
            if early:
                self.each(self.first, "wait_recv")

                @pl.loop(0, Z)
                def _(i):
                    self.total[i, p.y, p.x] += self.firsts[i]

                self.along_z(0, "start")
            else:
                self.add_layers(2)
                self.along_z(0, "wait_recv")
                self.add_z(0)
                self.along_z(1, "start")
        elif number == 4:
            step = 0 if early else 1
            if not early:
                self.add_layers(1)
            self.along_z(step, "wait_recv")
            self.add_z(step)
            self.along_z(step + 1, "start")
        elif number == 5:
            step = 1 if early else 2
            if not early:
                self.add_layers(0)
            self.along_z(step, "wait_recv")
            self.add_z(step)
            if early:
                self.along_z(2, "start")
            else:
                self.each(self.first, "start")
        elif number == 6:
            if early:
                self.along_z(2, "wait_recv")
                self.add_z(2)
                self.out[...] = self.total[p.z, p.y, p.x].astype(jnp.float32)
            else:
                self.each(self.first, "wait_recv")
                self.out[...] = self.total[p.z, p.y, p.x].astype(jnp.float32) + self.firsts[...].astype(jnp.float32)
            self.leave.start()
        else:
            self.leave.wait()
            p.by_core(self.last_sent)
            self.each(self.first, "wait_send")
            for step in range(3):
                self.along_z(step, "wait_send")


epsilon = 1e-06
masked_value = -1000000000.0
SHRINK = HEAD_DIM**-0.5
NT = (((1,), (1,)), ((), ()))
TN = (((0,), (0,)), ((), ()))
f32, bf16 = jnp.float32, jnp.bfloat16


def dot(a, b, dims=(((1,), (0,)), ((), ()))):
    return lax.dot_general(a, b, dims, preferred_element_type=f32)


def shrunk(values):
    return lax.rsqrt(jnp.mean(values * values, axis=-1, keepdims=True) + epsilon)


def norm(values, scales):
    return values * shrunk(values) * scales


def items_of(lengths_ref, places):
    item, boundary = jnp.zeros_like(places), 0
    for k in range(lengths_ref.shape[0]):
        boundary = boundary + lengths_ref[k]
        item = item + jnp.where(places >= boundary, 1, 0)
    return item


def fill_masks(enc_lengths, dec_lengths, enc_mask, self_mask, cross_mask):
    count = enc_lengths.shape[0]

    def grid(ref, axis):
        return lax.broadcasted_iota(jnp.int32, ref.shape, axis)

    def put(ref, rows, columns, both):
        kept = rows == columns
        if both is not None:
            kept = kept & both
        ref[...] = jnp.where(kept | (rows == count), 1.0, 0.0)

    put(enc_mask, items_of(enc_lengths, grid(enc_mask, 0)), items_of(enc_lengths, grid(enc_mask, 1)), None)
    put(
        self_mask, items_of(dec_lengths, grid(self_mask, 0)), items_of(dec_lengths, grid(self_mask, 1)),
        grid(self_mask, 1) <= grid(self_mask, 0),
    )
    put(cross_mask, items_of(dec_lengths, grid(cross_mask, 0)), items_of(enc_lengths, grid(cross_mask, 1)), None)


def live_rows(lengths_ref, rows):
    item = items_of(lengths_ref, lax.broadcasted_iota(jnp.int32, (rows, 1), 0))
    return jnp.where(item < lengths_ref.shape[0], 1.0, 0.0)


def head_lanes(which):
    lanes = lax.broadcasted_iota(jnp.int32, (1, 2 * HEAD_DIM), 1)
    return jnp.where(lanes // HEAD_DIM == which, 1.0, 0.0).astype(bf16)


def head_probs(q, k, kept):
    scores = jnp.where(kept[...] > 0.0, dot(q, k, NT) * SHRINK, masked_value)
    raised = jnp.exp(scores - jnp.max(scores, axis=1, keepdims=True))
    return raised * (1.0 / jnp.sum(raised, axis=1, keepdims=True))


def pair_columns(pair, offset):
    return pl.ds(pl.multiple_of(pair * (2 * HEAD_DIM) + offset, 2 * HEAD_DIM), 2 * HEAD_DIM)


def attend(q_ref, q_at, k_ref, k_at, v_ref, v_at, kept, out_ref):
    @pl.loop(0, HEADS // 2)
    def _(pair):
        q = q_ref[:, pair_columns(pair, q_at)]
        k = k_ref[:, pair_columns(pair, k_at)]
        v = v_ref[:, pair_columns(pair, v_at)]
        mixed = None
        for which in range(2):
            lanes = head_lanes(which)
            part = dot(head_probs(q * lanes, k, kept).astype(bf16), v * lanes)
            mixed = part if mixed is None else mixed + part
        out_ref[:, pair_columns(pair, 0)] = mixed.astype(bf16)


def gelu_tanh(t):
    return jnp.tanh(0.7978845608028654 * (t + 0.044715 * (t * t * t)))


class Forward:
    def __init__(self, refs, held, lengths, store):
        self.__dict__.update(refs)
        self.held, self.lengths, self.store, self.leaving = held, lengths, store, {}

    def at(self, name):
        buffer = self.held[HELD[name]]
        return buffer.at[pl.ds(0, self.rows("dec"))] if name[0] == "d" or name in ("c_o", "hq") else buffer

    def rows(self, side):
        return self.e_x0.shape[0] if side == "enc" else self.d_x0.shape[0]

    def opened(self, name):
        copy = self.leaving.pop(HELD[name], None)
        if copy is not None:
            copy.wait()
        return self.at(name)

    def kept(self, name):
        if name in KEPT:
            copy = self.store(name)
            copy.start()
            self.leaving[HELD[name]] = copy

    def close(self):
        for copy in self.leaving.values():
            copy.wait()

    def set_norm(self, values, k, name):
        self.opened(name)[...] = norm(values, self.gains[k : k + 1]).astype(bf16)
        self.kept(name)

    def live(self, side):
        return live_rows(self.lengths[side], self.rows(side))

    def step(self, m, start, size, weight):
        columns = pl.ds(start, size)
        side, rows = ("e", "enc") if m < 4 else ("d", "dec")
        first = start == 0
        if m == 0 or m == 4:
            h1, qkv, o = side + "_h1", side + "_qkv", side + "_o"
            if first:
                before = self.e_x0 if m == 0 else self.d_x0
                self.set_norm(before[...].astype(f32), 0 if m == 0 else 2, h1)
                self.opened(qkv)
            ref = self.at(qkv)
            ref[:, columns] = dot(self.at(h1)[...], weight).astype(bf16)
            if start + size == ref.shape[1]:
                self.kept(qkv)
                attend(ref, 0, ref, D, ref, 2 * D, self.enc_mask if m == 0 else self.self_mask, self.opened(o))
                self.kept(o)
        elif m == 1 or m == 5:
            before, x1 = (self.e_x0, "e_x1") if m == 1 else (self.d_x0, "d_x1")
            after = before[...].astype(f32) + self.live(rows) * dot(self.at(side + "_o")[...], weight)
            self.opened(x1)[...] = after
            self.kept(x1)
            self.set_norm(self.at(x1)[...], 1 if m == 1 else 3, "e_h2" if m == 1 else "hq")
        elif m == 6:
            self.at("q")[...] = dot(self.at("hq")[...], weight).astype(bf16)
        elif m == 7:
            kv = self.at("kv")
            kv[:, columns] = dot(self.at("hm")[...], weight).astype(bf16)
            if start + size == kv.shape[1]:
                attend(self.at("q"), 0, kv, 0, kv, D, self.cross_mask, self.opened("c_o"))
        elif m == 8:
            after = self.live(rows) * dot(self.at("c_o")[...], weight)
            self.opened("d_x2")[...] += after
            self.set_norm(self.at("d_x2")[...], 5, "d_h2")
        elif m == 2 or m == 9:
            u, a = side + "_u", side + "_a"
            if first:
                self.opened(u)
                self.opened(a)
            united = dot(self.at(side + "_h2")[...], weight)
            self.at(u)[:, columns] = united.astype(bf16)
            if start < FF:
                self.gates[pl.ds(0, united.shape[0]), columns] = united
            else:
                back = pl.ds(start - FF, size)
                gate = self.gates[pl.ds(0, united.shape[0]), back]
                self.at(a)[:, back] = (0.5 * gate * (1.0 + gelu_tanh(gate)) * united).astype(bf16)
            if start + size == 2 * FF:
                self.kept(u)
                self.kept(a)
        else:
            if m == 3 and first:
                self.opened("e_x2")
            before = self.at("e_x1" if m == 3 else "d_x2")
            after = before[:, columns] + self.live(rows) * dot(self.at(side + "_a")[...], weight)
            out = self.enc_out if m == 3 else self.dec_out
            out[:, columns] = after.astype(bf16)
            if m == 3:
                self.at("e_x2")[:, columns] = after
                if start + size == D:
                    self.kept("e_x2")
                    self.set_norm(self.at("e_x2")[...], 4, "hm")


class Backward:
    def __init__(self, refs, lengths, load, free):
        self.__dict__.update(refs)
        self.lengths, self.load, self.free = lengths, load, free

    def rows(self, side):
        return self.e_x0.shape[0] if side == "enc" else self.d_x0.shape[0]

    def live(self, side):
        return live_rows(self.lengths[side], self.rows(side))

    def gain(self, k):
        return self.gains[k : k + 1]

    def top(self, ref, side):
        return ref.at[pl.ds(0, self.rows(side))]

    def side(self, m):
        return "enc" if m < 4 else "dec"

    def through_norm(self, values, k, grad, into):
        small = shrunk(values)
        unit = values * small
        grad = grad * self.gain(k)
        into[...] += small * (grad - unit * jnp.mean(grad * unit, axis=-1, keepdims=True))

    def set_branch(self, side):
        grad = self.e_grad if side == "enc" else self.d_grad
        self.top(self.dz, side)[...] = (self.live(side) * grad[...]).astype(bf16)

    def before(self, m):
        side = self.side(m)
        if m == 10 or m == 3:
            if m == 10:
                self.d_grad[...] = self.d_cot[...].astype(f32)
            self.set_branch(side)
            self.load("d_a" if m == 10 else "e_a")
        elif m == 9 or m == 2:
            self.load("d_u" if m == 9 else "e_u")
            self.load("d_h2" if m == 9 else "e_h2")
            u, da = self.top(self.u, side), self.top(self.da, side)

            @pl.loop(0, FF // 256)
            def _(j):
                at = pl.multiple_of(j * 256, 256)
                gate_at, up_at = pl.ds(at, 256), pl.ds(pl.multiple_of(at + FF, 256), 256)
                t, up, grad = u[:, gate_at].astype(f32), u[:, up_at].astype(f32), da[:, gate_at]
                th = gelu_tanh(t)
                slope = 0.5 * (1.0 + th) + 0.5 * t * (1.0 - th * th) * (
                    0.7978845608028654 * (1.0 + 0.134145 * (t * t))
                )
                u[:, gate_at] = (slope * up * grad).astype(bf16)
                u[:, up_at] = (0.5 * t * (1.0 + th) * grad).astype(bf16)
        elif m == 8:
            self.set_branch("dec")
            self.load("c_o")
        elif m == 7:
            for name in ("q", "kv", "hm"):
                self.load(name)
            self.attend_back(self.q, 0, self.kv, 0, self.kv, D, self.cross_mask, "dec")
        elif m == 6:
            self.load("hq")
        elif m == 5 or m == 1:
            self.set_branch(side)
            self.load("d_o" if m == 5 else "e_o")
        else:
            self.load("d_h1" if m == 4 else "e_h1")
            self.load("d_qkv" if m == 4 else "e_qkv")
            qkv = self.top(self.qkv, side)
            self.attend_back(qkv, 0, qkv, D, qkv, 2 * D, self.self_mask if m == 4 else self.enc_mask, side)

    def attend_back(self, q_ref, q_at, k_ref, k_at, v_ref, v_at, kept, side):
        grad_ref = self.top(self.do, side)

        @pl.loop(0, HEADS // 2)
        def _(pair):
            q = q_ref[:, pair_columns(pair, q_at)]
            k = k_ref[:, pair_columns(pair, k_at)]
            v = v_ref[:, pair_columns(pair, v_at)]
            grad = grad_ref[:, pair_columns(pair, 0)]
            dq = dk = dv = 0.0
            for which in range(2):
                lanes = head_lanes(which)
                q_half, grad_half = q * lanes, grad * lanes
                probs = head_probs(q_half, k, kept)
                dv = dv + dot(probs.astype(bf16), grad_half, TN)
                dp = dot(grad_half, v, NT)
                centred = dp - jnp.sum(probs * dp, axis=1, keepdims=True)
                ds = (probs * centred * SHRINK).astype(bf16)
                dq = dq + dot(ds, k * lanes)
                dk = dk + dot(ds, q_half, TN)
            q_ref[:, pair_columns(pair, q_at)] = dq.astype(bf16)
            k_ref[:, pair_columns(pair, k_at)] = dk.astype(bf16)
            v_ref[:, pair_columns(pair, v_at)] = dv.astype(bf16)

    def factors(self, m):
        side = self.side(m)
        left = {
            10: self.a, 3: self.a, 9: self.h2, 2: self.h2, 8: self.o, 7: self.h2, 6: self.h1,
            5: self.o, 1: self.o, 4: self.h1, 0: self.h1,
        }[m]
        right = {
            10: self.dz, 3: self.dz, 9: self.u, 2: self.u, 8: self.dz, 7: self.kv, 6: self.q,
            5: self.dz, 1: self.dz, 4: self.qkv, 0: self.qkv,
        }[m]
        if m != 7:
            left, right = self.top(left, side), self.top(right, side)
        return left, right

    def back(self, m, columns, weight, first):
        side = self.side(m)
        right = self.factors(m)[1][:, columns]
        if m in (10, 3):
            into = self.top(self.da, side)
            tall = FF // Z
            for j in range(Z):
                share = dot(right, weight[j].reshape(tall, -1), NT)
                if first:
                    into[:, j * tall : (j + 1) * tall] = share
                else:
                    into[:, j * tall : (j + 1) * tall] += share
            return
        share = dot(right, weight[...].reshape(D, -1), NT)
        into = self.dh if m == 7 else self.top(self.dh, side)
        if m in (8, 5, 1):
            self.top(self.do, side)[...] = share.astype(bf16)
        elif first:
            into[...] = share
        else:
            into[...] += share
    def after(self, m):
        side = self.side(m)
        into = self.dh if m == 7 else self.top(self.dh, side)
        if m == 10:
            self.free("e_a")
        elif m == 9:
            self.load("d_x2")
            self.through_norm(self.top(self.x, "dec")[...], 5, into[...], self.d_grad)
            for name in ("e_x2", "e_u", "hm"):
                self.free(name)
        elif m == 8:
            self.free("d_o")
        elif m == 7:
            self.load("e_x2")
            self.e_grad[...] = self.e_cot[...].astype(f32)
            self.through_norm(self.x[...], 4, into[...], self.e_grad)
            self.free("d_x1")
            self.free("e_h2")
        elif m == 6:
            self.load("d_x1")
            self.through_norm(self.top(self.x, "dec")[...], 3, into[...], self.d_grad)
            self.free("e_x1")
            self.free("d_h1")
        elif m == 5:
            self.free("e_o")
        elif m == 4:
            self.through_norm(self.d_x0[...].astype(f32), 2, into[...], self.d_grad)
            self.free("e_h1")
            self.free("e_qkv")
        elif m == 2:
            self.load("e_x1")
            self.through_norm(self.x[...], 1, into[...], self.e_grad)
        elif m == 0:
            self.through_norm(self.e_x0[...].astype(f32), 0, into[...], self.e_grad)


HELD = dict(
    e_a="a", d_a="a", e_u="u", d_u="u", e_h2="h2", hm="h2", d_h2="h2", e_x1="x", d_x1="x", d_x2="x", e_x2="dh",
    e_o="o", d_o="o", c_o="o", e_h1="h1", d_h1="h1", hq="h1", e_qkv="qkv", d_qkv="qkv", q="q", kv="kv",
)
KEPT = dict(
    hm="h2", d_x1="x", d_o="o", d_h1="h1", e_a="a", e_u="u", e_h2="h2", e_x2="x", e_x1="x", e_o="o", e_qkv="qkv", e_h1="h1",
)
RING = 3


def whole_body(pieces, back_pieces, count, *refs):
    refs = list(refs)

    def take(n):
        got = refs[:n]
        del refs[:n]
        return got

    parts = take(count)
    scales, e_x0, d_x0, e_cot, d_cot, enc_lengths, dec_lengths = take(7)
    outs = take(count)
    e_grad, d_grad, enc_out, dec_out = take(4)
    wholes = take(count + 1)
    away = dict(zip(KEPT, take(len(KEPT))))
    send, recv, local, back_send, back_recv, stage_sem, ring_sem, out_sem, away_sem, come_sem = take(10)
    names = ["a", "u", "h2", "x", "q", "kv", "o", "qkv", "h1", "dh"]
    held = dict(zip(names, take(len(names))))
    dz, do, da, enc_mask, self_mask, cross_mask, gains, own_scales = take(8)
    wide_ring, deep_ring, wide_out, deep_out = take(4)
    place = Place()
    place.barrier()
    each = scales.shape[1]
    spots = lax.broadcasted_iota(jnp.int32, (each, D), 1) - lax.broadcasted_iota(jnp.int32, (each, D), 0)
    spots = jnp.where(spots == (place.w * 4 + place.n) * each, 1.0, 0.0).astype(bf16)
    own_scales[0] = dot(scales[...], spots).astype(bf16)
    parts.append(own_scales)

    gathers = [
        Gather(place, parts[m], wholes[m], pl.ds(start, size), z_first, (send, recv), k * Gather.SEMS, local.at[k])
        for k, (m, start, size, z_first) in enumerate(pieces)
    ]

    def moved(name, out):
        buffer = held[HELD[name] if out else KEPT[name]]
        there = away[name]
        here = buffer.at[pl.ds(0, there.shape[0])]
        sem = (away_sem if out else come_sem).at[list(KEPT).index(name)]
        return pltpu.make_async_copy(*((here, there) if out else (there, here)), sem)

    lengths = {"enc": enc_lengths, "dec": dec_lengths}
    shared = dict(
        e_x0=e_x0, d_x0=d_x0, e_cot=e_cot, d_cot=d_cot, gains=gains, e_grad=e_grad, d_grad=d_grad,
        enc_out=enc_out, dec_out=dec_out, enc_mask=enc_mask, self_mask=self_mask, cross_mask=cross_mask,
    )
    forward = Forward(dict(shared, gates=da), held, lengths, lambda name: moved(name, True))
    backward = Backward(
        dict(shared, **held, dz=dz, do=do, da=da), lengths,
        lambda name: moved(name, False).wait() if name in KEPT else None,
        lambda name: moved(name, False).start(),
    )
    tall = [w.shape[4] > 3 for w in wholes]

    def staged(k):
        m, start, size, _ = pieces[k]
        if m == count:
            into = wide_ring.at[k % 2, ..., pl.ds(0, 1), :, pl.ds(0, D)]
        else:
            into = (deep_ring.at[2] if tall[m] else wide_ring.at[k % 2]).at[..., pl.ds(0, size)]
        return pltpu.make_async_copy(wholes[m].at[..., pl.ds(start, size)], into, stage_sem.at[k]), into

    deep = [k for k, (m, *_) in enumerate(back_pieces) if tall[m]]

    def ring(k):
        _, _, size, _ = back_pieces[k]
        if k in deep:
            return deep_ring.at[deep.index(k) % 2, ..., pl.ds(0, size)]
        return wide_ring.at[k % RING, ..., pl.ds(0, size)]

    def weight(k):
        m, start, size, _ = back_pieces[k]
        return pltpu.make_async_copy(wholes[m].at[..., pl.ds(start, size)], ring(k), ring_sem.at[k])

    scatters = []
    for k, (m, start, size, z_first) in enumerate(back_pieces):
        total, lasts, zs, firsts = take(4)
        final = deep_out.at[deep.index(k) % 2] if k in deep else wide_out.at[k % 3]
        final = final.at[:, :, pl.ds(0, size)]
        leave = pltpu.make_async_copy(final, outs[m].at[:, :, pl.ds(start, size)], out_sem.at[k])
        scatters.append(
            Scatter(
                place, ring(k), z_first, final, leave, total, lasts, zs, firsts, (back_send, back_recv), k * Scatter.SEMS
            )
        )

    def gather_slot(slot):
        last = STRIDE * (Gather.PHASES - 1)
        for k in range(len(gathers)):
            if (slot - k) % STRIDE == 0 and 0 <= slot - k <= last:
                gathers[k].phase((slot - k) // STRIDE)
        if slot == 0:
            fill_masks(enc_lengths, dec_lengths, enc_mask, self_mask, cross_mask)
        k = slot - last - 1
        if 0 <= k < len(gathers):
            copy, stage = staged(k)
            copy.wait()
            m, start, size, _ = pieces[k]
            if m == count:
                gains[...] = jnp.sum(stage[...].reshape(-1, 8, D).astype(f32), axis=0)
            else:
                forward.step(m, start, size, stage[...].reshape(-1, size))
            if m == 10:
                backward.back(m, pl.ds(start, size), stage, start == 0)
            if k == len(gathers) - 1:
                forward.close()
                backward.after(10)
        if 0 <= slot - last < len(gathers):
            staged(slot - last)[0].start()

    def scatter_slot(slot):
        last_slot = STRIDE * (Scatter.PHASES - 1)
        for k in range(len(scatters)):
            if (slot - k) % STRIDE == 0 and STRIDE <= slot - k <= last_slot:
                scatters[k].phase((slot - k) // STRIDE)
        k = slot
        if k >= len(scatters):
            return
        if 0 < k < len(scatters) - 1:
            weight(k + 1).start()
        m, start, size, _ = back_pieces[k]
        first = k == 0 or back_pieces[k - 1][0] != m
        last = k == len(scatters) - 1 or back_pieces[k + 1][0] != m
        columns = pl.ds(start, size)
        if first:
            backward.before(m)
        left, right = backward.factors(m)
        part = ring(k)
        if m != 10:
            weight(k).wait()
            backward.back(m, columns, part, first)
        cut = Z if k in deep else 2
        height = left.shape[1] // cut
        grad_columns = right[:, columns]
        for j in range(cut):
            grad = dot(left[:, j * height : (j + 1) * height], grad_columns, TN)
            layers = part.at[pl.ds(j * (Z // cut), Z // cut)]
            layers[...] = grad.reshape(layers.shape).astype(bf16)
        scatters[k].phase(0)
        if last and m != 10:
            backward.after(m)

    start = min(k for k, (m, *_) in enumerate(pieces) if m == 10) + STRIDE * (Gather.PHASES - 1)
    gather_slots = len(gathers) + STRIDE * (Gather.PHASES - 1) + 1
    scatter_slots = len(scatters) + STRIDE * (Scatter.PHASES - 1)
    for slot in range(max(gather_slots, start + scatter_slots)):
        if slot < gather_slots:
            gather_slot(slot)
        if 0 <= slot - start < scatter_slots:
            scatter_slot(slot - start)


def whole_step(shards, scales, enc_input, dec_input, enc_cot, dec_cot, enc_lengths, dec_lengths):
    count = len(shards)
    parts = [s.reshape(s.shape[0] // 8, 8, s.shape[1]) for s in shards]
    shapes = [p.shape for p in parts] + [(1, 8, D)]
    pieces = tuple(p[:4] for p in PIECES)
    back = [(*p[:3], p[4]) for p in PIECES[1:]]
    back_pieces = tuple([p for p in back if p[0] == 10] + [p for p in back[::-1] if p[0] != 10])
    rows, short = enc_input.shape[0], dec_input.shape[0]
    hbm, vmem = pl.BlockSpec(memory_space=pl.ANY), pl.BlockSpec(memory_space=pltpu.VMEM)
    smem = pl.BlockSpec(memory_space=pltpu.SMEM)
    wide = max(size for m, _, size, _ in back_pieces if shapes[m][0] == 3)
    deep = max((shapes[m][0], size) for m, _, size, _ in back_pieces)
    buffers = dict(
        a=(rows, FF, bf16), u=(rows, 2 * FF, bf16), h2=(rows, D, bf16), x=(rows, D, f32), q=(short, D, bf16),
        kv=(rows, 2 * D, bf16), o=(rows, D, bf16), qkv=(rows, 3 * D, bf16), h1=(rows, D, bf16), dh=(rows, D, f32),
    )
    dma = pltpu.SemaphoreType.DMA
    scratch = [
        dma((len(pieces) * Gather.SEMS,)), dma((len(pieces) * Gather.SEMS,)), dma((len(pieces),)),
        dma((len(back_pieces) * Scatter.SEMS,)), dma((len(back_pieces) * Scatter.SEMS,)),
        dma((len(pieces),)), dma((len(back_pieces),)), dma((len(back_pieces),)), dma((len(KEPT),)), dma((len(KEPT),)),
    ]
    scratch += [pltpu.VMEM((tall, across), dtype) for tall, across, dtype in buffers.values()]
    scratch += [
        pltpu.VMEM((rows, D), bf16),
        pltpu.VMEM((rows, D), bf16),
        pltpu.VMEM((rows, FF), f32),
        pltpu.VMEM((rows, rows), f32),
        pltpu.VMEM((short, short), f32),
        pltpu.VMEM((short, rows), f32),
        pltpu.VMEM((8, D), f32),
        pltpu.VMEM((1, 8, D), bf16),
        pltpu.VMEM((RING, Z, 2, 2, 2, 3, 8, wide), bf16),
        pltpu.VMEM((3, Z, 2, 2, 2, deep[0], 8, deep[1]), bf16),
        pltpu.VMEM((3, 3, 8, wide), f32),
        pltpu.VMEM((2, deep[0], 8, deep[1]), f32),
    ]
    for m, _, size, z_first in back_pieces:
        block = (shapes[m][0], 8, size)
        scratch += [
            pltpu.VMEM((Z, 2, 2, *block), bf16),
            pltpu.VMEM((Z, 2, *block), bf16),
            pltpu.VMEM((5, *(() if z_first else (2,)), *block), bf16),
            pltpu.VMEM((*((Z,) if z_first else ()), *block), bf16),
        ]
    kept = [(short if name[0] == "d" else rows, *buffers[HELD[name]][1:]) for name in KEPT]
    outs = pl.pallas_call(
        functools.partial(whole_body, pieces, back_pieces, count),
        out_shape=[jax.ShapeDtypeStruct(p.shape, f32) for p in parts]
        + [
            jax.ShapeDtypeStruct((rows, D), f32),
            jax.ShapeDtypeStruct((short, D), f32),
            jax.ShapeDtypeStruct((rows, D), bf16),
            jax.ShapeDtypeStruct((short, D), bf16),
        ]
        + [jax.ShapeDtypeStruct((Z, 2, 2, 2, *shape), bf16) for shape in shapes]
        + [jax.ShapeDtypeStruct((tall, across), dtype) for tall, across, dtype in kept],
        in_specs=[hbm] * count + [vmem] * 5 + [smem] * 2,
        out_specs=[hbm] * count + [vmem] * 4 + [hbm] * (count + 1 + len(KEPT)),
        scratch_shapes=scratch,
        compiler_params=pltpu.CompilerParams(
            collective_id=0, has_side_effects=True, vmem_limit_bytes=VMEM_LIMIT
        ),
    )(*parts, scales, enc_input, dec_input, enc_cot, dec_cot, enc_lengths, dec_lengths)
    e_grad, d_grad, enc_out, dec_out = outs[count : count + 4]
    return outs[:count], (enc_out, dec_out, e_grad, d_grad)


VMEM_LIMIT = 62 * 2**20


def finish_body(count, scaled, *refs):
    refs = list(refs)

    def take(n):
        got = refs[:n]
        del refs[:n]
        return got

    totals, shards, (scales,), passed = take(count), take(len(scaled)), take(1), take(4)
    grads, scale_grads, through = take(count), take(len(scaled)), take(4)
    for total, grad in zip(totals, grads):
        grad[...] = total[...].reshape(grad.shape)
    for k, (m, shard, out) in enumerate(zip(scaled, shards, scale_grads)):
        product = grads[m][...] * shard[...].astype(f32)
        summed = lax.dot_general(
            jnp.ones((8, product.shape[1]), f32), product, NT,
            precision=lax.Precision.HIGHEST, preferred_element_type=f32,
        )
        out[...] = summed[0:1] / scales[k : k + 1].astype(f32)
    for src, out in zip(passed, through):
        out[...] = src[...]


def finish(totals, shards, scales, passed):
    scaled = [m for m, k in enumerate(SCALE_OF) if k is not None]
    vmem = pl.BlockSpec(memory_space=pltpu.VMEM)
    count = len(totals)
    outs = pl.pallas_call(
        functools.partial(finish_body, count, scaled),
        out_shape=[jax.ShapeDtypeStruct(s.shape, f32) for s in shards]
        + [jax.ShapeDtypeStruct((1, scales.shape[1]), f32)] * len(scaled)
        + [jax.ShapeDtypeStruct(p.shape, p.dtype) for p in passed],
        in_specs=[vmem] * (count + len(scaled) + 5),
        out_specs=[vmem] * (count + len(scaled) + 4),
        compiler_params=pltpu.CompilerParams(vmem_limit_bytes=VMEM_LIMIT),
    )(*totals, *[shards[m] for m in scaled], scales, *passed)
    return outs[:count], [g.reshape(-1) for g in outs[count:-4]], outs[-4:]


def norm_rows(values, scales):
    return values * lax.rsqrt(jnp.mean(values * values, axis=-1, keepdims=True) + epsilon) * scales


def norm_back(inputs, scales, grad):
    return jax.vjp(lambda v: norm_rows(v, scales), inputs)[1](grad)[0]


def gated_units(united):
    halfway = united.shape[-1] // 2
    return jax.nn.gelu(united[:, :halfway], approximate=True) * united[:, halfway:]


def row_items(lengths, row_count):
    places = jnp.arange(row_count, dtype=jnp.int32)
    count = lengths.shape[0]
    item, boundary = jnp.zeros((row_count,), jnp.int32), jnp.int32(0)
    for k in range(count):
        boundary = boundary + lengths[k]
        item = item + (places >= boundary).astype(jnp.int32)
    return item


def head_split(matrix):
    return matrix.reshape(matrix.shape[0], HEADS, HEAD_DIM)


def outer_rows(left, right):
    return jnp.einsum("rd,re->de", left, right, preferred_element_type=jnp.float32).astype(jnp.bfloat16)


def back_rows(incoming, matrix):
    return jnp.einsum("re,de->rd", incoming, matrix, preferred_element_type=jnp.float32)


def score_rows(query_heads, key_heads, allowed):
    raw_scores = jnp.einsum(
        "qhd,khd->hqk", query_heads, key_heads, preferred_element_type=jnp.float32
    )
    return jnp.where(allowed[None], raw_scores * HEAD_DIM ** (-0.5), masked_value)


def attend_forward(queries, keys_in, values_in, allowed):
    scores = score_rows(head_split(queries), head_split(keys_in), allowed)
    largest = jnp.max(scores, axis=2, keepdims=True)
    expanded = jnp.exp(scores - largest)
    totals = jnp.sum(expanded, axis=2, keepdims=True)
    weights = (expanded / totals).astype(jnp.bfloat16)
    mixed = jnp.einsum(
        "hqk,khd->qhd", weights, head_split(values_in), preferred_element_type=jnp.float32
    )
    return (mixed.reshape(queries.shape[0], D), largest + jnp.log(totals))


def attend_backward(queries, keys_in, values_in, allowed, log_totals, grad_mixed):
    query_heads = head_split(queries)
    key_heads = head_split(keys_in)
    value_heads = head_split(values_in)
    probs = jnp.exp(score_rows(query_heads, key_heads, allowed) - log_totals)
    grad_heads = head_split(grad_mixed)
    grad_values = jnp.einsum(
        "hqk,qhd->khd", probs.astype(jnp.bfloat16), grad_heads, preferred_element_type=jnp.float32
    )
    grad_probs = jnp.einsum(
        "qhd,khd->hqk", grad_heads, value_heads, preferred_element_type=jnp.float32
    )
    centred = grad_probs - jnp.sum(probs * grad_probs, axis=2, keepdims=True)
    grad_scores = (probs * centred * HEAD_DIM ** (-0.5)).astype(jnp.bfloat16)
    grad_queries = jnp.einsum(
        "hqk,khd->qhd", grad_scores, key_heads, preferred_element_type=jnp.float32
    )
    grad_keys = jnp.einsum(
        "hqk,qhd->khd", grad_scores, query_heads, preferred_element_type=jnp.float32
    )
    return (
        grad_queries.reshape(queries.shape[0], D),
        grad_keys.reshape(keys_in.shape[0], D),
        grad_values.reshape(keys_in.shape[0], D),
    )


def self_forward(inputs, params, allowed, live_rows):
    scales, joined, outward = params
    normed = norm_rows(inputs, scales).astype(jnp.bfloat16)
    projected = jnp.dot(normed, joined, preferred_element_type=jnp.float32).astype(jnp.bfloat16)
    mixed, log_totals = attend_forward(
        projected[:, :D], projected[:, D : 2 * D], projected[:, 2 * D :], allowed
    )
    mixed_low = mixed.astype(jnp.bfloat16)
    branch = jnp.dot(mixed_low, outward, preferred_element_type=jnp.float32)
    return (inputs + live_rows[:, None] * branch, (normed, projected, mixed_low, log_totals))


def self_backward(inputs, params, allowed, live_rows, stored, incoming):
    scales, joined, outward = params
    normed, projected, mixed_low, log_totals = stored
    grad_branch = (live_rows[:, None] * incoming).astype(jnp.bfloat16)
    grad_outward = outer_rows(mixed_low, grad_branch)
    grad_mixed = back_rows(grad_branch, outward).astype(jnp.bfloat16)
    grad_parts = attend_backward(
        projected[:, :D],
        projected[:, D : 2 * D],
        projected[:, 2 * D :],
        allowed,
        log_totals,
        grad_mixed,
    )
    grad_projected = jnp.concatenate(grad_parts, axis=1).astype(jnp.bfloat16)
    grad_joined = outer_rows(normed, grad_projected)
    grad_inputs = norm_back(inputs, scales, back_rows(grad_projected, joined))
    return (incoming + grad_inputs, (grad_joined, grad_outward))


def cross_forward(inputs, memory, params, allowed, live_rows):
    scales, memory_scales, query_map, pair_map, outward = params
    normed = norm_rows(inputs, scales).astype(jnp.bfloat16)
    memory_normed = norm_rows(memory, memory_scales).astype(jnp.bfloat16)
    queries = jnp.dot(normed, query_map, preferred_element_type=jnp.float32).astype(jnp.bfloat16)
    pairs = jnp.dot(memory_normed, pair_map, preferred_element_type=jnp.float32).astype(
        jnp.bfloat16
    )
    mixed, log_totals = attend_forward(queries, pairs[:, :D], pairs[:, D:], allowed)
    mixed_low = mixed.astype(jnp.bfloat16)
    branch = jnp.dot(mixed_low, outward, preferred_element_type=jnp.float32)
    return (
        inputs + live_rows[:, None] * branch,
        (normed, memory_normed, queries, pairs, mixed_low, log_totals),
    )


def cross_backward(inputs, memory, params, allowed, live_rows, stored, incoming):
    scales, memory_scales, query_map, pair_map, outward = params
    normed, memory_normed, queries, pairs, mixed_low, log_totals = stored
    grad_branch = (live_rows[:, None] * incoming).astype(jnp.bfloat16)
    grad_outward = outer_rows(mixed_low, grad_branch)
    grad_mixed = back_rows(grad_branch, outward).astype(jnp.bfloat16)
    grad_queries, grad_keys, grad_values = attend_backward(
        queries, pairs[:, :D], pairs[:, D:], allowed, log_totals, grad_mixed
    )
    grad_queries_low = grad_queries.astype(jnp.bfloat16)
    grad_pairs = jnp.concatenate([grad_keys, grad_values], axis=1).astype(jnp.bfloat16)
    grad_query_map = outer_rows(normed, grad_queries_low)
    grad_pair_map = outer_rows(memory_normed, grad_pairs)
    grad_inputs = norm_back(inputs, scales, back_rows(grad_queries_low, query_map))
    grad_memory = norm_back(memory, memory_scales, back_rows(grad_pairs, pair_map))
    return (
        incoming + grad_inputs,
        grad_memory,
        (grad_query_map, grad_pair_map, grad_outward),
    )


def mlp_forward(inputs, params, live_rows):
    scales, inward, outward = params
    normed = norm_rows(inputs, scales).astype(jnp.bfloat16)
    united = jnp.dot(normed, inward, preferred_element_type=jnp.float32)
    activated = gated_units(united).astype(jnp.bfloat16)
    branch = jnp.dot(activated, outward, preferred_element_type=jnp.float32)
    return (inputs + live_rows[:, None] * branch, (normed, united, activated))


def mlp_backward(inputs, params, live_rows, stored, incoming):
    scales, inward, outward = params
    normed, united, activated = stored
    grad_branch = (live_rows[:, None] * incoming).astype(jnp.bfloat16)
    grad_outward = outer_rows(activated, grad_branch)
    grad_activated = back_rows(grad_branch, outward)
    _, pullback = jax.vjp(gated_units, united)
    grad_united = pullback(grad_activated)[0].astype(jnp.bfloat16)
    grad_inward = outer_rows(normed, grad_united)
    grad_inputs = norm_back(inputs, scales, back_rows(grad_united, inward))
    return (incoming + grad_inputs, (grad_inward, grad_outward))


def plain_gather(shards):
    return [lax.all_gather(s, AXES, axis=0, tiled=True) for s in shards]


def plain_scatter(sums):
    return [lax.psum_scatter(s.astype(jnp.float32), AXES, scatter_dimension=0, tiled=True) for s in sums]


SCALE_OF = (0, None, 1, None, 2, None, 3, 4, None, 5, None)


def per_device(
    linked,
    enc_input,
    dec_input,
    enc_lengths,
    dec_lengths,
    enc_attn_gain,
    enc_qkv,
    enc_attn_out,
    enc_mlp_gain,
    enc_mlp_in,
    enc_mlp_out,
    dec_self_gain,
    dec_qkv,
    dec_self_out,
    cross_gain,
    memory_gain,
    cross_query,
    cross_kv,
    cross_out,
    dec_mlp_gain,
    dec_mlp_in,
    dec_mlp_out,
    enc_cotangent,
    dec_cotangent,
):
    gains = [enc_attn_gain, enc_mlp_gain, dec_self_gain, cross_gain, memory_gain, dec_mlp_gain]
    shards = (
        enc_qkv, enc_attn_out, enc_mlp_in, enc_mlp_out, dec_qkv, dec_self_out,
        cross_query, cross_kv, cross_out, dec_mlp_in, dec_mlp_out,
    )
    if linked:
        stacked = jnp.stack(gains + [jnp.zeros_like(gains[0])] * (8 - len(gains)))
        summed, passed = whole_step(
            shards, stacked, enc_input, dec_input, enc_cotangent, dec_cotangent, enc_lengths, dec_lengths
        )
        grads, scale_grads, (enc_out, dec_out, grad_encoder_start, grad_decoder_start) = finish(
            summed, shards, stacked, passed
        )
    else:
        item_count = enc_lengths.shape[0]
        enc_items = row_items(enc_lengths, enc_input.shape[0])
        dec_items = row_items(dec_lengths, dec_input.shape[0])
        enc_live = (enc_items < item_count).astype(jnp.float32)
        dec_live = (dec_items < item_count).astype(jnp.float32)
        enc_padded = enc_items[:, None] == item_count
        dec_padded = dec_items[:, None] == item_count
        enc_allowed = (enc_items[:, None] == enc_items[None, :]) | enc_padded
        dec_places = jnp.arange(dec_input.shape[0], dtype=jnp.int32)
        self_allowed = (dec_items[:, None] == dec_items[None, :]) & (
            dec_places[None, :] <= dec_places[:, None]
        ) | dec_padded
        cross_allowed = (dec_items[:, None] == enc_items[None, :]) | dec_padded
        whole = plain_gather(shards)
        own = [g.astype(jnp.float32) for g in gains]
        gains = plain_gather(own)
        encoder_start = enc_input.astype(jnp.float32)
        decoder_start = dec_input.astype(jnp.float32)
        enc_middle, enc_attn_store = self_forward(encoder_start, (gains[0], *whole[0:2]), enc_allowed, enc_live)
        encoder_final, enc_mlp_store = mlp_forward(enc_middle, (gains[1], *whole[2:4]), enc_live)
        dec_middle, dec_self_store = self_forward(decoder_start, (gains[2], *whole[4:6]), self_allowed, dec_live)
        dec_crossed, cross_store = cross_forward(
            dec_middle, encoder_final, (gains[3], gains[4], *whole[6:9]), cross_allowed, dec_live
        )
        decoder_final, dec_mlp_store = mlp_forward(dec_crossed, (gains[5], *whole[9:11]), dec_live)
        enc_out, dec_out = encoder_final.astype(jnp.bfloat16), decoder_final.astype(jnp.bfloat16)
        grad_crossed, dec_mlp_grads = mlp_backward(
            dec_crossed, (gains[5], *whole[9:11]), dec_live, dec_mlp_store, dec_cotangent.astype(jnp.float32)
        )
        grad_middle, grad_memory, cross_grads = cross_backward(
            dec_middle,
            encoder_final,
            (gains[3], gains[4], *whole[6:9]),
            cross_allowed,
            dec_live,
            cross_store,
            grad_crossed,
        )
        grad_decoder_start, dec_self_grads = self_backward(
            decoder_start, (gains[2], *whole[4:6]), self_allowed, dec_live, dec_self_store, grad_middle
        )
        grad_enc_middle, enc_mlp_grads = mlp_backward(
            enc_middle,
            (gains[1], *whole[2:4]),
            enc_live,
            enc_mlp_store,
            enc_cotangent.astype(jnp.float32) + grad_memory,
        )
        grad_encoder_start, enc_attn_grads = self_backward(
            encoder_start, (gains[0], *whole[0:2]), enc_allowed, enc_live, enc_attn_store, grad_enc_middle
        )
        sums = enc_attn_grads + enc_mlp_grads + dec_self_grads + cross_grads + dec_mlp_grads
        summed = plain_scatter(sums)
        grads, scale_grads = [], {}
        for total, shard, k in zip(summed, shards, SCALE_OF):
            if k is not None:
                scale_grads[k] = jnp.sum(total * shard.astype(jnp.float32), axis=1) / own[k]
            grads.append(total)
    return (
        enc_out,
        dec_out,
        grad_encoder_start,
        grad_decoder_start,
        scale_grads[0], grads[0], grads[1],
        scale_grads[1], grads[2], grads[3],
        scale_grads[2], grads[4], grads[5],
        scale_grads[3], scale_grads[4], grads[6], grads[7], grads[8],
        scale_grads[5], grads[9], grads[10],
    )


def solution(mesh):
    rows, line = P(AXES, None), P(AXES)
    linked = mesh.shape["wide"] == 2 * Z and mesh.shape["narrow"] == 4
    weights = (
        line, rows, rows, line, rows, rows, line, rows, rows,
        line, line, rows, rows, rows, line, rows, rows,
    )
    return jax.shard_map(
        functools.partial(per_device, linked),
        mesh=mesh,
        in_specs=(rows, rows, line, line, *weights, rows, rows),
        out_specs=(rows, rows, rows, rows, *weights),
        check_vma=False,
    )
```

```python
import functools

import jax
import jax.numpy as jnp
from jax import lax
from jax.experimental import pallas as pl
from jax.experimental.pallas import tpu as pltpu
from jax.sharding import PartitionSpec as P

D = 768
HEADS = 12
HEAD_DIM = 64
FF = 2048
AXES = ("wide", "narrow")
MESH = pl.DeviceIdType.MESH

Z = 4
PIECES = (
    (11, 0, 768, False, False),
    (0, 0, 1152, True, True),
    (0, 1152, 1152, False, True),
    (1, 0, 768, True, False),
    (2, 0, 1024, False, True),
    (2, 1024, 1024, False, False),
    (2, 2048, 1024, True, False),
    (2, 3072, 1024, False, True),
    (3, 0, 384, False, False),
    (3, 384, 384, True, True),
    (4, 0, 1152, False, False),
    (4, 1152, 1152, False, False),
    (5, 0, 768, True, False),
    (6, 0, 768, False, False),
    (7, 0, 768, False, False),
    (7, 768, 768, True, False),
    (8, 0, 768, False, True),
    (9, 0, 1024, False, True),
    (9, 1024, 1024, False, False),
    (9, 2048, 1024, True, False),
    (9, 3072, 1024, False, False),
    (10, 0, 384, False, False),
    (10, 384, 384, False, False),
)
STRIDE = 2


class Place:
    def __init__(self):
        self.w, self.n = lax.axis_index("wide"), lax.axis_index("narrow")
        self.z, self.y = self.w // 2, self.w % 2
        self.x, self.c = self.n // 2, self.n % 2
        w, n, y, x, c = self.w, self.n, self.y, self.x, self.c
        self.sibling = (w, n + 1 - 2 * c)
        self.first = (w + (1 - c) * (1 - 2 * y), n + c * (2 - 4 * x))
        self.last = (w + c * (1 - 2 * y), n + (1 - c) * (2 - 4 * x))
        self.above = (w + 2, n)
        self.below = (w - 2, n)

    def barrier(self):
        sem = pltpu.get_barrier_semaphore()
        for device in (self.sibling, self.first, self.last):
            pl.semaphore_signal(sem, inc=1, device_id=device, device_id_type=MESH)

        @pl.when(self.z < Z - 1)
        def _():
            pl.semaphore_signal(sem, inc=1, device_id=self.above, device_id_type=MESH)

        @pl.when(self.z > 0)
        def _():
            pl.semaphore_signal(sem, inc=1, device_id=self.below, device_id_type=MESH)

        inner = jnp.where(self.z * (Z - 1 - self.z) > 0, 1, 0)
        pl.semaphore_wait(sem, 4 + inner)

    def by_core(self, do):
        @pl.when(self.c == 0)
        def _():
            do(0)

        @pl.when(self.c == 1)
        def _():
            do(1)


def remote(src, dst, sems, index, device):
    send, recv = sems
    return pltpu.make_async_remote_copy(
        src_ref=src, dst_ref=dst, send_sem=send.at[index], recv_sem=recv.at[index],
        device_id=device, device_id_type=MESH,
    )


class Gather:
    PHASES = 7
    SEMS = 13

    def __init__(self, place, part, whole, columns, z_first, sems, base, local_sem):
        self.p, self.z_first, self.sems, self.base = place, z_first, sems, base
        self.part = part.at[:, :, columns]
        self.whole = whole.at[:, :, :, :, :, :, columns]
        self.local = pltpu.make_async_copy(self.part, self.own(), local_sem)

    def own(self):
        p = self.p
        return self.whole.at[p.z, p.y, p.x, p.c]

    def copy(self, src, dst, slot, device):
        return remote(src, dst, self.sems, self.base + slot, device)

    def layer(self, zz, core):
        p = self.p
        if self.z_first:
            return self.whole.at[zz, p.y, p.x, core]
        return self.whole.at[zz, :, p.x, 0] if core == 0 else self.whole.at[zz, p.y, :, 1]

    def half(self, core, mine):
        p = self.p
        if core == 0:
            return self.whole.at[:, :, p.x if mine else 1 - p.x, 0]
        return self.whole.at[:, p.y if mine else 1 - p.y, :, 1]

    def along_z(self, step, sending):
        p = self.p

        def go(core):
            for up in (True, False):
                if sending:
                    zz = p.z - step if up else p.z + step
                    there = (p.z < Z - 1) & (zz >= 0) if up else (p.z > 0) & (zz < Z)
                else:
                    zz = p.z - 1 - step if up else p.z + 1 + step
                    there = zz >= 0 if up else zz < Z

                target = (p.above if up else p.below) if sending else p.last

                @pl.when(there)
                def _():
                    block = self.layer(zz, core)
                    copy = self.copy(block, block, 1 + step * 2 + up, target)
                    copy.start() if sending else copy.wait_recv()

        p.by_core(go)

    def along_z_sent(self):
        p = self.p

        def go(core):
            for step in range(3):
                for up in (True, False):
                    zz = p.z - step if up else p.z + step
                    there = (p.z < Z - 1) & (zz >= 0) if up else (p.z > 0) & (zz < Z)

                    @pl.when(there)
                    def _():
                        block = self.layer(zz, core)
                        self.copy(block, block, 1 + step * 2 + up, p.last).wait_send()

        p.by_core(go)

    def first(self, core):
        p = self.p
        if not self.z_first:
            return self.copy(self.part, self.own(), 0, p.first)
        block = self.whole.at[:, p.y, p.x, core]
        return self.copy(block, block, 0, p.first)

    def last(self, core):
        block = self.half(core, True)
        return self.copy(block, block, 7, self.p.last)

    def last_layer(self, zz, core, mine=True):
        p = self.p
        if core == 0:
            block = self.whole.at[zz, :, p.x if mine else 1 - p.x, 0]
        else:
            block = self.whole.at[zz, p.y if mine else 1 - p.y, :, 1]
        return self.copy(block, block, 7 + zz, p.last)

    def far_layers(self, far, core, verb):
        z = self.p.z
        if far == 0:
            getattr(self.last_layer(z, core), verb)()
            return

        @pl.when(z + far < Z)
        def _():
            getattr(self.last_layer(z + far, core), verb)()

        @pl.when(z - far >= 0)
        def _():
            getattr(self.last_layer(z - far, core), verb)()

    def send_far(self, far):
        self.p.by_core(lambda core: self.far_layers(far, core, "start"))

    def wait_last(self, core, verb):
        if self.z_first:
            getattr(self.last(core), verb)()
        else:
            for zz in range(Z):
                getattr(self.last_layer(zz, core, verb == "wait_send"), verb)()

    def across(self, core, mine):
        block = self.half(core, mine)
        return self.copy(block, block, 11 if mine else 12, self.p.sibling)

    def each(self, make, *verbs):
        def go(core):
            copy = make(core)
            for verb in verbs:
                getattr(copy, verb)()

        self.p.by_core(go)

    def phase(self, number):
        early = not self.z_first
        if number == 0:
            self.local.start()
            if early:
                self.each(self.first, "start")
            self.local.wait()
            if not early:
                self.along_z(0, True)
        elif number == 1:
            if early:
                self.each(self.first, "wait_recv")
                self.along_z(0, True)
                self.send_far(0)
            else:
                self.along_z(0, False)
                self.along_z(1, True)
        elif number == 2:
            self.along_z(0 if early else 1, False)
            self.along_z(1 if early else 2, True)
            if early:
                self.send_far(1)
        elif number == 3:
            self.along_z(1 if early else 2, False)
            if early:
                self.along_z(2, True)
                self.send_far(2)
            else:
                self.each(self.first, "start")
        elif number == 4:
            if early:
                self.along_z(2, False)
                self.send_far(3)
            else:
                self.each(self.first, "wait_recv")
                self.each(self.last, "start")
            self.each(lambda core: self.across(core, True), "start")
        elif number == 5:
            self.p.by_core(lambda core: self.wait_last(core, "wait_recv"))
            self.each(lambda core: self.across(core, False), "start")
        else:
            for core in (0, 1):
                @pl.when(self.p.c == core)
                def _():
                    for mine in (True, False):
                        self.across(1 - core, mine).wait_recv()

    def settle(self):
        def go(core):
            for mine in (True, False):
                self.across(core, mine).wait_send()
            self.first(core).wait_send()
            self.wait_last(core, "wait_send")

        self.p.by_core(go)
        self.along_z_sent()


class Scatter:
    PHASES = 8
    SEMS = 12

    def __init__(self, place, parts, z_first, out, leave, total, lasts, zs, firsts, sems, base):
        self.p, self.z_first, self.sems, self.base = place, z_first, sems, base
        self.parts, self.out, self.leave = parts, out, leave
        self.total, self.lasts, self.zs, self.firsts = total, lasts, zs, firsts

    def copy(self, src, dst, slot, device):
        return remote(src, dst, self.sems, self.base + slot, device)

    def spot(self, core, last, first=None):
        every = slice(None)
        if first is None:
            return (every, last) if core else (every, every, last)
        return (last, first) if core else (first, last)

    def place_of(self, core):
        p = self.p
        return (p.y, p.x) if core else (p.x, p.y)

    def across(self, core):
        return self.copy(self.parts.at[:, :, :, 1 - core], self.total, 0, self.p.sibling)

    def last(self, core):
        last, _ = self.place_of(core)
        return self.copy(self.total.at[self.spot(core, 1 - last)], self.lasts, 8, self.p.last)

    def last_layer(self, zz, core):
        last, _ = self.place_of(core)
        src = self.total.at[(zz, *self.spot(core, 1 - last)[1:])]
        return self.copy(src, self.lasts.at[zz], 8 + zz, self.p.last)

    def far_layers(self, far, do):
        z = self.p.z
        if far == 0:
            do(z)
            return

        @pl.when(z + far < Z)
        def _():
            do(z + far)

        @pl.when(z - far >= 0)
        def _():
            do(z - far)

    def send_layers(self, core):
        for far in (3, 2, 1, 0):
            self.far_layers(far, lambda zz: self.last_layer(zz, core).start())

    def add_layers(self, far):
        def one(zz):
            self.p.by_core(lambda core: self.last_layer(zz, core).wait_recv())
            for k in range(2):
                self.total[(zz, *self.pair(k))] += self.lasts[zz, k]

        self.far_layers(far, one)

    def last_sent(self, core):
        if self.z_first:
            self.last(core).wait_send()
        else:
            for zz in range(Z):
                self.last_layer(zz, core).wait_send()

    def first(self, core):
        p = self.p
        last, first = self.place_of(core)
        if self.z_first:
            src = self.total.at[(slice(None), *self.spot(core, last, 1 - first))]
        else:
            src = self.total.at[(p.z, *self.spot(core, last, 1 - first))]
        return self.copy(src, self.firsts, 1, p.first)

    def layer(self, zz, core):
        last, first = self.place_of(core)
        if self.z_first:
            return self.total.at[(zz, *self.spot(core, last, first))]
        return self.total.at[(zz, *self.spot(core, last)[1:])]

    def way(self, step, up, sending):
        z, far = self.p.z, 2 - step
        if sending:
            zz = z + 1 + far if up else z - 1 - far
            return zz, zz < Z if up else zz >= 0
        zz = z + far if up else z - far
        return zz, (z > 0) & (zz < Z) if up else (z < Z - 1) & (zz >= 0)

    def landing(self, step, up):
        return 0 if step == 0 else 2 * step - 1 + up

    def along_z(self, step, verb):
        p = self.p

        def go(core):
            for up in (True, False):
                zz, there = self.way(step, up, verb != "wait_recv")
                target = (p.above if up else p.below) if verb == "start" else p.last

                @pl.when(there)
                def _():
                    copy = self.copy(self.layer(zz, core), self.zs.at[self.landing(step, up)], 2 + step * 2 + up, target)
                    getattr(copy, verb)()

        p.by_core(go)

    def add_z(self, step):
        p = self.p
        for up in (True, False):
            zz, there = self.way(step, up, False)

            @pl.when(there)
            def _():
                arrived = self.zs.at[self.landing(step, up)]
                if self.z_first:
                    self.total[zz, p.y, p.x] += arrived[...]
                else:
                    for k in range(2):
                        self.total[(zz, *self.pair(k))] += arrived[k]

    def pair(self, k):
        p = self.p
        return k * (1 - p.c) + p.y * p.c, p.x * (1 - p.c) + k * p.c

    def each(self, make, *verbs):
        def go(core):
            copy = make(core)
            for verb in verbs:
                getattr(copy, verb)()

        self.p.by_core(go)

    def phase(self, number):
        p, early = self.p, self.z_first
        if number == 0:
            self.each(self.across, "start")
        elif number == 1:
            self.each(self.across, "wait_recv")

            @pl.loop(0, 16)
            def _(i):
                self.total[i // 4, i // 2 % 2, i % 2] += self.parts[i // 4, i // 2 % 2, i % 2, p.c]

            if early:
                self.each(self.last, "start")
            else:
                p.by_core(self.send_layers)
            self.each(self.across, "wait_send")
        elif number == 2:
            if early:
                self.each(self.last, "wait_recv")

                @pl.loop(0, 8)
                def _(i):
                    self.total[(i // 2, *self.pair(i % 2))] += self.lasts[i // 2, i % 2]

                self.each(self.first, "start")
            else:
                self.add_layers(3)
                self.along_z(0, "start")
        elif number == 3:
            if early:
                self.each(self.first, "wait_recv")

                @pl.loop(0, Z)
                def _(i):
                    self.total[i, p.y, p.x] += self.firsts[i]

                self.along_z(0, "start")
            else:
                self.add_layers(2)
                self.along_z(0, "wait_recv")
                self.add_z(0)
                self.along_z(1, "start")
        elif number == 4:
            step = 0 if early else 1
            if not early:
                self.add_layers(1)
            self.along_z(step, "wait_recv")
            self.add_z(step)
            self.along_z(step + 1, "start")
        elif number == 5:
            step = 1 if early else 2
            if not early:
                self.add_layers(0)
            self.along_z(step, "wait_recv")
            self.add_z(step)
            if early:
                self.along_z(2, "start")
            else:
                self.each(self.first, "start")
        elif number == 6:
            if early:
                self.along_z(2, "wait_recv")
                self.add_z(2)
                self.out[...] = self.total[p.z, p.y, p.x].astype(jnp.float32)
            else:
                self.each(self.first, "wait_recv")
                self.out[...] = self.total[p.z, p.y, p.x].astype(jnp.float32) + self.firsts[...].astype(jnp.float32)
            self.leave.start()
        else:
            self.leave.wait()
            p.by_core(self.last_sent)
            self.each(self.first, "wait_send")
            for step in range(3):
                self.along_z(step, "wait_send")


epsilon = 1e-06
masked_value = -1000000000.0
SHRINK = HEAD_DIM**-0.5
NT = (((1,), (1,)), ((), ()))
TN = (((0,), (0,)), ((), ()))
f32, bf16 = jnp.float32, jnp.bfloat16


def dot(a, b, dims=(((1,), (0,)), ((), ()))):
    return lax.dot_general(a, b, dims, preferred_element_type=f32)


def shrunk(values):
    return lax.rsqrt(jnp.mean(values * values, axis=-1, keepdims=True) + epsilon)


def norm(values, scales):
    return values * shrunk(values) * scales


def items_of(lengths_ref, places):
    item, boundary = jnp.zeros_like(places), 0
    for k in range(lengths_ref.shape[0]):
        boundary = boundary + lengths_ref[k]
        item = item + jnp.where(places >= boundary, 1, 0)
    return item


def fill_masks(enc_lengths, dec_lengths, enc_mask, self_mask, cross_mask):
    count = enc_lengths.shape[0]

    def grid(ref, axis):
        return lax.broadcasted_iota(jnp.int32, ref.shape, axis)

    def put(ref, rows, columns, both):
        kept = rows == columns
        if both is not None:
            kept = kept & both
        ref[...] = jnp.where(kept | (rows == count), 1.0, 0.0)

    put(enc_mask, items_of(enc_lengths, grid(enc_mask, 0)), items_of(enc_lengths, grid(enc_mask, 1)), None)
    put(
        self_mask, items_of(dec_lengths, grid(self_mask, 0)), items_of(dec_lengths, grid(self_mask, 1)),
        grid(self_mask, 1) <= grid(self_mask, 0),
    )
    put(cross_mask, items_of(dec_lengths, grid(cross_mask, 0)), items_of(enc_lengths, grid(cross_mask, 1)), None)


def live_rows(lengths_ref, rows):
    item = items_of(lengths_ref, lax.broadcasted_iota(jnp.int32, (rows, 1), 0))
    return jnp.where(item < lengths_ref.shape[0], 1.0, 0.0)


def head_lanes(which):
    lanes = lax.broadcasted_iota(jnp.int32, (1, 2 * HEAD_DIM), 1)
    return jnp.where(lanes // HEAD_DIM == which, 1.0, 0.0).astype(bf16)


def head_probs(q, k, kept):
    scores = jnp.where(kept[...] > 0.0, dot(q, k, NT) * SHRINK, masked_value)
    raised = jnp.exp(scores - jnp.max(scores, axis=1, keepdims=True))
    return raised * (1.0 / jnp.sum(raised, axis=1, keepdims=True))


def pair_columns(pair, offset):
    return pl.ds(pl.multiple_of(pair * (2 * HEAD_DIM) + offset, 2 * HEAD_DIM), 2 * HEAD_DIM)


def attend(q_ref, q_at, k_ref, k_at, v_ref, v_at, kept, out_ref):
    @pl.loop(0, HEADS // 2)
    def _(pair):
        q = q_ref[:, pair_columns(pair, q_at)]
        k = k_ref[:, pair_columns(pair, k_at)]
        v = v_ref[:, pair_columns(pair, v_at)]
        mixed = None
        for which in range(2):
            lanes = head_lanes(which)
            part = dot(head_probs(q * lanes, k, kept).astype(bf16), v * lanes)
            mixed = part if mixed is None else mixed + part
        out_ref[:, pair_columns(pair, 0)] = mixed.astype(bf16)


def gelu_tanh(t):
    return jnp.tanh(0.7978845608028654 * (t + 0.044715 * (t * t * t)))


class Forward:
    def __init__(self, refs, held, lengths, store):
        self.__dict__.update(refs)
        self.held, self.lengths, self.store, self.leaving = held, lengths, store, {}

    def at(self, name):
        buffer = self.held[HELD[name]]
        return buffer.at[pl.ds(0, self.rows("dec"))] if name[0] == "d" or name in ("c_o", "hq") else buffer

    def rows(self, side):
        return self.e_x0.shape[0] if side == "enc" else self.d_x0.shape[0]

    def opened(self, name):
        copy = self.leaving.pop(HELD[name], None)
        if copy is not None:
            copy.wait()
        return self.at(name)

    def kept(self, name):
        if name in KEPT:
            copy = self.store(name)
            copy.start()
            self.leaving[HELD[name]] = copy

    def close(self):
        for copy in self.leaving.values():
            copy.wait()

    def set_norm(self, values, k, name):
        self.opened(name)[...] = norm(values, self.gains[k : k + 1]).astype(bf16)
        self.kept(name)

    def live(self, side):
        return live_rows(self.lengths[side], self.rows(side))

    def step(self, m, start, size, weight):
        columns = pl.ds(start, size)
        side, rows = ("e", "enc") if m < 4 else ("d", "dec")
        first = start == 0
        if m == 0 or m == 4:
            h1, qkv, o = side + "_h1", side + "_qkv", side + "_o"
            if first:
                before = self.e_x0 if m == 0 else self.d_x0
                self.set_norm(before[...].astype(f32), 0 if m == 0 else 2, h1)
                self.opened(qkv)
            ref = self.at(qkv)
            ref[:, columns] = dot(self.at(h1)[...], weight).astype(bf16)
            if start + size == ref.shape[1]:
                self.kept(qkv)
                attend(ref, 0, ref, D, ref, 2 * D, self.enc_mask if m == 0 else self.self_mask, self.opened(o))
                self.kept(o)
        elif m == 1 or m == 5:
            before, x1 = (self.e_x0, "e_x1") if m == 1 else (self.d_x0, "d_x1")
            after = before[...].astype(f32) + self.live(rows) * dot(self.at(side + "_o")[...], weight)
            self.opened(x1)[...] = after
            self.kept(x1)
            self.set_norm(self.at(x1)[...], 1 if m == 1 else 3, "e_h2" if m == 1 else "hq")
        elif m == 6:
            self.at("q")[...] = dot(self.at("hq")[...], weight).astype(bf16)
        elif m == 7:
            kv = self.at("kv")
            kv[:, columns] = dot(self.at("hm")[...], weight).astype(bf16)
            if start + size == kv.shape[1]:
                attend(self.at("q"), 0, kv, 0, kv, D, self.cross_mask, self.opened("c_o"))
        elif m == 8:
            after = self.live(rows) * dot(self.at("c_o")[...], weight)
            self.opened("d_x2")[...] += after
            self.set_norm(self.at("d_x2")[...], 5, "d_h2")
        elif m == 2 or m == 9:
            u, a = side + "_u", side + "_a"
            if first:
                self.opened(u)
                self.opened(a)
            united = dot(self.at(side + "_h2")[...], weight)
            self.at(u)[:, columns] = united.astype(bf16)
            if start < FF:
                self.gates[pl.ds(0, united.shape[0]), columns] = united
            else:
                back = pl.ds(start - FF, size)
                gate = self.gates[pl.ds(0, united.shape[0]), back]
                self.at(a)[:, back] = (0.5 * gate * (1.0 + gelu_tanh(gate)) * united).astype(bf16)
            if start + size == 2 * FF:
                self.kept(u)
                self.kept(a)
        else:
            if m == 3 and first:
                self.opened("e_x2")
            before = self.at("e_x1" if m == 3 else "d_x2")
            after = before[:, columns] + self.live(rows) * dot(self.at(side + "_a")[...], weight)
            out = self.enc_out if m == 3 else self.dec_out
            out[:, columns] = after.astype(bf16)
            if m == 3:
                self.at("e_x2")[:, columns] = after
                if start + size == D:
                    self.kept("e_x2")
                    self.set_norm(self.at("e_x2")[...], 4, "hm")


class Backward:
    def __init__(self, refs, lengths, load, free):
        self.__dict__.update(refs)
        self.lengths, self.load, self.free = lengths, load, free

    def rows(self, side):
        return self.e_x0.shape[0] if side == "enc" else self.d_x0.shape[0]

    def live(self, side):
        return live_rows(self.lengths[side], self.rows(side))

    def gain(self, k):
        return self.gains[k : k + 1]

    def top(self, ref, side):
        return ref.at[pl.ds(0, self.rows(side))]

    def side(self, m):
        return "enc" if m < 4 else "dec"

    def through_norm(self, values, k, grad, into):
        small = shrunk(values)
        unit = values * small
        grad = grad * self.gain(k)
        into[...] += small * (grad - unit * jnp.mean(grad * unit, axis=-1, keepdims=True))

    def set_branch(self, side):
        grad = self.e_grad if side == "enc" else self.d_grad
        self.top(self.dz, side)[...] = (self.live(side) * grad[...]).astype(bf16)

    def before(self, m):
        side = self.side(m)
        if m == 10 or m == 3:
            if m == 10:
                self.d_grad[...] = self.d_cot[...].astype(f32)
            self.set_branch(side)
            self.load("d_a" if m == 10 else "e_a")
        elif m == 9 or m == 2:
            self.load("d_u" if m == 9 else "e_u")
            self.load("d_h2" if m == 9 else "e_h2")
            u, da = self.top(self.u, side), self.top(self.da, side)

            @pl.loop(0, FF // 256)
            def _(j):
                at = pl.multiple_of(j * 256, 256)
                gate_at, up_at = pl.ds(at, 256), pl.ds(pl.multiple_of(at + FF, 256), 256)
                t, up, grad = u[:, gate_at].astype(f32), u[:, up_at].astype(f32), da[:, gate_at]
                th = gelu_tanh(t)
                slope = 0.5 * (1.0 + th) + 0.5 * t * (1.0 - th * th) * (
                    0.7978845608028654 * (1.0 + 0.134145 * (t * t))
                )
                u[:, gate_at] = (slope * up * grad).astype(bf16)
                u[:, up_at] = (0.5 * t * (1.0 + th) * grad).astype(bf16)
        elif m == 8:
            self.set_branch("dec")
            self.load("c_o")
        elif m == 7:
            for name in ("q", "kv", "hm"):
                self.load(name)
            self.attend_back(self.q, 0, self.kv, 0, self.kv, D, self.cross_mask, "dec")
        elif m == 6:
            self.load("hq")
        elif m == 5 or m == 1:
            self.set_branch(side)
            self.load("d_o" if m == 5 else "e_o")
        else:
            self.load("d_h1" if m == 4 else "e_h1")
            self.load("d_qkv" if m == 4 else "e_qkv")
            qkv = self.top(self.qkv, side)
            self.attend_back(qkv, 0, qkv, D, qkv, 2 * D, self.self_mask if m == 4 else self.enc_mask, side)

    def attend_back(self, q_ref, q_at, k_ref, k_at, v_ref, v_at, kept, side):
        grad_ref = self.top(self.do, side)

        @pl.loop(0, HEADS // 2)
        def _(pair):
            q = q_ref[:, pair_columns(pair, q_at)]
            k = k_ref[:, pair_columns(pair, k_at)]
            v = v_ref[:, pair_columns(pair, v_at)]
            grad = grad_ref[:, pair_columns(pair, 0)]
            dq = dk = dv = 0.0
            for which in range(2):
                lanes = head_lanes(which)
                q_half, grad_half = q * lanes, grad * lanes
                probs = head_probs(q_half, k, kept)
                dv = dv + dot(probs.astype(bf16), grad_half, TN)
                dp = dot(grad_half, v, NT)
                centred = dp - jnp.sum(probs * dp, axis=1, keepdims=True)
                ds = (probs * centred * SHRINK).astype(bf16)
                dq = dq + dot(ds, k * lanes)
                dk = dk + dot(ds, q_half, TN)
            q_ref[:, pair_columns(pair, q_at)] = dq.astype(bf16)
            k_ref[:, pair_columns(pair, k_at)] = dk.astype(bf16)
            v_ref[:, pair_columns(pair, v_at)] = dv.astype(bf16)

    def factors(self, m):
        side = self.side(m)
        left = {
            10: self.a, 3: self.a, 9: self.h2, 2: self.h2, 8: self.o, 7: self.h2, 6: self.h1,
            5: self.o, 1: self.o, 4: self.h1, 0: self.h1,
        }[m]
        right = {
            10: self.dz, 3: self.dz, 9: self.u, 2: self.u, 8: self.dz, 7: self.kv, 6: self.q,
            5: self.dz, 1: self.dz, 4: self.qkv, 0: self.qkv,
        }[m]
        if m != 7:
            left, right = self.top(left, side), self.top(right, side)
        return left, right

    def back(self, m, columns, weight, first):
        side = self.side(m)
        right = self.factors(m)[1][:, columns]
        if m in (10, 3):
            into = self.top(self.da, side)
            tall = FF // Z
            for j in range(Z):
                share = dot(right, weight[j].reshape(tall, -1), NT)
                if first:
                    into[:, j * tall : (j + 1) * tall] = share
                else:
                    into[:, j * tall : (j + 1) * tall] += share
            return
        share = dot(right, weight[...].reshape(D, -1), NT)
        into = self.dh if m == 7 else self.top(self.dh, side)
        if m in (8, 5, 1):
            self.top(self.do, side)[...] = share.astype(bf16)
        elif first:
            into[...] = share
        else:
            into[...] += share
    def after(self, m):
        side = self.side(m)
        into = self.dh if m == 7 else self.top(self.dh, side)
        if m == 10:
            self.free("e_a")
        elif m == 9:
            self.load("d_x2")
            self.through_norm(self.top(self.x, "dec")[...], 5, into[...], self.d_grad)
            for name in ("e_x2", "e_u", "hm"):
                self.free(name)
        elif m == 8:
            self.free("d_o")
        elif m == 7:
            self.load("e_x2")
            self.e_grad[...] = self.e_cot[...].astype(f32)
            self.through_norm(self.x[...], 4, into[...], self.e_grad)
            self.free("d_x1")
            self.free("e_h2")
        elif m == 6:
            self.load("d_x1")
            self.through_norm(self.top(self.x, "dec")[...], 3, into[...], self.d_grad)
            self.free("e_x1")
            self.free("d_h1")
        elif m == 5:
            self.free("e_o")
        elif m == 4:
            self.through_norm(self.d_x0[...].astype(f32), 2, into[...], self.d_grad)
            self.free("e_h1")
            self.free("e_qkv")
        elif m == 2:
            self.load("e_x1")
            self.through_norm(self.x[...], 1, into[...], self.e_grad)
        elif m == 0:
            self.through_norm(self.e_x0[...].astype(f32), 0, into[...], self.e_grad)


HELD = dict(
    e_a="a", d_a="a", e_u="u", d_u="u", e_h2="h2", hm="h2", d_h2="h2", e_x1="x", d_x1="x", d_x2="x", e_x2="dh",
    e_o="o", d_o="o", c_o="o", e_h1="h1", d_h1="h1", hq="h1", e_qkv="qkv", d_qkv="qkv", q="q", kv="kv",
)
KEPT = dict(
    hm="h2", d_x1="x", d_o="o", d_h1="h1", e_a="a", e_u="u", e_h2="h2", e_x2="x", e_x1="x", e_o="o", e_qkv="qkv", e_h1="h1",
)
RING = 3


def whole_body(pieces, back_pieces, count, *refs):
    refs = list(refs)

    def take(n):
        got = refs[:n]
        del refs[:n]
        return got

    parts = take(count)
    scales, e_x0, d_x0, e_cot, d_cot, enc_lengths, dec_lengths = take(7)
    outs = take(count)
    e_grad, d_grad, enc_out, dec_out = take(4)
    wholes = take(count + 1)
    away = dict(zip(KEPT, take(len(KEPT))))
    send, recv, local, back_send, back_recv, stage_sem, ring_sem, out_sem, away_sem, come_sem = take(10)
    names = ["a", "u", "h2", "x", "q", "kv", "o", "qkv", "h1", "dh"]
    held = dict(zip(names, take(len(names))))
    dz, do, da, enc_mask, self_mask, cross_mask, gains, own_scales = take(8)
    wide_ring, deep_ring, wide_out, deep_out = take(4)
    place = Place()
    place.barrier()
    each = scales.shape[1]
    spots = lax.broadcasted_iota(jnp.int32, (each, D), 1) - lax.broadcasted_iota(jnp.int32, (each, D), 0)
    spots = jnp.where(spots == (place.w * 4 + place.n) * each, 1.0, 0.0).astype(bf16)
    own_scales[0] = dot(scales[...], spots).astype(bf16)
    parts.append(own_scales)

    gathers = [
        Gather(place, parts[m], wholes[m], pl.ds(start, size), z_first, (send, recv), k * Gather.SEMS, local.at[k])
        for k, (m, start, size, z_first) in enumerate(pieces)
    ]

    def moved(name, out):
        buffer = held[HELD[name] if out else KEPT[name]]
        there = away[name]
        here = buffer.at[pl.ds(0, there.shape[0])]
        sem = (away_sem if out else come_sem).at[list(KEPT).index(name)]
        return pltpu.make_async_copy(*((here, there) if out else (there, here)), sem)

    lengths = {"enc": enc_lengths, "dec": dec_lengths}
    shared = dict(
        e_x0=e_x0, d_x0=d_x0, e_cot=e_cot, d_cot=d_cot, gains=gains, e_grad=e_grad, d_grad=d_grad,
        enc_out=enc_out, dec_out=dec_out, enc_mask=enc_mask, self_mask=self_mask, cross_mask=cross_mask,
    )
    forward = Forward(dict(shared, gates=da), held, lengths, lambda name: moved(name, True))
    backward = Backward(
        dict(shared, **held, dz=dz, do=do, da=da), lengths,
        lambda name: moved(name, False).wait() if name in KEPT else None,
        lambda name: moved(name, False).start(),
    )
    tall = [w.shape[4] > 3 for w in wholes]

    def staged(k):
        m, start, size, _ = pieces[k]
        if m == count:
            into = wide_ring.at[k % 2, ..., pl.ds(0, 1), :, pl.ds(0, D)]
        else:
            into = (deep_ring.at[2] if tall[m] else wide_ring.at[k % 2]).at[..., pl.ds(0, size)]
        return pltpu.make_async_copy(wholes[m].at[..., pl.ds(start, size)], into, stage_sem.at[k]), into

    deep = [k for k, (m, *_) in enumerate(back_pieces) if tall[m]]

    def ring(k):
        _, _, size, _ = back_pieces[k]
        if k in deep:
            return deep_ring.at[deep.index(k) % 2, ..., pl.ds(0, size)]
        return wide_ring.at[k % RING, ..., pl.ds(0, size)]

    def weight(k):
        m, start, size, _ = back_pieces[k]
        return pltpu.make_async_copy(wholes[m].at[..., pl.ds(start, size)], ring(k), ring_sem.at[k])

    scatters = []
    for k, (m, start, size, z_first) in enumerate(back_pieces):
        total, lasts, zs, firsts = take(4)
        final = deep_out.at[deep.index(k) % 2] if k in deep else wide_out.at[k % 3]
        final = final.at[:, :, pl.ds(0, size)]
        leave = pltpu.make_async_copy(final, outs[m].at[:, :, pl.ds(start, size)], out_sem.at[k])
        scatters.append(
            Scatter(
                place, ring(k), z_first, final, leave, total, lasts, zs, firsts, (back_send, back_recv), k * Scatter.SEMS
            )
        )

    def gather_slot(slot):
        last = STRIDE * (Gather.PHASES - 1)
        for k in range(len(gathers)):
            if (slot - k) % STRIDE == 0 and 0 <= slot - k <= last:
                gathers[k].phase((slot - k) // STRIDE)
        if slot == 0:
            fill_masks(enc_lengths, dec_lengths, enc_mask, self_mask, cross_mask)
        k = slot - last - 1
        if 0 <= k < len(gathers):
            copy, stage = staged(k)
            copy.wait()
            m, start, size, _ = pieces[k]
            if m == count:
                gains[...] = jnp.sum(stage[...].reshape(-1, 8, D).astype(f32), axis=0)
            else:
                forward.step(m, start, size, stage[...].reshape(-1, size))
            if m == 10:
                backward.back(m, pl.ds(start, size), stage, start == 0)
            if k == len(gathers) - 1:
                forward.close()
                backward.after(10)
        if 0 <= slot - last < len(gathers):
            staged(slot - last)[0].start()

    def scatter_slot(slot):
        last_slot = STRIDE * (Scatter.PHASES - 1)
        many = -(-len(gathers) // last_slot)
        for k in range(len(gathers)):
            if slot == len(scatters) + k // many:
                gathers[k].settle()
        for k in range(len(scatters)):
            if (slot - k) % STRIDE == 0 and STRIDE <= slot - k <= last_slot:
                scatters[k].phase((slot - k) // STRIDE)
        k = slot
        if k >= len(scatters):
            return
        if 0 < k < len(scatters) - 1:
            weight(k + 1).start()
        m, start, size, _ = back_pieces[k]
        first = k == 0 or back_pieces[k - 1][0] != m
        last = k == len(scatters) - 1 or back_pieces[k + 1][0] != m
        columns = pl.ds(start, size)
        if first:
            backward.before(m)
        left, right = backward.factors(m)
        part = ring(k)
        if m != 10:
            weight(k).wait()
            backward.back(m, columns, part, first)
        cut = Z if k in deep else 2
        height = left.shape[1] // cut
        grad_columns = right[:, columns]
        for j in range(cut):
            grad = dot(left[:, j * height : (j + 1) * height], grad_columns, TN)
            layers = part.at[pl.ds(j * (Z // cut), Z // cut)]
            layers[...] = grad.reshape(layers.shape).astype(bf16)
        scatters[k].phase(0)
        if last and m != 10:
            backward.after(m)

    start = min(k for k, (m, *_) in enumerate(pieces) if m == 10) + STRIDE * (Gather.PHASES - 1)
    gather_slots = len(gathers) + STRIDE * (Gather.PHASES - 1) + 1
    scatter_slots = len(scatters) + STRIDE * (Scatter.PHASES - 1)
    for slot in range(max(gather_slots, start + scatter_slots)):
        if slot < gather_slots:
            gather_slot(slot)
        if 0 <= slot - start < scatter_slots:
            scatter_slot(slot - start)


def whole_step(shards, scales, enc_input, dec_input, enc_cot, dec_cot, enc_lengths, dec_lengths):
    count = len(shards)
    parts = [s.reshape(s.shape[0] // 8, 8, s.shape[1]) for s in shards]
    shapes = [p.shape for p in parts] + [(1, 8, D)]
    pieces = tuple(p[:4] for p in PIECES)
    back = [(*p[:3], p[4]) for p in PIECES[1:]]
    back_pieces = tuple([p for p in back if p[0] == 10] + [p for p in back[::-1] if p[0] != 10])
    rows, short = enc_input.shape[0], dec_input.shape[0]
    hbm, vmem = pl.BlockSpec(memory_space=pl.ANY), pl.BlockSpec(memory_space=pltpu.VMEM)
    smem = pl.BlockSpec(memory_space=pltpu.SMEM)
    wide = max(size for m, _, size, _ in back_pieces if shapes[m][0] == 3)
    deep = max((shapes[m][0], size) for m, _, size, _ in back_pieces)
    buffers = dict(
        a=(rows, FF, bf16), u=(rows, 2 * FF, bf16), h2=(rows, D, bf16), x=(rows, D, f32), q=(short, D, bf16),
        kv=(rows, 2 * D, bf16), o=(rows, D, bf16), qkv=(rows, 3 * D, bf16), h1=(rows, D, bf16), dh=(rows, D, f32),
    )
    dma = pltpu.SemaphoreType.DMA
    scratch = [
        dma((len(pieces) * Gather.SEMS,)), dma((len(pieces) * Gather.SEMS,)), dma((len(pieces),)),
        dma((len(back_pieces) * Scatter.SEMS,)), dma((len(back_pieces) * Scatter.SEMS,)),
        dma((len(pieces),)), dma((len(back_pieces),)), dma((len(back_pieces),)), dma((len(KEPT),)), dma((len(KEPT),)),
    ]
    scratch += [pltpu.VMEM((tall, across), dtype) for tall, across, dtype in buffers.values()]
    scratch += [
        pltpu.VMEM((rows, D), bf16),
        pltpu.VMEM((rows, D), bf16),
        pltpu.VMEM((rows, FF), f32),
        pltpu.VMEM((rows, rows), f32),
        pltpu.VMEM((short, short), f32),
        pltpu.VMEM((short, rows), f32),
        pltpu.VMEM((8, D), f32),
        pltpu.VMEM((1, 8, D), bf16),
        pltpu.VMEM((RING, Z, 2, 2, 2, 3, 8, wide), bf16),
        pltpu.VMEM((3, Z, 2, 2, 2, deep[0], 8, deep[1]), bf16),
        pltpu.VMEM((3, 3, 8, wide), f32),
        pltpu.VMEM((2, deep[0], 8, deep[1]), f32),
    ]
    for m, _, size, z_first in back_pieces:
        block = (shapes[m][0], 8, size)
        scratch += [
            pltpu.VMEM((Z, 2, 2, *block), bf16),
            pltpu.VMEM((Z, 2, *block), bf16),
            pltpu.VMEM((5, *(() if z_first else (2,)), *block), bf16),
            pltpu.VMEM((*((Z,) if z_first else ()), *block), bf16),
        ]
    kept = [(short if name[0] == "d" else rows, *buffers[HELD[name]][1:]) for name in KEPT]
    outs = pl.pallas_call(
        functools.partial(whole_body, pieces, back_pieces, count),
        out_shape=[jax.ShapeDtypeStruct(p.shape, f32) for p in parts]
        + [
            jax.ShapeDtypeStruct((rows, D), f32),
            jax.ShapeDtypeStruct((short, D), f32),
            jax.ShapeDtypeStruct((rows, D), bf16),
            jax.ShapeDtypeStruct((short, D), bf16),
        ]
        + [jax.ShapeDtypeStruct((Z, 2, 2, 2, *shape), bf16) for shape in shapes]
        + [jax.ShapeDtypeStruct((tall, across), dtype) for tall, across, dtype in kept],
        in_specs=[hbm] * count + [vmem] * 5 + [smem] * 2,
        out_specs=[hbm] * count + [vmem] * 4 + [hbm] * (count + 1 + len(KEPT)),
        scratch_shapes=scratch,
        compiler_params=pltpu.CompilerParams(
            collective_id=0, has_side_effects=True, vmem_limit_bytes=VMEM_LIMIT
        ),
    )(*parts, scales, enc_input, dec_input, enc_cot, dec_cot, enc_lengths, dec_lengths)
    e_grad, d_grad, enc_out, dec_out = outs[count : count + 4]
    return outs[:count], (enc_out, dec_out, e_grad, d_grad)


VMEM_LIMIT = 62 * 2**20


def finish_body(count, scaled, *refs):
    refs = list(refs)

    def take(n):
        got = refs[:n]
        del refs[:n]
        return got

    totals, shards, (scales,), passed = take(count), take(len(scaled)), take(1), take(4)
    grads, scale_grads, through = take(count), take(len(scaled)), take(4)
    for total, grad in zip(totals, grads):
        grad[...] = total[...].reshape(grad.shape)
    for k, (m, shard, out) in enumerate(zip(scaled, shards, scale_grads)):
        product = grads[m][...] * shard[...].astype(f32)
        summed = lax.dot_general(
            jnp.ones((8, product.shape[1]), f32), product, NT,
            precision=lax.Precision.HIGHEST, preferred_element_type=f32,
        )
        out[...] = summed[0:1] / scales[k : k + 1].astype(f32)
    for src, out in zip(passed, through):
        out[...] = src[...]


def finish(totals, shards, scales, passed):
    scaled = [m for m, k in enumerate(SCALE_OF) if k is not None]
    vmem = pl.BlockSpec(memory_space=pltpu.VMEM)
    count = len(totals)
    outs = pl.pallas_call(
        functools.partial(finish_body, count, scaled),
        out_shape=[jax.ShapeDtypeStruct(s.shape, f32) for s in shards]
        + [jax.ShapeDtypeStruct((1, scales.shape[1]), f32)] * len(scaled)
        + [jax.ShapeDtypeStruct(p.shape, p.dtype) for p in passed],
        in_specs=[vmem] * (count + len(scaled) + 5),
        out_specs=[vmem] * (count + len(scaled) + 4),
        compiler_params=pltpu.CompilerParams(vmem_limit_bytes=VMEM_LIMIT),
    )(*totals, *[shards[m] for m in scaled], scales, *passed)
    return outs[:count], [g.reshape(-1) for g in outs[count:-4]], outs[-4:]


def norm_rows(values, scales):
    return values * lax.rsqrt(jnp.mean(values * values, axis=-1, keepdims=True) + epsilon) * scales


def norm_back(inputs, scales, grad):
    return jax.vjp(lambda v: norm_rows(v, scales), inputs)[1](grad)[0]


def gated_units(united):
    halfway = united.shape[-1] // 2
    return jax.nn.gelu(united[:, :halfway], approximate=True) * united[:, halfway:]


def row_items(lengths, row_count):
    places = jnp.arange(row_count, dtype=jnp.int32)
    count = lengths.shape[0]
    item, boundary = jnp.zeros((row_count,), jnp.int32), jnp.int32(0)
    for k in range(count):
        boundary = boundary + lengths[k]
        item = item + (places >= boundary).astype(jnp.int32)
    return item


def head_split(matrix):
    return matrix.reshape(matrix.shape[0], HEADS, HEAD_DIM)


def outer_rows(left, right):
    return jnp.einsum("rd,re->de", left, right, preferred_element_type=jnp.float32).astype(jnp.bfloat16)


def back_rows(incoming, matrix):
    return jnp.einsum("re,de->rd", incoming, matrix, preferred_element_type=jnp.float32)


def score_rows(query_heads, key_heads, allowed):
    raw_scores = jnp.einsum(
        "qhd,khd->hqk", query_heads, key_heads, preferred_element_type=jnp.float32
    )
    return jnp.where(allowed[None], raw_scores * HEAD_DIM ** (-0.5), masked_value)


def attend_forward(queries, keys_in, values_in, allowed):
    scores = score_rows(head_split(queries), head_split(keys_in), allowed)
    largest = jnp.max(scores, axis=2, keepdims=True)
    expanded = jnp.exp(scores - largest)
    totals = jnp.sum(expanded, axis=2, keepdims=True)
    weights = (expanded / totals).astype(jnp.bfloat16)
    mixed = jnp.einsum(
        "hqk,khd->qhd", weights, head_split(values_in), preferred_element_type=jnp.float32
    )
    return (mixed.reshape(queries.shape[0], D), largest + jnp.log(totals))


def attend_backward(queries, keys_in, values_in, allowed, log_totals, grad_mixed):
    query_heads = head_split(queries)
    key_heads = head_split(keys_in)
    value_heads = head_split(values_in)
    probs = jnp.exp(score_rows(query_heads, key_heads, allowed) - log_totals)
    grad_heads = head_split(grad_mixed)
    grad_values = jnp.einsum(
        "hqk,qhd->khd", probs.astype(jnp.bfloat16), grad_heads, preferred_element_type=jnp.float32
    )
    grad_probs = jnp.einsum(
        "qhd,khd->hqk", grad_heads, value_heads, preferred_element_type=jnp.float32
    )
    centred = grad_probs - jnp.sum(probs * grad_probs, axis=2, keepdims=True)
    grad_scores = (probs * centred * HEAD_DIM ** (-0.5)).astype(jnp.bfloat16)
    grad_queries = jnp.einsum(
        "hqk,khd->qhd", grad_scores, key_heads, preferred_element_type=jnp.float32
    )
    grad_keys = jnp.einsum(
        "hqk,qhd->khd", grad_scores, query_heads, preferred_element_type=jnp.float32
    )
    return (
        grad_queries.reshape(queries.shape[0], D),
        grad_keys.reshape(keys_in.shape[0], D),
        grad_values.reshape(keys_in.shape[0], D),
    )


def self_forward(inputs, params, allowed, live_rows):
    scales, joined, outward = params
    normed = norm_rows(inputs, scales).astype(jnp.bfloat16)
    projected = jnp.dot(normed, joined, preferred_element_type=jnp.float32).astype(jnp.bfloat16)
    mixed, log_totals = attend_forward(
        projected[:, :D], projected[:, D : 2 * D], projected[:, 2 * D :], allowed
    )
    mixed_low = mixed.astype(jnp.bfloat16)
    branch = jnp.dot(mixed_low, outward, preferred_element_type=jnp.float32)
    return (inputs + live_rows[:, None] * branch, (normed, projected, mixed_low, log_totals))


def self_backward(inputs, params, allowed, live_rows, stored, incoming):
    scales, joined, outward = params
    normed, projected, mixed_low, log_totals = stored
    grad_branch = (live_rows[:, None] * incoming).astype(jnp.bfloat16)
    grad_outward = outer_rows(mixed_low, grad_branch)
    grad_mixed = back_rows(grad_branch, outward).astype(jnp.bfloat16)
    grad_parts = attend_backward(
        projected[:, :D],
        projected[:, D : 2 * D],
        projected[:, 2 * D :],
        allowed,
        log_totals,
        grad_mixed,
    )
    grad_projected = jnp.concatenate(grad_parts, axis=1).astype(jnp.bfloat16)
    grad_joined = outer_rows(normed, grad_projected)
    grad_inputs = norm_back(inputs, scales, back_rows(grad_projected, joined))
    return (incoming + grad_inputs, (grad_joined, grad_outward))


def cross_forward(inputs, memory, params, allowed, live_rows):
    scales, memory_scales, query_map, pair_map, outward = params
    normed = norm_rows(inputs, scales).astype(jnp.bfloat16)
    memory_normed = norm_rows(memory, memory_scales).astype(jnp.bfloat16)
    queries = jnp.dot(normed, query_map, preferred_element_type=jnp.float32).astype(jnp.bfloat16)
    pairs = jnp.dot(memory_normed, pair_map, preferred_element_type=jnp.float32).astype(
        jnp.bfloat16
    )
    mixed, log_totals = attend_forward(queries, pairs[:, :D], pairs[:, D:], allowed)
    mixed_low = mixed.astype(jnp.bfloat16)
    branch = jnp.dot(mixed_low, outward, preferred_element_type=jnp.float32)
    return (
        inputs + live_rows[:, None] * branch,
        (normed, memory_normed, queries, pairs, mixed_low, log_totals),
    )


def cross_backward(inputs, memory, params, allowed, live_rows, stored, incoming):
    scales, memory_scales, query_map, pair_map, outward = params
    normed, memory_normed, queries, pairs, mixed_low, log_totals = stored
    grad_branch = (live_rows[:, None] * incoming).astype(jnp.bfloat16)
    grad_outward = outer_rows(mixed_low, grad_branch)
    grad_mixed = back_rows(grad_branch, outward).astype(jnp.bfloat16)
    grad_queries, grad_keys, grad_values = attend_backward(
        queries, pairs[:, :D], pairs[:, D:], allowed, log_totals, grad_mixed
    )
    grad_queries_low = grad_queries.astype(jnp.bfloat16)
    grad_pairs = jnp.concatenate([grad_keys, grad_values], axis=1).astype(jnp.bfloat16)
    grad_query_map = outer_rows(normed, grad_queries_low)
    grad_pair_map = outer_rows(memory_normed, grad_pairs)
    grad_inputs = norm_back(inputs, scales, back_rows(grad_queries_low, query_map))
    grad_memory = norm_back(memory, memory_scales, back_rows(grad_pairs, pair_map))
    return (
        incoming + grad_inputs,
        grad_memory,
        (grad_query_map, grad_pair_map, grad_outward),
    )


def mlp_forward(inputs, params, live_rows):
    scales, inward, outward = params
    normed = norm_rows(inputs, scales).astype(jnp.bfloat16)
    united = jnp.dot(normed, inward, preferred_element_type=jnp.float32)
    activated = gated_units(united).astype(jnp.bfloat16)
    branch = jnp.dot(activated, outward, preferred_element_type=jnp.float32)
    return (inputs + live_rows[:, None] * branch, (normed, united, activated))


def mlp_backward(inputs, params, live_rows, stored, incoming):
    scales, inward, outward = params
    normed, united, activated = stored
    grad_branch = (live_rows[:, None] * incoming).astype(jnp.bfloat16)
    grad_outward = outer_rows(activated, grad_branch)
    grad_activated = back_rows(grad_branch, outward)
    _, pullback = jax.vjp(gated_units, united)
    grad_united = pullback(grad_activated)[0].astype(jnp.bfloat16)
    grad_inward = outer_rows(normed, grad_united)
    grad_inputs = norm_back(inputs, scales, back_rows(grad_united, inward))
    return (incoming + grad_inputs, (grad_inward, grad_outward))


def plain_gather(shards):
    return [lax.all_gather(s, AXES, axis=0, tiled=True) for s in shards]


def plain_scatter(sums):
    return [lax.psum_scatter(s.astype(jnp.float32), AXES, scatter_dimension=0, tiled=True) for s in sums]


SCALE_OF = (0, None, 1, None, 2, None, 3, 4, None, 5, None)


def per_device(
    linked,
    enc_input,
    dec_input,
    enc_lengths,
    dec_lengths,
    enc_attn_gain,
    enc_qkv,
    enc_attn_out,
    enc_mlp_gain,
    enc_mlp_in,
    enc_mlp_out,
    dec_self_gain,
    dec_qkv,
    dec_self_out,
    cross_gain,
    memory_gain,
    cross_query,
    cross_kv,
    cross_out,
    dec_mlp_gain,
    dec_mlp_in,
    dec_mlp_out,
    enc_cotangent,
    dec_cotangent,
):
    gains = [enc_attn_gain, enc_mlp_gain, dec_self_gain, cross_gain, memory_gain, dec_mlp_gain]
    shards = (
        enc_qkv, enc_attn_out, enc_mlp_in, enc_mlp_out, dec_qkv, dec_self_out,
        cross_query, cross_kv, cross_out, dec_mlp_in, dec_mlp_out,
    )
    if linked:
        stacked = jnp.stack(gains + [jnp.zeros_like(gains[0])] * (8 - len(gains)))
        summed, passed = whole_step(
            shards, stacked, enc_input, dec_input, enc_cotangent, dec_cotangent, enc_lengths, dec_lengths
        )
        grads, scale_grads, (enc_out, dec_out, grad_encoder_start, grad_decoder_start) = finish(
            summed, shards, stacked, passed
        )
    else:
        item_count = enc_lengths.shape[0]
        enc_items = row_items(enc_lengths, enc_input.shape[0])
        dec_items = row_items(dec_lengths, dec_input.shape[0])
        enc_live = (enc_items < item_count).astype(jnp.float32)
        dec_live = (dec_items < item_count).astype(jnp.float32)
        enc_padded = enc_items[:, None] == item_count
        dec_padded = dec_items[:, None] == item_count
        enc_allowed = (enc_items[:, None] == enc_items[None, :]) | enc_padded
        dec_places = jnp.arange(dec_input.shape[0], dtype=jnp.int32)
        self_allowed = (dec_items[:, None] == dec_items[None, :]) & (
            dec_places[None, :] <= dec_places[:, None]
        ) | dec_padded
        cross_allowed = (dec_items[:, None] == enc_items[None, :]) | dec_padded
        whole = plain_gather(shards)
        own = [g.astype(jnp.float32) for g in gains]
        gains = plain_gather(own)
        encoder_start = enc_input.astype(jnp.float32)
        decoder_start = dec_input.astype(jnp.float32)
        enc_middle, enc_attn_store = self_forward(encoder_start, (gains[0], *whole[0:2]), enc_allowed, enc_live)
        encoder_final, enc_mlp_store = mlp_forward(enc_middle, (gains[1], *whole[2:4]), enc_live)
        dec_middle, dec_self_store = self_forward(decoder_start, (gains[2], *whole[4:6]), self_allowed, dec_live)
        dec_crossed, cross_store = cross_forward(
            dec_middle, encoder_final, (gains[3], gains[4], *whole[6:9]), cross_allowed, dec_live
        )
        decoder_final, dec_mlp_store = mlp_forward(dec_crossed, (gains[5], *whole[9:11]), dec_live)
        enc_out, dec_out = encoder_final.astype(jnp.bfloat16), decoder_final.astype(jnp.bfloat16)
        grad_crossed, dec_mlp_grads = mlp_backward(
            dec_crossed, (gains[5], *whole[9:11]), dec_live, dec_mlp_store, dec_cotangent.astype(jnp.float32)
        )
        grad_middle, grad_memory, cross_grads = cross_backward(
            dec_middle,
            encoder_final,
            (gains[3], gains[4], *whole[6:9]),
            cross_allowed,
            dec_live,
            cross_store,
            grad_crossed,
        )
        grad_decoder_start, dec_self_grads = self_backward(
            decoder_start, (gains[2], *whole[4:6]), self_allowed, dec_live, dec_self_store, grad_middle
        )
        grad_enc_middle, enc_mlp_grads = mlp_backward(
            enc_middle,
            (gains[1], *whole[2:4]),
            enc_live,
            enc_mlp_store,
            enc_cotangent.astype(jnp.float32) + grad_memory,
        )
        grad_encoder_start, enc_attn_grads = self_backward(
            encoder_start, (gains[0], *whole[0:2]), enc_allowed, enc_live, enc_attn_store, grad_enc_middle
        )
        sums = enc_attn_grads + enc_mlp_grads + dec_self_grads + cross_grads + dec_mlp_grads
        summed = plain_scatter(sums)
        grads, scale_grads = [], {}
        for total, shard, k in zip(summed, shards, SCALE_OF):
            if k is not None:
                scale_grads[k] = jnp.sum(total * shard.astype(jnp.float32), axis=1) / own[k]
            grads.append(total)
    return (
        enc_out,
        dec_out,
        grad_encoder_start,
        grad_decoder_start,
        scale_grads[0], grads[0], grads[1],
        scale_grads[1], grads[2], grads[3],
        scale_grads[2], grads[4], grads[5],
        scale_grads[3], scale_grads[4], grads[6], grads[7], grads[8],
        scale_grads[5], grads[9], grads[10],
    )


def solution(mesh):
    rows, line = P(AXES, None), P(AXES)
    linked = mesh.shape["wide"] == 2 * Z and mesh.shape["narrow"] == 4
    weights = (
        line, rows, rows, line, rows, rows, line, rows, rows,
        line, line, rows, rows, rows, line, rows, rows,
    )
    return jax.shard_map(
        functools.partial(per_device, linked),
        mesh=mesh,
        in_specs=(rows, rows, line, line, *weights, rows, rows),
        out_specs=(rows, rows, rows, rows, *weights),
        check_vma=False,
    )
```
